128 devices in a mesh: dp: 4 (over z), ctx: 32 (over y, x, core).
Axes of the slice: x: 4, y: 4, z: 4, core: 2. Of those that a mesh axis runs over, the one named last changes fastest.
Arguments:
- queries: bfloat16 [32768, 4096], P(('dp', 'ctx')), may hold values from -27 to 27
- keys: bfloat16 [32768, 512], P(('dp', 'ctx')), may hold values from -9 to 9
- values: bfloat16 [32768, 512], P(('dp', 'ctx')), may hold values from -6 to 6
- upstream: bfloat16 [32768, 4096], P(('dp', 'ctx')), may hold values from -24 to 24
- ancestors: int32 [256, 6], P(('dp', 'ctx')), may hold values from -1 to 63, as said below
- segments: int32 [32768], P(('dp', 'ctx')), may hold values from -1 to 2, as said below
- responses: int32 [32768], P(('dp', 'ctx')), may hold values from -1 to 15, as said below
- rewards: int32 [64], P('dp'), may hold values from 0 to 4, as said below
- lengths: int32 [64], P('dp'), may hold values from 64 to 1024, as said below
Outputs:
- attended: bfloat16 [32768, 4096], P(('dp', 'ctx'))
- grad_q: bfloat16 [32768, 4096], P(('dp', 'ctx'))
- grad_k: float32 [32768, 512], P(('dp', 'ctx'))
- grad_v: float32 [32768, 512], P(('dp', 'ctx'))
The draws below stay inside these ranges and needn't reach their ends.
Inputs may be any that keep to these rules, and one draw needn't show every extreme that they name: `ancestors`: row b lists the ancestor blocks of block b by their index among the 64 blocks of its group, which lie 2 to a device along ctx in order; unused slots hold -1 and come last. A group's prompt is the 2 blocks of one device: its block number j lists prompt blocks 0 to j - 1. Every other block lists the 2 prompt blocks in its first 2 slots and then k response blocks, 0 <= k <= 4, the one in slot 2 + u lying on the device k - u places before the block's own device along ctx, cyclically; in every group some block has k = 4. All tokens of a listed block have segment 0. `segments`: -1 marks padding at a block's end, 0 the part that continues the block's ancestors, 1 and 2 later leaves branching off segment 0. `responses`: -1 for prompt and padding tokens, else the response within the token's group. `rewards`: in some groups all responses but one share a reward and that one is higher by one. `lengths`: lengths in group number g lie between 128 // 2 * (g + 1) and 2 * 128 * (g + 1).
All inputs are finite; a program needn't handle non-finite values.
Results may differ from the reference program's by a relative error of at most 0.012.
The reference program's roundings to bfloat16 on the way count: a program that leaves them out, or rounds other values in their place, can miss the bound.
Values may be sent and summed in bfloat16 or wider, within the bound.
A program may use at most 128 MiB of HBM per device.

```python
import math
import jax
import jax.numpy as jnp
from jax import lax

QUERY_HEAD_COUNT = 32
KEY_VALUE_HEADS = 4
HEAD_WIDTH = 128
TREE_BLOCK_SIZE = 128
NB_DEV = 2
DEPTH = 4
G = 16
ANC = 6
NBLK = 64
GROUPS = 4
TOTAL_BLOCKS = 256
TOKENS = 32768
QUERY_FEATURES = 4096
KVW = 512


def draw_queries(key, part):
    key = jax.random.fold_in(key, 1)
    return jnp.clip(1.5 * jax.random.normal(key, (TOKENS, QUERY_FEATURES), jnp.float32), -9.0, 9.0).astype(jnp.bfloat16)


def draw_keys(key, part):
    key = jax.random.fold_in(key, 2)
    return jnp.clip(1.5 * jax.random.normal(key, (TOKENS, KVW), jnp.float32), -9.0, 9.0).astype(jnp.bfloat16)


def grow_group(group_key):
    device_count = NBLK // NB_DEV
    keys_list = jax.random.split(group_key, 6)
    prompt_device = jax.random.randint(keys_list[0], (), 0, device_count)
    coins = jax.random.randint(keys_list[1], (device_count,), 0, 3)

    def advance(previous, item):
        offset, coin = item
        grown = jnp.where((coin > 0) & (previous < DEPTH), previous + 1, 0)
        level = jnp.where(offset == 0, -1, jnp.where(offset <= DEPTH + 1, offset - 1, grown))
        return (level, level)
    _, level_by_offset = lax.scan(advance, jnp.int32(-1), (jnp.arange(device_count), coins))
    devices = jnp.arange(device_count)
    device_level = level_by_offset[(devices - prompt_device) % device_count]
    parent_local = jax.random.randint(keys_list[2], (device_count, NB_DEV), 0, NB_DEV)
    chain_reward = jax.random.randint(keys_list[3], (NBLK,), 0, G)
    block_device = jnp.repeat(devices, NB_DEV)
    block_local = jnp.tile(jnp.arange(NB_DEV), device_count)
    block_level = device_level[block_device]
    walker = block_local
    chain_list = []
    for distance in range(1, DEPTH + 1):
        walker = parent_local[(block_device - distance + 1) % device_count, walker]
        chain_list.append((block_device - distance) % device_count * NB_DEV + walker)
    chain = jnp.stack(chain_list)
    block_ids = jnp.arange(NBLK)
    chain_root = jnp.where(block_level >= 1, chain[jnp.clip(block_level - 1, 0, DEPTH - 1), block_ids], block_ids)
    response_base = chain_reward[chain_root]
    slots = jnp.arange(ANC)[None, :]
    upper = slots - NB_DEV
    gap = block_level[:, None] - upper
    response_ids = chain[jnp.clip(gap - 1, 0, DEPTH - 1), block_ids[:, None]]
    prompt_valid = (block_level[:, None] >= 0) | (slots < block_local[:, None])
    response_valid = (upper >= 0) & (upper < block_level[:, None])
    table = jnp.where(slots < NB_DEV, jnp.where(prompt_valid, prompt_device * NB_DEV + slots, -1), jnp.where(response_valid, response_ids, -1))
    next_device = (block_device + 1) % device_count
    has_child = (device_level[next_device] >= 1) & jnp.any(parent_local[next_device] == block_local[:, None], axis=1)
    inner = (block_level < 0) | has_child
    position = jnp.arange(TREE_BLOCK_SIZE)[None, :]
    cuts = jax.random.randint(keys_list[4], (NBLK, 2), TREE_BLOCK_SIZE // 8, TREE_BLOCK_SIZE)
    lower_cut = jnp.min(cuts, axis=1, keepdims=True)
    upper_cut = jnp.max(cuts, axis=1, keepdims=True)
    leaves = (position >= lower_cut).astype(jnp.int32) + (position >= upper_cut).astype(jnp.int32)
    pad_length = jax.random.randint(keys_list[5], (NBLK, 1), 0, TREE_BLOCK_SIZE // 4 + 1)
    node = jnp.where(position >= TREE_BLOCK_SIZE - pad_length, -1, leaves)
    node = jnp.where(inner[:, None], 0, node)
    owner_response = jnp.where((block_level[:, None] < 0) | (node < 0), -1, (response_base[:, None] + node) % G)
    return (table.astype(jnp.int32), node.reshape(-1).astype(jnp.int32), owner_response.reshape(-1).astype(jnp.int32))


def grow_tree(key):
    key = jax.random.fold_in(key, 202)
    group_keys = jax.random.split(key, GROUPS)
    table, node, owner_response = jax.vmap(grow_group)(group_keys)
    return (table.reshape(TOTAL_BLOCKS, ANC), node.reshape(TOKENS), owner_response.reshape(TOKENS))


def draw_ancestors(key, part):
    tree = grow_tree(key)
    return tree[0]


def draw_segments(key, part):
    tree = grow_tree(key)
    return tree[1]


def draw_responses(key, part):
    tree = grow_tree(key)
    return tree[2]


def draw_rewards(key, part):
    key = jax.random.fold_in(key, 5)
    keys_list = jax.random.split(key, 4)
    flip = jax.random.randint(keys_list[0], (), 0, 2)
    level_group = (jnp.arange(GROUPS) + flip) % 2 == 0
    varied = jax.random.randint(keys_list[1], (GROUPS, G), 0, 5)
    common = jax.random.randint(keys_list[2], (GROUPS, 1), 0, 4)
    raised = jax.random.randint(keys_list[3], (GROUPS, 1), 0, G)
    nearly = common + (jnp.arange(G)[None, :] == raised).astype(jnp.int32)
    return jnp.where(level_group[:, None], nearly, varied).reshape(-1).astype(jnp.int32)


def draw_lengths(key, part):
    key = jax.random.fold_in(key, 6)
    group = jnp.arange(GROUPS * G) // G
    index = jnp.arange(GROUPS * G)
    drawn = jax.random.randint(key, (GROUPS * G,), TREE_BLOCK_SIZE // 2, 2 * TREE_BLOCK_SIZE + 1)
    drawn = jnp.where(index == 0, TREE_BLOCK_SIZE // 2, drawn)
    drawn = jnp.where(index == GROUPS * G - 1, 2 * TREE_BLOCK_SIZE, drawn)
    return (drawn * (1 + group)).astype(jnp.int32)


def steps_of(stream_key, shape, shards, low, high):
    gain, own = 1.0, jax.random.fold_in(stream_key, 6)
    for axis_at, blocks in shards:
        steps = jnp.exp(jax.random.uniform(jax.random.fold_in(own, axis_at), (blocks,), jnp.float32, low / len(shards), high / len(shards)))
        gain = gain * jnp.repeat(steps, shape[axis_at] // blocks).reshape([-1 if axis == axis_at else 1 for axis in range(len(shape))])
    return gain


def bell_draw(own_key, dims, scale, limit, cuts=(), held_as=jnp.bfloat16):
    factor_of = steps_of(own_key, dims, cuts, -0.22, 0.18) if cuts else 1.0
    values = jax.random.normal(own_key, dims, jnp.float32) * scale * factor_of
    return jnp.minimum(jnp.maximum(values, -limit), limit).astype(held_as)


def setup_inputs(seed: int = 0) -> dict:
    arg_keys = jax.random.split(jax.random.key(seed), 10)
    return {
        "queries": draw_queries(jax.random.fold_in(arg_keys[9], 71), 0),
        "keys": draw_keys(jax.random.fold_in(arg_keys[9], 71), 0),
        "values": bell_draw(arg_keys[2], (TOKENS, KVW), 1.0, 6.0, ((0, 128),)),
        "upstream": bell_draw(arg_keys[3], (TOKENS, QUERY_FEATURES), 4.0, 24.0, ((0, 128),)),
        "ancestors": draw_ancestors(jax.random.fold_in(arg_keys[9], 71), 0),
        "segments": draw_segments(jax.random.fold_in(arg_keys[9], 71), 0),
        "responses": draw_responses(jax.random.fold_in(arg_keys[9], 71), 0),
        "rewards": draw_rewards(jax.random.fold_in(arg_keys[9], 71), 0),
        "lengths": draw_lengths(jax.random.fold_in(arg_keys[9], 71), 0),
    }


def visibility(seg_row, slot_valid):
    rows = jnp.arange(seg_row.shape[0])
    earlier = rows[None, :] <= rows[:, None]
    related = (seg_row[None, :] == seg_row[:, None]) | (seg_row[None, :] == 0)
    own_block = earlier & (seg_row[:, None] >= 0) & related | (rows[None, :] == rows[:, None])
    width = seg_row.shape[0]
    remote = jnp.broadcast_to(slot_valid[None, :, None], (width, slot_valid.shape[0], width))
    return jnp.concatenate([remote, own_block[:, None, :]], axis=1)

def block_step(query_block, slot_keys, slot_values, visible, up_block, weight_block):
    inv_root = 1.0 / math.sqrt(query_block.shape[-1])
    query_wide = query_block.astype(jnp.float32)
    keys_wide = slot_keys.astype(jnp.float32)
    values_wide = slot_values.astype(jnp.float32)
    scores = jnp.einsum('ihgd,sjhd->hgisj', query_wide, keys_wide) * inv_root
    masked = jnp.where(visible[None, None], scores, -jnp.inf)
    peak = lax.optimization_barrier(jnp.max(masked, axis=(3, 4), keepdims=True))
    exponent = jnp.exp(masked - peak)
    denominator = lax.optimization_barrier(jnp.sum(exponent, axis=(3, 4), keepdims=True))
    probability = exponent / denominator
    prob_low = lax.optimization_barrier(probability.astype(jnp.bfloat16))
    attended = jnp.einsum('hgisj,sjhd->ihgd', prob_low.astype(jnp.float32), values_wide).astype(jnp.bfloat16)
    attended = lax.optimization_barrier(attended)
    grad_out = (up_block.astype(jnp.float32) * weight_block[:, None]).astype(jnp.bfloat16)
    grad_out = lax.optimization_barrier(grad_out).reshape(query_block.shape)
    delta = lax.optimization_barrier(jnp.sum(grad_out.astype(jnp.float32) * attended.astype(jnp.float32), axis=-1))
    delta = jnp.transpose(delta, (1, 2, 0))[..., None, None]
    dprobs = jnp.einsum('ihgd,sjhd->hgisj', grad_out.astype(jnp.float32), values_wide)
    dscores = lax.optimization_barrier((probability * (dprobs - delta) * inv_root).astype(jnp.bfloat16))
    dscores_wide = dscores.astype(jnp.float32)
    grad_query = jnp.einsum('hgisj,sjhd->ihgd', dscores_wide, keys_wide).astype(jnp.bfloat16)
    grad_keys = jnp.einsum('hgisj,ihgd->sjhd', dscores_wide, query_wide)
    grad_values = jnp.einsum('hgisj,ihgd->sjhd', prob_low.astype(jnp.float32), grad_out.astype(jnp.float32))
    return (attended, grad_query, grad_keys, grad_values)

def reference(queries, keys, values, upstream, ancestors, segments, responses, rewards, lengths):
    groups = rewards.shape[0] // G
    total = jnp.sum(lengths.astype(jnp.float32))
    scored = rewards.astype(jnp.float32).reshape(groups, G)
    centre = lax.optimization_barrier(jnp.mean(scored, axis=1, keepdims=True))
    spread = jnp.sqrt(lax.optimization_barrier(jnp.mean(jnp.square(scored - centre), axis=1, keepdims=True)))
    advantage = (scored - centre) / jnp.maximum(spread, 0.5)
    scale = groups * G * TREE_BLOCK_SIZE / total
    token_group = jnp.arange(TOKENS) // (NBLK * TREE_BLOCK_SIZE)
    picked = advantage[token_group, jnp.clip(responses, 0, G - 1)]
    weight = jnp.where(responses >= 0, picked * scale, 0.0)
    group_members = QUERY_HEAD_COUNT // KEY_VALUE_HEADS
    blocked_queries = queries.reshape(TOTAL_BLOCKS, TREE_BLOCK_SIZE, KEY_VALUE_HEADS, group_members, HEAD_WIDTH)
    blocked_keys = keys.reshape(TOTAL_BLOCKS, TREE_BLOCK_SIZE, KEY_VALUE_HEADS, HEAD_WIDTH)
    blocked_values = values.reshape(TOTAL_BLOCKS, TREE_BLOCK_SIZE, KEY_VALUE_HEADS, HEAD_WIDTH)
    up_blocks = upstream.reshape(TOTAL_BLOCKS, TREE_BLOCK_SIZE, QUERY_FEATURES)
    weight_blocks = weight.reshape(TOTAL_BLOCKS, TREE_BLOCK_SIZE)
    seg_blocks = segments.reshape(TOTAL_BLOCKS, TREE_BLOCK_SIZE)
    offset = (jnp.arange(TOTAL_BLOCKS) // NBLK * NBLK).astype(jnp.int32)
    slot_valid = ancestors >= 0
    global_ids = jnp.where(slot_valid, ancestors + offset[:, None], 0).astype(jnp.int32)

    def visit(carry, number):
        key_grads, value_grads = carry
        members = jnp.concatenate([global_ids[number], number[None]]).astype(jnp.int32)
        valid_all = jnp.concatenate([slot_valid[number], jnp.ones((1,), bool)])
        visible = visibility(seg_blocks[number], slot_valid[number])
        attended, grad_query, grad_key, grad_value = block_step(blocked_queries[number], blocked_keys[members], blocked_values[members], visible, up_blocks[number], weight_blocks[number])
        keep = valid_all[:, None, None, None]
        key_grads = key_grads.at[members].add(jnp.where(keep, grad_key, 0.0))
        value_grads = value_grads.at[members].add(jnp.where(keep, grad_value, 0.0))
        return ((key_grads, value_grads), (attended, grad_query))
    zero_filled = jnp.zeros((TOTAL_BLOCKS, TREE_BLOCK_SIZE, KEY_VALUE_HEADS, HEAD_WIDTH), jnp.float32)
    (key_grads, value_grads), (attended, grad_query) = lax.scan(visit, (zero_filled, zero_filled), jnp.arange(TOTAL_BLOCKS, dtype=jnp.int32))
    return (attended.reshape(TOKENS, QUERY_FEATURES), grad_query.reshape(TOKENS, QUERY_FEATURES), key_grads.reshape(TOKENS, KVW), value_grads.reshape(TOKENS, KVW))
```

```python
import functools
import math

import jax
import jax.numpy as jnp
from jax import lax
from jax.experimental import pallas as pl
from jax.experimental.pallas import tpu as pltpu
from jax.sharding import PartitionSpec as P

MESH = pl.DeviceIdType.MESH
F32, BF16 = jnp.float32, jnp.bfloat16
W = 128
T = 2 * W
R = 8
C = R * W
N = 7 * W
HOPS = 4
K_, V_ = 0, 1


def nn(a, b):
    return lax.dot_general(a, b, (((1,), (0,)), ((), ())), preferred_element_type=F32)


def nt(a, b):
    return lax.dot_general(a, b, (((1,), (1,)), ((), ())), preferred_element_type=F32)


def tn(a, b):
    return lax.dot_general(a, b, (((0,), (0,)), ((), ())), preferred_element_type=F32)


SCRATCH = dict(
    kvp=pltpu.VMEM((2, 2, 6, T, W), BF16),
    qb=pltpu.VMEM((2, 2, T, C), BF16),
    ub=pltpu.VMEM((2, 2, T, C), BF16),
    ob=pltpu.VMEM((2, 2, T, C), BF16),
    gb=pltpu.VMEM((2, 2, T, C), BF16),
    cand=pltpu.VMEM((16, 2, 2, 16, W), BF16),
    scat=pltpu.VMEM((16, 2, 2, 16, W), BF16),
    sel=pltpu.VMEM((2, 2, 16, W), BF16),
    gath=pltpu.VMEM((16, 2, 2, 16, W), BF16),
    meta=pltpu.VMEM((2, 2, 8, W), jnp.int32),
    lens=pltpu.VMEM((4, 8, W), jnp.int32),
    wt=pltpu.VMEM((2, 2, W, W), F32),
    mb=pltpu.VMEM((2, 2, W, W), F32),
    ku=pltpu.VMEM((4, N, W), BF16),
    vu=pltpu.VMEM((4, N, W), BF16),
    pf=pltpu.VMEM((4, 4, N, 2 * W), F32),
    dl=pltpu.VMEM((4, 4, 8, 2 * W), F32),
    do=pltpu.VMEM((4, 4, 2 * W, W), BF16),
    ps=pltpu.VMEM((N, 2 * W), F32),
    acc=pltpu.VMEM((N, W), F32),
    gacc=pltpu.VMEM((6, T, W), F32),
    pacc=pltpu.VMEM((T, W), F32),
    own=pltpu.VMEM((2, 2, T, W), F32),
    msend=pltpu.VMEM((2, 2, T, W), F32),
    mrecv=pltpu.VMEM((2, 2, T, W), F32),
    gsend=pltpu.VMEM((2, 2, 4, T, W), BF16),
    grecv=pltpu.VMEM((2, 2, 2, 2, T, W), BF16),
    psend=pltpu.VMEM((2, 2, 16, 16, W), BF16),
    prec=pltpu.VMEM((2, 2, 16, 16, W), BF16),
    agsend=pltpu.VMEM((2, 2, 16, W), BF16),
    ag=pltpu.VMEM((2, 32, 2, 16, W), BF16),
    one_send=pltpu.SemaphoreType.DMA((64,)),
    local=pltpu.SemaphoreType.DMA((12,)),
    kv_recv=pltpu.SemaphoreType.DMA((2, 2)),
    mate_kv=pltpu.SemaphoreType.DMA,
    meta_recv=pltpu.SemaphoreType.DMA,
    lens_send=pltpu.SemaphoreType.DMA,
    lens_recv=pltpu.SemaphoreType.DMA,
    qu_recv=pltpu.SemaphoreType.DMA((2, 2)),
    out_recv=pltpu.SemaphoreType.DMA((2, 2)),
    pr_send=pltpu.SemaphoreType.DMA((2,)),
    pr_recv=pltpu.SemaphoreType.DMA((2,)),
    g_recv=pltpu.SemaphoreType.DMA((2, 2)),
    m_recv=pltpu.SemaphoreType.DMA((2, 2)),
    ps_send=pltpu.SemaphoreType.DMA((2, 2)),
    ps_recv=pltpu.SemaphoreType.DMA((2, 2)),
    ag_send=pltpu.SemaphoreType.DMA((2,)),
    ag_recv=pltpu.SemaphoreType.DMA((2,)),
)


class Names:
    def __init__(self, names, refs):
        for name, ref in zip(names, refs):
            setattr(self, name, ref)


def kernel(groups, ring, q, k, v, u, anc, seg, resp, rew, leng, attn, gq, gk, gv, *refs):
    s = Names(list(SCRATCH), refs)
    me, z = lax.axis_index("ctx"), lax.axis_index("dp")
    chips = ring // 2
    chip, core = me // 2, lax.rem(me, 2)
    other = 1 - core
    mate = 2 * chip + other
    inv_root = 1.0 / math.sqrt(W)
    exp_scale = math.log2(math.e) * inv_root

    first = anc[0, 0]
    root = jnp.where(first < 0, me, lax.div(first, 2))
    root_chip, root_core = lax.div(root, 2), lax.rem(root, 2)

    sends = []

    def send(src, dst, recv_sem, to):
        copy = pltpu.make_async_remote_copy(
            src_ref=src,
            dst_ref=dst,
            send_sem=s.one_send.at[len(sends)],
            recv_sem=recv_sem,
            device_id={"ctx": to},
            device_id_type=MESH,
        )
        copy.start()
        sends.append(copy)

    def await_bytes(ref, sem):
        pltpu.make_async_copy(ref, ref, sem).wait()

    barrier = pltpu.get_barrier_semaphore()

    def greet(i, carry):
        pl.semaphore_signal(
            barrier, inc=1, device_id={"ctx": lax.rem(me + i, ring)}, device_id_type=MESH
        )
        return carry

    lax.fori_loop(1, ring, greet, 0)
    for i in range(1, groups):
        pl.semaphore_signal(
            barrier, inc=1, device_id={"dp": lax.rem(z + i, groups)}, device_id_type=MESH
        )

    def kcols(lane, h):
        return pl.ds(pl.multiple_of((2 * lane + h) * W, W), W)

    def qcols(lane, h):
        return pl.ds(pl.multiple_of((2 * lane + h) * C, C), C)

    local = []

    def fetch(src, dst):
        copy = pltpu.make_async_copy(src, dst, s.local.at[len(local)])
        copy.start()
        local.append(copy)
        return copy

    own_kv = [
        fetch(src.at[:, kcols(core, h)], s.kvp.at[kv, h, 4 + core])
        for h in range(2)
        for kv, src in ((K_, k), (V_, v))
    ]
    own_qu = [
        (
            fetch(q.at[:, qcols(core, h)], s.qb.at[core, h]),
            fetch(u.at[:, qcols(core, h)], s.ub.at[core, h]),
        )
        for h in range(2)
    ]

    total = leng[0]
    for i in range(1, 16):
        total = total + leng[i]
    s.lens[z] = jnp.full((8, W), total, jnp.int32)
    for b in range(2):
        rows = [jnp.where(anc[b, 0] >= 0, 1, 0), jnp.where(anc[b, 1] >= 0, 1, 0)]
        for hop in range(1, HOPS + 1):
            chosen = jnp.int32(-1)
            for slot in range(2, 6):
                a = anc[b, slot]
                away = lax.rem(me - lax.div(jnp.maximum(a, 0), 2) + ring, ring)
                chosen = jnp.where((a >= 0) & (away == hop), lax.rem(a, 2), chosen)
            rows.append(chosen)
        for i, row in enumerate(rows):
            s.meta[core, b, i : i + 1, :] = jnp.full((1, W), row, jnp.int32)
        s.meta[core, b, 6:7, :] = seg[b : b + 1, :]
        s.meta[core, b, 7:8, :] = resp[b : b + 1, :]

    pl.semaphore_wait(barrier, ring - 1 + groups - 1)

    for h in range(2):
        for kv, src in ((K_, k), (V_, v)):
            send(src.at[:, kcols(other, h)], s.kvp.at[kv, h, 4 + core], s.mate_kv, mate)
    for i in range(1, groups):
        pltpu.make_async_remote_copy(
            src_ref=s.lens.at[z],
            dst_ref=s.lens.at[z],
            send_sem=s.lens_send,
            recv_sem=s.lens_recv,
            device_id={"dp": lax.rem(z + i, groups)},
            device_id_type=MESH,
        ).start()
    send(s.meta.at[core], s.meta.at[core], s.meta_recv, mate)

    def send_chain(h):
        for kv, src in ((K_, k), (V_, v)):
            for hop in (1, 2):
                for lane in range(2):
                    send(
                        src.at[:, kcols(lane, h)],
                        s.kvp.at[kv, h, 2 * (2 - hop) + core],
                        s.kv_recv.at[kv, h],
                        2 * lax.rem(chip + hop, chips) + lane,
                    )

    def send_qu(h):
        send(q.at[:, qcols(other, h)], s.qb.at[core, h], s.qu_recv.at[h, 0], mate)
        send(u.at[:, qcols(other, h)], s.ub.at[core, h], s.qu_recv.at[h, 1], mate)

    send_chain(0)
    send_qu(0)

    for copy in own_kv:
        copy.wait()
    await_bytes(s.kvp.at[0, 0, pl.ds(0, 4)], s.mate_kv)
    for h in range(2):
        for kv in range(2):
            x = lax.select(root_core == 0, s.kvp[kv, h, 4], s.kvp[kv, h, 5])
            s.cand[:, h, kv] = x.reshape(16, 16, W)

    def to_chips(start):
        def step(i, carry):
            start(lax.rem(chip + i, chips))
            return carry

        lax.fori_loop(1, chips, step, 0)

    def loop_send(src, dst, send_sem, recv_sem, to):
        pltpu.make_async_remote_copy(
            src_ref=src,
            dst_ref=dst,
            send_sem=send_sem,
            recv_sem=recv_sem,
            device_id={"ctx": to},
            device_id_type=MESH,
        ).start()

    to_chips(
        lambda c: loop_send(
            s.cand.at[c], s.scat.at[chip], s.pr_send.at[0], s.pr_recv.at[0], 2 * c + core
        )
    )
    s.scat[chip] = s.cand[chip]
    send_chain(1)
    send_qu(1)

    await_bytes(s.meta.at[0], s.meta_recv)
    await_bytes(s.lens.at[pl.ds(0, groups - 1)], s.lens_recv)
    everything = s.lens[0, 0:1, :]
    for i in range(1, groups):
        everything = everything + s.lens[i, 0:1, :]
    scale = float(groups * 16 * W) / everything.astype(F32)
    scored = [rew[i].astype(F32) for i in range(16)]
    centre = functools.reduce(lambda a, b: a + b, scored) * (1.0 / 16)
    apart = [x - centre for x in scored]
    variance = functools.reduce(lambda a, b: a + b, [x * x for x in apart]) * (1.0 / 16)
    spread = jnp.sqrt(jnp.full((1, W), variance, F32))
    divisor = jnp.maximum(spread, 0.5)
    key_row = lax.broadcasted_iota(jnp.int32, (W, W), 0)
    query_col = lax.broadcasted_iota(jnp.int32, (W, W), 1)
    for o in range(2):
        for b in range(2):
            answer = s.meta[o, b, 7:8, :]
            row = jnp.zeros((1, W), F32)
            for i in range(16):
                row = row + jnp.where(answer == i, apart[i], 0.0)
            row = row / divisor * scale
            s.wt[o, b] = jnp.transpose(jnp.broadcast_to(row, (W, W)))
            of_query = jnp.broadcast_to(s.meta[o, b, 6:7, :].astype(F32), (W, W))
            of_key = jnp.transpose(of_query)
            seen = (key_row <= query_col) & (of_query >= 0.0)
            seen = seen & ((of_key == of_query) | (of_key == 0.0))
            seen = seen | (key_row == query_col)
            s.mb[o, b] = jnp.where(seen, 0.0, -jnp.inf)

    await_bytes(s.scat.at[pl.ds(0, chips - 1)], s.pr_recv.at[0])
    prompt_slice = s.scat[root_chip]
    s.sel[...] = prompt_slice
    s.gath[chip] = prompt_slice
    to_chips(
        lambda c: loop_send(s.sel, s.gath.at[chip], s.pr_send.at[1], s.pr_recv.at[1], 2 * c + core)
    )

    def where_is(t, h):
        return lax.rem(core + t // 2 + h, 2), lax.rem(t, 2)

    def gather_block(t, h, kv, to):
        o, b = where_is(t, h)
        to[t, 0 : 2 * W] = s.gath[:, h, kv].reshape(T, W)
        for i in range(HOPS):
            chosen = s.meta[o, b, 5 - i : 6 - i, :]
            both = s.kvp[kv, h, o + i].astype(F32)
            picked = jnp.where(jnp.broadcast_to(chosen, (W, W)) == 1, both[W:], both[:W])
            to[t, (2 + i) * W : (3 + i) * W] = picked.astype(BF16)
        to[t, 6 * W :] = s.kvp[kv, h, o + 4, pl.ds(pl.multiple_of(b * W, W), W), :]

    def spread_block(t, h):
        o, b = where_is(t, h)
        s.pacc[...] += s.acc[0 : 2 * W]
        for i in range(HOPS):
            chosen = jnp.broadcast_to(s.meta[o, b, 5 - i : 6 - i, :], (W, W)) == 1
            x = s.acc[(2 + i) * W : (3 + i) * W]
            s.gacc[o + i, 0:W] += jnp.where(chosen, 0.0, x)
            s.gacc[o + i, W:] += jnp.where(chosen, x, 0.0)
        s.gacc[o + 4, pl.ds(pl.multiple_of(b * W, W), W), :] += s.acc[6 * W :]

    def pair(ref, o, h, b, g):
        rows = pl.ds(pl.multiple_of(b * W, W), W)
        return [ref.at[o, h, rows, pl.ds((2 * g + i) * W, W)] for i in range(2)]

    def forward(h):
        def step(t, carry):
            o, b = where_is(t, h)
            gather_block(t, h, K_, s.ku)
            gather_block(t, h, V_, s.vu)
            bias = []
            for i in range(6):
                row = s.meta[o, b, (0, 1, 5, 4, 3, 2)[i] : (0, 1, 5, 4, 3, 2)[i] + 1, :]
                unseen = row <= 0 if i < 2 else row < 0
                row = jnp.where(unseen, -jnp.inf, 0.0)
                bias.append(jnp.concatenate([row, row], axis=1))
            mask = jnp.concatenate([s.mb[o, b], s.mb[o, b]], axis=1)
            weight = s.wt[o, b]
            for g in range(4):
                queries = jnp.concatenate([x[...] for x in pair(s.qb, o, h, b, g)], axis=0)
                scores = nt(s.ku[t], queries)
                s.ps[0 : 6 * W] = scores[0 : 6 * W]
                s.ps[6 * W :] = scores[6 * W :] + mask
                peak = jnp.max(s.ps[6 * W :], axis=0, keepdims=True)
                for i in range(6):
                    top = jnp.max(s.ps[i * W : (i + 1) * W], axis=0, keepdims=True)
                    peak = jnp.maximum(peak, top + bias[i])
                shift = peak * exp_scale
                denominator = jnp.zeros((1, 2 * W), F32)
                for i in range(7):
                    here = shift if i == 6 else shift - bias[i]
                    e = jnp.exp2(s.ps[i * W : (i + 1) * W] * exp_scale - here)
                    s.ps[i * W : (i + 1) * W] = e
                    denominator = denominator + jnp.sum(e, axis=0, keepdims=True)
                probs = s.ps[...] * (1.0 / denominator)
                s.pf[t, g] = probs
                low = probs.astype(BF16)
                up = [x[...].astype(F32) * weight for x in pair(s.ub, o, h, b, g)]
                grad_out = jnp.concatenate(up, axis=0).astype(BF16)
                s.do[t, g] = grad_out
                attended = jnp.transpose(tn(s.vu[t], low)).astype(BF16)
                for i, x in enumerate(pair(s.ob, o, h, b, g)):
                    x[...] = attended[i * W : (i + 1) * W]
                product = grad_out.astype(F32) * attended.astype(F32)
                s.dl[t, g, 0:1] = jnp.sum(jnp.transpose(product), axis=0, keepdims=True)
                term = nn(low, grad_out)
                if g == 0:
                    s.acc[...] = term
                else:
                    s.acc[...] += term
            spread_block(t, h)
            return carry

        lax.fori_loop(0, 4, step, 0)

    def backward(h):
        def step(t, carry):
            o, b = where_is(t, h)
            for g in range(4):
                queries = jnp.concatenate([x[...] for x in pair(s.qb, o, h, b, g)], axis=0)
                dprobs = nt(s.vu[t], s.do[t, g])
                dscores = s.pf[t, g] * (dprobs - s.dl[t, g, 0:1]) * inv_root
                dscores = dscores.astype(BF16)
                grad = jnp.transpose(tn(s.ku[t], dscores)).astype(BF16)
                for i, x in enumerate(pair(s.gb, o, h, b, g)):
                    x[...] = grad[i * W : (i + 1) * W]
                term = nn(dscores, queries)
                if g == 0:
                    s.acc[...] = term
                else:
                    s.acc[...] += term
            spread_block(t, h)
            return carry

        lax.fori_loop(0, 4, step, 0)

    def clear():
        s.gacc[...] = jnp.zeros_like(s.gacc)
        s.pacc[...] = jnp.zeros_like(s.pacc)

    def send_grads(kv, h):
        for i in range(4):
            s.gsend[kv, h, i] = s.gacc[i].astype(BF16)
            hop = 2 if i < 2 else 1
            send(
                s.gsend.at[kv, h, i],
                s.grecv.at[kv, h, hop - 1, core],
                s.g_recv.at[kv, h],
                2 * lax.rem(chip - hop + chips, chips) + i % 2,
            )
        s.psend[kv, h] = s.pacc[...].reshape(16, 16, W).astype(BF16)
        to_chips(
            lambda c: loop_send(
                s.psend.at[kv, h, c],
                s.prec.at[kv, h, chip],
                s.ps_send.at[kv, h],
                s.ps_recv.at[kv, h],
                2 * c + core,
            )
        )
        s.prec[kv, h, chip] = s.psend[kv, h, chip]
        s.msend[kv, h] = s.gacc[4 + other]
        send(s.msend.at[kv, h], s.mrecv.at[kv, h], s.m_recv.at[kv, h], mate)
        s.own[kv, h] = s.gacc[4 + core]

    own_out = []

    def send_rows(staged, out, h, recv_sem):
        send(staged.at[other, h], out.at[:, qcols(core, h)], recv_sem, mate)
        own_out.append(fetch(staged.at[core, h], out.at[:, qcols(core, h)]))

    def sum_prompt(h):
        for kv in range(2):
            await_bytes(s.prec.at[kv, h, pl.ds(0, chips - 1)], s.ps_recv.at[kv, h])
            summed = jnp.sum(s.prec[kv, h].astype(F32), axis=0).astype(BF16)
            s.agsend[h, kv] = summed
            s.ag[h, 16 * core + chip, kv] = summed

        def step(i, carry):
            loop_send(
                s.agsend.at[h],
                s.ag.at[h, 16 * core + chip],
                s.ag_send.at[h],
                s.ag_recv.at[h],
                lax.rem(me + i, ring),
            )
            return carry

        lax.fori_loop(1, ring, step, 0)

    def finish(h):
        await_bytes(s.ag.at[h, pl.ds(0, ring - 1)], s.ag_recv.at[h])
        for kv, out in ((K_, gk), (V_, gv)):
            await_bytes(s.grecv.at[kv, h], s.g_recv.at[kv, h])
            await_bytes(s.mrecv.at[kv, h], s.m_recv.at[kv, h])
            for lane, mine in ((core, s.own), (other, s.mrecv)):
                x = mine[kv, h] + s.grecv[kv, h, 0, lane].astype(F32)
                x = x + s.grecv[kv, h, 1, lane].astype(F32)
                prompt = s.ag[h, pl.ds(16 * lane, 16), kv].astype(F32).reshape(T, W)
                here = jnp.full((T, W), root, jnp.int32) == me
                out[:, kcols(lane, h)] = x + jnp.where(here, prompt, 0.0)

    for h in range(2):
        if h == 0:
            await_bytes(s.gath.at[pl.ds(0, chips - 1)], s.pr_recv.at[1])
        for kv in range(2):
            await_bytes(s.kvp.at[kv, h, pl.ds(0, 4)], s.kv_recv.at[kv, h])
            await_bytes((s.qb, s.ub)[kv].at[other, h], s.qu_recv.at[h, kv])
            own_qu[h][kv].wait()
        clear()
        forward(h)
        send_grads(V_, h)
        send_rows(s.ob, attn, h, s.out_recv.at[0, h])
        if h == 1:
            sum_prompt(0)
        clear()
        backward(h)
        send_grads(K_, h)
        send_rows(s.gb, gq, h, s.out_recv.at[1, h])
    finish(0)
    sum_prompt(1)
    finish(1)

    for copy in own_out:
        copy.wait()
    for h in range(2):
        for i in range(2):
            await_bytes(s.ob.at[other, h], s.out_recv.at[i, h])
    for copy in sends:
        copy.wait_send()
    await_bytes(s.lens.at[pl.ds(0, groups - 1)], s.lens_send)
    for i in range(2):
        await_bytes(s.scat.at[pl.ds(0, chips - 1)], s.pr_send.at[i])
        await_bytes(s.ag.at[i, pl.ds(0, ring - 1)], s.ag_send.at[i])
        for h in range(2):
            await_bytes(s.prec.at[i, h, pl.ds(0, chips - 1)], s.ps_send.at[i, h])


def body(queries, keys, values, upstream, ancestors, segments, responses, rewards, lengths):
    any_spec = pl.BlockSpec(memory_space=pl.ANY)
    smem = pl.BlockSpec(memory_space=pltpu.SMEM)
    vmem = pl.BlockSpec(memory_space=pltpu.VMEM)
    return pl.pallas_call(
        functools.partial(kernel, lax.axis_size("dp"), lax.axis_size("ctx")),
        out_shape=[
            jax.ShapeDtypeStruct(queries.shape, BF16),
            jax.ShapeDtypeStruct(queries.shape, BF16),
            jax.ShapeDtypeStruct(keys.shape, F32),
            jax.ShapeDtypeStruct(keys.shape, F32),
        ],
        in_specs=[any_spec] * 4 + [smem, vmem, vmem, smem, smem],
        out_specs=[vmem] * 4,
        scratch_shapes=list(SCRATCH.values()),
        compiler_params=pltpu.CompilerParams(
            collective_id=0, has_side_effects=True, vmem_limit_bytes=60 * 1024 * 1024
        ),
    )(
        queries,
        keys,
        values,
        upstream,
        ancestors,
        segments.reshape(2, W),
        responses.reshape(2, W),
        rewards,
        lengths,
    )


def solution(mesh):
    rows, flat = P(("dp", "ctx"), None), P(("dp", "ctx"))
    return jax.shard_map(
        body,
        mesh=mesh,
        in_specs=(rows, rows, rows, rows, rows, flat, flat, P("dp"), P("dp")),
        out_specs=(rows, rows, rows, rows),
        check_vma=False,
    )
```

```python
import functools
import math

import jax
import jax.numpy as jnp
from jax import lax
from jax.experimental import pallas as pl
from jax.experimental.pallas import tpu as pltpu
from jax.sharding import PartitionSpec as P

MESH = pl.DeviceIdType.MESH
F32, BF16 = jnp.float32, jnp.bfloat16
W = 128
T = 2 * W
R = 8
C = R * W
N = 7 * W
HOPS = 4
K_, V_ = 0, 1


def nn(a, b):
    return lax.dot_general(a, b, (((1,), (0,)), ((), ())), preferred_element_type=F32)


def nt(a, b):
    return lax.dot_general(a, b, (((1,), (1,)), ((), ())), preferred_element_type=F32)


def tn(a, b):
    return lax.dot_general(a, b, (((0,), (0,)), ((), ())), preferred_element_type=F32)


SCRATCH = dict(
    kvp=pltpu.VMEM((2, 2, 6, T, W), BF16),
    qb=pltpu.VMEM((2, 2, T, C), BF16),
    ub=pltpu.VMEM((2, 2, T, C), BF16),
    ob=pltpu.VMEM((2, 2, T, C), BF16),
    gb=pltpu.VMEM((2, 2, T, C), BF16),
    cand=pltpu.VMEM((16, 2, 2, 16, W), BF16),
    scat=pltpu.VMEM((16, 2, 2, 16, W), BF16),
    sel=pltpu.VMEM((2, 2, 16, W), BF16),
    gath=pltpu.VMEM((16, 2, 2, 16, W), BF16),
    meta=pltpu.VMEM((2, 2, 8, W), jnp.int32),
    lens=pltpu.VMEM((4, 8, W), jnp.int32),
    wt=pltpu.VMEM((2, 2, W, W), F32),
    mb=pltpu.VMEM((2, 2, W, W), F32),
    ku=pltpu.VMEM((4, N, W), BF16),
    vu=pltpu.VMEM((4, N, W), BF16),
    kt=pltpu.VMEM((4, W, N), BF16),
    vt=pltpu.VMEM((4, W, N), BF16),
    pf=pltpu.VMEM((16, N, 2 * W), F32),
    dl=pltpu.VMEM((16, 8, 2 * W), F32),
    do=pltpu.VMEM((16, 2 * W, W), BF16),
    ps0=pltpu.VMEM((N, 2 * W), F32),
    ps1=pltpu.VMEM((N, 2 * W), F32),
    pk0=pltpu.VMEM((8, 2 * W), F32),
    pk1=pltpu.VMEM((8, 2 * W), F32),
    low0=pltpu.VMEM((N, 2 * W), BF16),
    low1=pltpu.VMEM((N, 2 * W), BF16),
    do0=pltpu.VMEM((2 * W, W), BF16),
    do1=pltpu.VMEM((2 * W, W), BF16),
    acc=pltpu.VMEM((4, N, W), F32),
    gacc=pltpu.VMEM((6, T, W), F32),
    pacc=pltpu.VMEM((T, W), F32),
    own=pltpu.VMEM((2, 2, T, W), F32),
    msend=pltpu.VMEM((2, 2, T, W), F32),
    mrecv=pltpu.VMEM((2, 2, T, W), F32),
    gsend=pltpu.VMEM((2, 2, 4, T, W), BF16),
    grecv=pltpu.VMEM((2, 2, 2, 2, T, W), BF16),
    psend=pltpu.VMEM((2, 2, 16, 16, W), BF16),
    prec=pltpu.VMEM((2, 2, 16, 16, W), BF16),
    agsend=pltpu.VMEM((2, 2, 16, W), BF16),
    ag=pltpu.VMEM((2, 32, 2, 16, W), BF16),
    one_send=pltpu.SemaphoreType.DMA((64,)),
    local=pltpu.SemaphoreType.DMA((12,)),
    kv_recv=pltpu.SemaphoreType.DMA((2, 2)),
    mate_kv=pltpu.SemaphoreType.DMA,
    meta_recv=pltpu.SemaphoreType.DMA,
    lens_send=pltpu.SemaphoreType.DMA,
    lens_recv=pltpu.SemaphoreType.DMA,
    qu_recv=pltpu.SemaphoreType.DMA((2, 2)),
    out_recv=pltpu.SemaphoreType.DMA((2, 2)),
    pr_send=pltpu.SemaphoreType.DMA((2,)),
    pr_recv=pltpu.SemaphoreType.DMA((2,)),
    g_recv=pltpu.SemaphoreType.DMA((2, 2)),
    m_recv=pltpu.SemaphoreType.DMA((2, 2)),
    ps_send=pltpu.SemaphoreType.DMA((2, 2)),
    ps_recv=pltpu.SemaphoreType.DMA((2, 2)),
    ag_send=pltpu.SemaphoreType.DMA((2,)),
    ag_recv=pltpu.SemaphoreType.DMA((2,)),
)


class Names:
    def __init__(self, names, refs):
        for name, ref in zip(names, refs):
            setattr(self, name, ref)


def kernel(groups, ring, q, k, v, u, anc, seg, resp, rew, leng, attn, gq, gk, gv, *refs):
    s = Names(list(SCRATCH), refs)
    me, z = lax.axis_index("ctx"), lax.axis_index("dp")
    chips = ring // 2
    chip, core = me // 2, lax.rem(me, 2)
    other = 1 - core
    mate = 2 * chip + other
    inv_root = 1.0 / math.sqrt(W)
    exp_scale = math.log2(math.e) * inv_root

    first = anc[0, 0]
    root = jnp.where(first < 0, me, lax.div(first, 2))
    root_chip, root_core = lax.div(root, 2), lax.rem(root, 2)

    sends = []

    def send(src, dst, recv_sem, to):
        copy = pltpu.make_async_remote_copy(
            src_ref=src,
            dst_ref=dst,
            send_sem=s.one_send.at[len(sends)],
            recv_sem=recv_sem,
            device_id={"ctx": to},
            device_id_type=MESH,
        )
        copy.start()
        sends.append(copy)

    def await_bytes(ref, sem):
        pltpu.make_async_copy(ref, ref, sem).wait()

    barrier = pltpu.get_barrier_semaphore()

    def greet(i, carry):
        pl.semaphore_signal(
            barrier, inc=1, device_id={"ctx": lax.rem(me + i, ring)}, device_id_type=MESH
        )
        return carry

    lax.fori_loop(1, ring, greet, 0)
    for i in range(1, groups):
        pl.semaphore_signal(
            barrier, inc=1, device_id={"dp": lax.rem(z + i, groups)}, device_id_type=MESH
        )

    def kcols(lane, h):
        return pl.ds(pl.multiple_of((2 * lane + h) * W, W), W)

    def qcols(lane, h):
        return pl.ds(pl.multiple_of((2 * lane + h) * C, C), C)

    local = []

    def fetch(src, dst):
        copy = pltpu.make_async_copy(src, dst, s.local.at[len(local)])
        copy.start()
        local.append(copy)
        return copy

    own_kv = [
        fetch(src.at[:, kcols(core, h)], s.kvp.at[kv, h, 4 + core])
        for h in range(2)
        for kv, src in ((K_, k), (V_, v))
    ]
    own_qu = [
        (
            fetch(q.at[:, qcols(core, h)], s.qb.at[core, h]),
            fetch(u.at[:, qcols(core, h)], s.ub.at[core, h]),
        )
        for h in range(2)
    ]

    total = leng[0]
    for i in range(1, 16):
        total = total + leng[i]
    s.lens[z] = jnp.full((8, W), total, jnp.int32)
    for b in range(2):
        rows = [jnp.where(anc[b, 0] >= 0, 1, 0), jnp.where(anc[b, 1] >= 0, 1, 0)]
        for hop in range(1, HOPS + 1):
            chosen = jnp.int32(-1)
            for slot in range(2, 6):
                a = anc[b, slot]
                away = lax.rem(me - lax.div(jnp.maximum(a, 0), 2) + ring, ring)
                chosen = jnp.where((a >= 0) & (away == hop), lax.rem(a, 2), chosen)
            rows.append(chosen)
        for i, row in enumerate(rows):
            s.meta[core, b, i : i + 1, :] = jnp.full((1, W), row, jnp.int32)
        s.meta[core, b, 6:7, :] = seg[b : b + 1, :]
        s.meta[core, b, 7:8, :] = resp[b : b + 1, :]

    pl.semaphore_wait(barrier, ring - 1 + groups - 1)

    for h in range(2):
        for kv, src in ((K_, k), (V_, v)):
            send(src.at[:, kcols(other, h)], s.kvp.at[kv, h, 4 + core], s.mate_kv, mate)
    for i in range(1, groups):
        pltpu.make_async_remote_copy(
            src_ref=s.lens.at[z],
            dst_ref=s.lens.at[z],
            send_sem=s.lens_send,
            recv_sem=s.lens_recv,
            device_id={"dp": lax.rem(z + i, groups)},
            device_id_type=MESH,
        ).start()
    send(s.meta.at[core], s.meta.at[core], s.meta_recv, mate)

    def send_chain(h):
        for kv, src in ((K_, k), (V_, v)):
            for hop in (1, 2):
                for lane in range(2):
                    send(
                        src.at[:, kcols(lane, h)],
                        s.kvp.at[kv, h, 2 * (2 - hop) + core],
                        s.kv_recv.at[kv, h],
                        2 * lax.rem(chip + hop, chips) + lane,
                    )

    def send_qu(h):
        send(q.at[:, qcols(other, h)], s.qb.at[core, h], s.qu_recv.at[h, 0], mate)
        send(u.at[:, qcols(other, h)], s.ub.at[core, h], s.qu_recv.at[h, 1], mate)

    send_chain(0)
    send_qu(0)

    for copy in own_kv:
        copy.wait()
    await_bytes(s.kvp.at[0, 0, pl.ds(0, 4)], s.mate_kv)
    for h in range(2):
        for kv in range(2):
            x = lax.select(root_core == 0, s.kvp[kv, h, 4], s.kvp[kv, h, 5])
            s.cand[:, h, kv] = x.reshape(16, 16, W)

    def to_chips(start):
        def step(i, carry):
            start(lax.rem(chip + i, chips))
            return carry

        lax.fori_loop(1, chips, step, 0)

    def loop_send(src, dst, send_sem, recv_sem, to):
        pltpu.make_async_remote_copy(
            src_ref=src,
            dst_ref=dst,
            send_sem=send_sem,
            recv_sem=recv_sem,
            device_id={"ctx": to},
            device_id_type=MESH,
        ).start()

    to_chips(
        lambda c: loop_send(
            s.cand.at[c], s.scat.at[chip], s.pr_send.at[0], s.pr_recv.at[0], 2 * c + core
        )
    )
    s.scat[chip] = s.cand[chip]
    send_chain(1)
    send_qu(1)

    await_bytes(s.meta.at[0], s.meta_recv)
    await_bytes(s.lens.at[pl.ds(0, groups - 1)], s.lens_recv)
    everything = s.lens[0, 0:1, :]
    for i in range(1, groups):
        everything = everything + s.lens[i, 0:1, :]
    scale = float(groups * 16 * W) / everything.astype(F32)
    scored = [rew[i].astype(F32) for i in range(16)]
    centre = functools.reduce(lambda a, b: a + b, scored) * (1.0 / 16)
    apart = [x - centre for x in scored]
    variance = functools.reduce(lambda a, b: a + b, [x * x for x in apart]) * (1.0 / 16)
    spread = jnp.sqrt(jnp.full((1, W), variance, F32))
    divisor = jnp.maximum(spread, 0.5)
    key_row = lax.broadcasted_iota(jnp.int32, (W, W), 0)
    query_col = lax.broadcasted_iota(jnp.int32, (W, W), 1)
    for o in range(2):
        for b in range(2):
            answer = s.meta[o, b, 7:8, :]
            row = jnp.zeros((1, W), F32)
            for i in range(16):
                row = row + jnp.where(answer == i, apart[i], 0.0)
            row = row / divisor * scale
            s.wt[o, b] = jnp.transpose(jnp.broadcast_to(row, (W, W)))
            of_query = jnp.broadcast_to(s.meta[o, b, 6:7, :].astype(F32), (W, W))
            of_key = jnp.transpose(of_query)
            seen = (key_row <= query_col) & (of_query >= 0.0)
            seen = seen & ((of_key == of_query) | (of_key == 0.0))
            seen = seen | (key_row == query_col)
            s.mb[o, b] = jnp.where(seen, 0.0, -jnp.inf)

    await_bytes(s.scat.at[pl.ds(0, chips - 1)], s.pr_recv.at[0])
    prompt_slice = s.scat[root_chip]
    s.sel[...] = prompt_slice
    s.gath[chip] = prompt_slice
    to_chips(
        lambda c: loop_send(s.sel, s.gath.at[chip], s.pr_send.at[1], s.pr_recv.at[1], 2 * c + core)
    )

    def where_is(t, h):
        return lax.rem(core + t // 2 + h, 2), lax.rem(t, 2)

    def gather_block(t, h, kv, to):
        o, b = where_is(t, h)
        to[t, 0 : 2 * W] = s.gath[:, h, kv].reshape(T, W)
        for i in range(HOPS):
            chosen = s.meta[o, b, 5 - i : 6 - i, :]
            both = s.kvp[kv, h, o + i].astype(F32)
            picked = jnp.where(jnp.broadcast_to(chosen, (W, W)) == 1, both[W:], both[:W])
            to[t, (2 + i) * W : (3 + i) * W] = picked.astype(BF16)
        to[t, 6 * W :] = s.kvp[kv, h, o + 4, pl.ds(pl.multiple_of(b * W, W), W), :]

    def spread_blocks(h):
        def step(t, carry):
            o, b = where_is(t, h)
            s.pacc[...] += s.acc[t, 0 : 2 * W]
            for i in range(HOPS):
                chosen = jnp.broadcast_to(s.meta[o, b, 5 - i : 6 - i, :], (W, W)) == 1
                x = s.acc[t, (2 + i) * W : (3 + i) * W]
                s.gacc[o + i, 0:W] += jnp.where(chosen, 0.0, x)
                s.gacc[o + i, W:] += jnp.where(chosen, x, 0.0)
            s.gacc[o + 4, pl.ds(pl.multiple_of(b * W, W), W), :] += s.acc[t, 6 * W :]
            return carry

        lax.fori_loop(0, 4, step, 0)

    def chunk(j, h):
        t = j // 4
        o, b = where_is(t, h)
        return t, o, b, lax.rem(j, 4)

    def pair(ref, o, h, b, g):
        rows = pl.ds(pl.multiple_of(b * W, W), W)
        return [
            ref.at[o, h, rows, pl.ds(pl.multiple_of((2 * g + i) * W, W), W)] for i in range(2)
        ]

    def joined(ref, o, h, b, g):
        return jnp.concatenate([x[...] for x in pair(ref, o, h, b, g)], axis=0)

    def twice(row):
        return jnp.concatenate([row, row], axis=1)

    META_ROWS = (0, 1, 5, 4, 3, 2)

    def biases(o, b):
        rows = []
        for i in range(6):
            row = s.meta[o, b, META_ROWS[i] : META_ROWS[i] + 1, :]
            unseen = row <= 0 if i < 2 else row < 0
            rows.append(twice(jnp.where(unseen, -jnp.inf, 0.0)))
        return rows

    def score(j, h, ps, pk):
        t, o, b, g = chunk(j, h)
        scores = nt(s.ku[t], joined(s.qb, o, h, b, g))
        seen = scores[6 * W :] + twice(s.mb[o, b])
        peak = jnp.max(seen, axis=0, keepdims=True)
        for i, bias in enumerate(biases(o, b)):
            top = jnp.max(scores[i * W : (i + 1) * W], axis=0, keepdims=True)
            peak = jnp.maximum(peak, top + bias)
        ps[0 : 6 * W] = scores[0 : 6 * W]
        ps[6 * W :] = seen
        pk[0:1] = peak * exp_scale

    def soften(j, h, ps, pk, low, do):
        t, o, b, g = chunk(j, h)
        shift = pk[0:1]
        bias = biases(o, b)
        denominator = jnp.zeros((1, 2 * W), F32)
        for i in range(7):
            here = shift if i == 6 else shift - bias[i]
            e = jnp.exp2(ps[i * W : (i + 1) * W] * exp_scale - here)
            ps[i * W : (i + 1) * W] = e
            denominator = denominator + jnp.sum(e, axis=0, keepdims=True)
        inverse = 1.0 / denominator
        for i in range(7):
            probs = ps[i * W : (i + 1) * W] * inverse
            s.pf[j, i * W : (i + 1) * W] = probs
            low[i * W : (i + 1) * W] = probs.astype(BF16)
        weight = s.wt[o, b]
        up = [x[...].astype(F32) * weight for x in pair(s.ub, o, h, b, g)]
        grad_out = jnp.concatenate(up, axis=0).astype(BF16)
        do[...] = grad_out
        s.do[j] = grad_out

    def attend(j, h, low, do):
        t, o, b, g = chunk(j, h)
        attended = jnp.transpose(nn(s.vt[t], low[...])).astype(BF16)
        s.acc[t] += nn(low[...], do[...])
        for i, x in enumerate(pair(s.ob, o, h, b, g)):
            x[...] = attended[i * W : (i + 1) * W]
        product = do[...].astype(F32) * attended.astype(F32)
        s.dl[j, 0:1] = jnp.sum(jnp.transpose(product), axis=0, keepdims=True)

    def forward(h):
        def prepare(t, carry):
            gather_block(t, h, K_, s.ku)
            gather_block(t, h, V_, s.vu)
            s.kt[t] = jnp.transpose(s.ku[t])
            s.vt[t] = jnp.transpose(s.vu[t])
            return carry

        lax.fori_loop(0, 4, prepare, 0)
        s.acc[...] = jnp.zeros_like(s.acc)
        even, odd = (s.ps0, s.pk0), (s.ps1, s.pk1)
        low_even, low_odd = (s.low0, s.do0), (s.low1, s.do1)
        score(0, h, *even)
        score(1, h, *odd)
        soften(0, h, *even, *low_even)

        def step(i, carry):
            j = 2 * i
            attend(j - 2, h, *low_even)
            score(j, h, *even)
            soften(j - 1, h, *odd, *low_odd)
            attend(j - 1, h, *low_odd)
            score(j + 1, h, *odd)
            soften(j, h, *even, *low_even)
            return carry

        lax.fori_loop(1, 8, step, 0)
        attend(14, h, *low_even)
        soften(15, h, *odd, *low_odd)
        attend(15, h, *low_odd)
        spread_blocks(h)

    def score_grad(j, h, low):
        t, o, b, g = chunk(j, h)
        dprobs = nt(s.vu[t], s.do[j])
        low[...] = (s.pf[j] * (dprobs - s.dl[j, 0:1]) * inv_root).astype(BF16)

    def input_grads(j, h, low):
        t, o, b, g = chunk(j, h)
        grad = jnp.transpose(nn(s.kt[t], low[...])).astype(BF16)
        s.acc[t] += nn(low[...], joined(s.qb, o, h, b, g))
        for i, x in enumerate(pair(s.gb, o, h, b, g)):
            x[...] = grad[i * W : (i + 1) * W]

    def backward(h):
        s.acc[...] = jnp.zeros_like(s.acc)
        score_grad(0, h, s.low0)

        def step(i, carry):
            j = 2 * i
            score_grad(j + 1, h, s.low1)
            input_grads(j, h, s.low0)
            score_grad(j + 2, h, s.low0)
            input_grads(j + 1, h, s.low1)
            return carry

        lax.fori_loop(0, 7, step, 0)
        score_grad(15, h, s.low1)
        input_grads(14, h, s.low0)
        input_grads(15, h, s.low1)
        spread_blocks(h)

    def clear():
        s.gacc[...] = jnp.zeros_like(s.gacc)
        s.pacc[...] = jnp.zeros_like(s.pacc)

    def send_grads(kv, h):
        for i in range(4):
            s.gsend[kv, h, i] = s.gacc[i].astype(BF16)
            hop = 2 if i < 2 else 1
            send(
                s.gsend.at[kv, h, i],
                s.grecv.at[kv, h, hop - 1, core],
                s.g_recv.at[kv, h],
                2 * lax.rem(chip - hop + chips, chips) + i % 2,
            )
        s.psend[kv, h] = s.pacc[...].reshape(16, 16, W).astype(BF16)
        to_chips(
            lambda c: loop_send(
                s.psend.at[kv, h, c],
                s.prec.at[kv, h, chip],
                s.ps_send.at[kv, h],
                s.ps_recv.at[kv, h],
                2 * c + core,
            )
        )
        s.prec[kv, h, chip] = s.psend[kv, h, chip]
        s.msend[kv, h] = s.gacc[4 + other]
        send(s.msend.at[kv, h], s.mrecv.at[kv, h], s.m_recv.at[kv, h], mate)
        s.own[kv, h] = s.gacc[4 + core]

    own_out = []

    def send_rows(staged, out, h, recv_sem):
        send(staged.at[other, h], out.at[:, qcols(core, h)], recv_sem, mate)
        own_out.append(fetch(staged.at[core, h], out.at[:, qcols(core, h)]))

    def sum_prompt(h):
        for kv in range(2):
            await_bytes(s.prec.at[kv, h, pl.ds(0, chips - 1)], s.ps_recv.at[kv, h])
            summed = jnp.sum(s.prec[kv, h].astype(F32), axis=0).astype(BF16)
            s.agsend[h, kv] = summed
            s.ag[h, 16 * core + chip, kv] = summed

        def step(i, carry):
            loop_send(
                s.agsend.at[h],
                s.ag.at[h, 16 * core + chip],
                s.ag_send.at[h],
                s.ag_recv.at[h],
                lax.rem(me + i, ring),
            )
            return carry

        lax.fori_loop(1, ring, step, 0)

    def finish(h):
        await_bytes(s.ag.at[h, pl.ds(0, ring - 1)], s.ag_recv.at[h])
        for kv, out in ((K_, gk), (V_, gv)):
            await_bytes(s.grecv.at[kv, h], s.g_recv.at[kv, h])
            await_bytes(s.mrecv.at[kv, h], s.m_recv.at[kv, h])
            for lane, mine in ((core, s.own), (other, s.mrecv)):
                x = mine[kv, h] + s.grecv[kv, h, 0, lane].astype(F32)
                x = x + s.grecv[kv, h, 1, lane].astype(F32)
                prompt = s.ag[h, pl.ds(16 * lane, 16), kv].astype(F32).reshape(T, W)
                here = jnp.full((T, W), root, jnp.int32) == me
                out[:, kcols(lane, h)] = x + jnp.where(here, prompt, 0.0)

    for h in range(2):
        if h == 0:
            await_bytes(s.gath.at[pl.ds(0, chips - 1)], s.pr_recv.at[1])
        for kv in range(2):
            await_bytes(s.kvp.at[kv, h, pl.ds(0, 4)], s.kv_recv.at[kv, h])
            await_bytes((s.qb, s.ub)[kv].at[other, h], s.qu_recv.at[h, kv])
            own_qu[h][kv].wait()
        clear()
        forward(h)
        send_grads(V_, h)
        send_rows(s.ob, attn, h, s.out_recv.at[0, h])
        if h == 1:
            sum_prompt(0)
        clear()
        backward(h)
        send_grads(K_, h)
        send_rows(s.gb, gq, h, s.out_recv.at[1, h])
    finish(0)
    sum_prompt(1)
    finish(1)

    for copy in own_out:
        copy.wait()
    for h in range(2):
        for i in range(2):
            await_bytes(s.ob.at[other, h], s.out_recv.at[i, h])
    for copy in sends:
        copy.wait_send()
    await_bytes(s.lens.at[pl.ds(0, groups - 1)], s.lens_send)
    for i in range(2):
        await_bytes(s.scat.at[pl.ds(0, chips - 1)], s.pr_send.at[i])
        await_bytes(s.ag.at[i, pl.ds(0, ring - 1)], s.ag_send.at[i])
        for h in range(2):
            await_bytes(s.prec.at[i, h, pl.ds(0, chips - 1)], s.ps_send.at[i, h])


def write_out(*refs):
    sems = refs[8]
    copies = [pltpu.make_async_copy(refs[i], refs[4 + i], sems.at[i]) for i in range(4)]
    for copy in copies:
        copy.start()
    for copy in copies:
        copy.wait()


def body(queries, keys, values, upstream, ancestors, segments, responses, rewards, lengths):
    any_spec = pl.BlockSpec(memory_space=pltpu.HBM)
    smem = pl.BlockSpec(memory_space=pltpu.SMEM)
    vmem = pl.BlockSpec(memory_space=pltpu.VMEM)
    results = pl.pallas_call(
        functools.partial(kernel, lax.axis_size("dp"), lax.axis_size("ctx")),
        out_shape=[
            pltpu.VMEM(queries.shape, BF16),
            pltpu.VMEM(queries.shape, BF16),
            pltpu.VMEM(keys.shape, F32),
            pltpu.VMEM(keys.shape, F32),
        ],
        in_specs=[any_spec] * 4 + [smem, vmem, vmem, smem, smem],
        out_specs=[vmem] * 4,
        scratch_shapes=list(SCRATCH.values()),
        compiler_params=pltpu.CompilerParams(
            collective_id=0, has_side_effects=True, vmem_limit_bytes=56 * 1024 * 1024
        ),
    )(
        queries,
        keys,
        values,
        upstream,
        ancestors,
        segments.reshape(2, W),
        responses.reshape(2, W),
        rewards,
        lengths,
    )
    return pl.pallas_call(
        write_out,
        out_shape=[jax.ShapeDtypeStruct(x.shape, x.dtype) for x in results],
        in_specs=[vmem] * 4,
        out_specs=[any_spec] * 4,
        scratch_shapes=[pltpu.SemaphoreType.DMA((4,))],
    )(*results)


def solution(mesh):
    rows, flat = P(("dp", "ctx"), None), P(("dp", "ctx"))
    return jax.shard_map(
        body,
        mesh=mesh,
        in_specs=(rows, rows, rows, rows, rows, flat, flat, P("dp"), P("dp")),
        out_specs=(rows, rows, rows, rows),
        check_vma=False,
    )
```

```python
import functools
import math

import jax
import jax.numpy as jnp
from jax import lax
from jax.experimental import pallas as pl
from jax.experimental.pallas import tpu as pltpu
from jax.sharding import PartitionSpec as P

MESH = pl.DeviceIdType.MESH
F32, BF16 = jnp.float32, jnp.bfloat16
W = 128
T = 2 * W
R = 8
C = R * W
N = 7 * W
HOPS = 4
K_, V_ = 0, 1


def nn(a, b):
    return lax.dot_general(a, b, (((1,), (0,)), ((), ())), preferred_element_type=F32)


def nt(a, b):
    return lax.dot_general(a, b, (((1,), (1,)), ((), ())), preferred_element_type=F32)


def tn(a, b):
    return lax.dot_general(a, b, (((0,), (0,)), ((), ())), preferred_element_type=F32)


SCRATCH = dict(
    kvp=pltpu.VMEM((2, 2, 6, T, W), BF16),
    qb=pltpu.VMEM((2, 2, T, C), BF16),
    ub=pltpu.VMEM((2, 2, T, C), BF16),
    ob=pltpu.VMEM((2, 2, T, C), BF16),
    gb=pltpu.VMEM((2, 2, T, C), BF16),
    cand=pltpu.VMEM((2, 16, 2, 16, W), BF16),
    scat0=pltpu.VMEM((16, 2, 16, W), BF16),
    scat1=pltpu.VMEM((16, 2, 16, W), BF16),
    sel=pltpu.VMEM((2, 2, 16, W), BF16),
    gath=pltpu.VMEM((2, 16, 2, 16, W), BF16),
    meta=pltpu.VMEM((2, 2, 8, W), jnp.int32),
    lens=pltpu.VMEM((4, 8, W), jnp.int32),
    wt=pltpu.VMEM((2, 2, W, W), F32),
    mb=pltpu.VMEM((2, 2, W, W), F32),
    ku=pltpu.VMEM((4, N, W), BF16),
    vu=pltpu.VMEM((4, N, W), BF16),
    kt=pltpu.VMEM((4, W, N), BF16),
    vt=pltpu.VMEM((4, W, N), BF16),
    pf=pltpu.VMEM((16, N, 2 * W), F32),
    dl=pltpu.VMEM((16, 8, 2 * W), F32),
    do=pltpu.VMEM((16, 2 * W, W), BF16),
    ps0=pltpu.VMEM((N, 2 * W), F32),
    ps1=pltpu.VMEM((N, 2 * W), F32),
    pk0=pltpu.VMEM((8, 2 * W), F32),
    pk1=pltpu.VMEM((8, 2 * W), F32),
    low0=pltpu.VMEM((N, 2 * W), BF16),
    low1=pltpu.VMEM((N, 2 * W), BF16),
    do0=pltpu.VMEM((2 * W, W), BF16),
    do1=pltpu.VMEM((2 * W, W), BF16),
    acc=pltpu.VMEM((4, N, W), F32),
    gacc=pltpu.VMEM((6, T, W), F32),
    pacc=pltpu.VMEM((T, W), F32),
    own=pltpu.VMEM((2, 2, T, W), F32),
    msend=pltpu.VMEM((2, 2, T, W), F32),
    mrecv=pltpu.VMEM((2, 2, T, W), F32),
    gsend=pltpu.VMEM((2, 2, 4, T, W), BF16),
    grecv=pltpu.VMEM((2, 2, 2, 2, T, W), BF16),
    psend=pltpu.VMEM((2, 2, 16, 16, W), BF16),
    prec=pltpu.VMEM((2, 2, 16, 16, W), BF16),
    agsend=pltpu.VMEM((2, 2, 16, W), BF16),
    ag=pltpu.VMEM((2, 2, 32, 16, W), BF16),
    one_send=pltpu.SemaphoreType.DMA((64,)),
    local=pltpu.SemaphoreType.DMA((12,)),
    kv_recv=pltpu.SemaphoreType.DMA((2, 2)),
    mate_kv=pltpu.SemaphoreType.DMA,
    meta_recv=pltpu.SemaphoreType.DMA,
    lens_send=pltpu.SemaphoreType.DMA,
    lens_recv=pltpu.SemaphoreType.DMA,
    qu_recv=pltpu.SemaphoreType.DMA((2, 2)),
    out_recv=pltpu.SemaphoreType.DMA((2, 2)),
    pr_send=pltpu.SemaphoreType.DMA((2, 2)),
    pr_recv=pltpu.SemaphoreType.DMA((2, 2)),
    g_recv=pltpu.SemaphoreType.DMA((2, 2)),
    m_recv=pltpu.SemaphoreType.DMA((2, 2)),
    ps_send=pltpu.SemaphoreType.DMA((2, 2)),
    ps_recv=pltpu.SemaphoreType.DMA((2, 2)),
    ag_send=pltpu.SemaphoreType.DMA((2, 2)),
    ag_recv=pltpu.SemaphoreType.DMA((2, 2)),
)


class Names:
    def __init__(self, names, refs):
        for name, ref in zip(names, refs):
            setattr(self, name, ref)


def kernel(groups, ring, q, k, v, u, anc, seg, resp, rew, leng, attn, gq, gk, gv, *refs):
    s = Names(list(SCRATCH), refs)
    me, z = lax.axis_index("ctx"), lax.axis_index("dp")
    chips = ring // 2
    chip, core = me // 2, lax.rem(me, 2)
    other = 1 - core
    mate = 2 * chip + other
    inv_root = 1.0 / math.sqrt(W)
    exp_scale = math.log2(math.e) * inv_root

    first = anc[0, 0]
    root = jnp.where(first < 0, me, lax.div(first, 2))
    root_chip, root_core = lax.div(root, 2), lax.rem(root, 2)

    sends = []
    scat = (s.scat0, s.scat1)

    def send(src, dst, recv_sem, to):
        copy = pltpu.make_async_remote_copy(
            src_ref=src,
            dst_ref=dst,
            send_sem=s.one_send.at[len(sends)],
            recv_sem=recv_sem,
            device_id={"ctx": to},
            device_id_type=MESH,
        )
        copy.start()
        sends.append(copy)

    def await_bytes(ref, sem):
        pltpu.make_async_copy(ref, ref, sem).wait()

    barrier = pltpu.get_barrier_semaphore()

    def greet(i, carry):
        pl.semaphore_signal(
            barrier, inc=1, device_id={"ctx": lax.rem(me + i, ring)}, device_id_type=MESH
        )
        return carry

    lax.fori_loop(1, ring, greet, 0)
    for i in range(1, groups):
        pl.semaphore_signal(
            barrier, inc=1, device_id={"dp": lax.rem(z + i, groups)}, device_id_type=MESH
        )

    def kcols(lane, h):
        return pl.ds(pl.multiple_of((2 * lane + h) * W, W), W)

    def qcols(lane, h):
        return pl.ds(pl.multiple_of((2 * lane + h) * C, C), C)

    local = []

    def fetch(src, dst):
        copy = pltpu.make_async_copy(src, dst, s.local.at[len(local)])
        copy.start()
        local.append(copy)
        return copy

    own_kv = [
        fetch(src.at[:, kcols(core, h)], s.kvp.at[kv, h, 4 + core])
        for h in range(2)
        for kv, src in ((K_, k), (V_, v))
    ]
    own_qu = [
        (
            fetch(q.at[:, qcols(core, h)], s.qb.at[core, h]),
            fetch(u.at[:, qcols(core, h)], s.ub.at[core, h]),
        )
        for h in range(2)
    ]

    total = leng[0]
    for i in range(1, 16):
        total = total + leng[i]
    s.lens[z] = jnp.full((8, W), total, jnp.int32)
    for b in range(2):
        rows = [jnp.where(anc[b, 0] >= 0, 1, 0), jnp.where(anc[b, 1] >= 0, 1, 0)]
        for hop in range(1, HOPS + 1):
            chosen = jnp.int32(-1)
            for slot in range(2, 6):
                a = anc[b, slot]
                away = lax.rem(me - lax.div(jnp.maximum(a, 0), 2) + ring, ring)
                chosen = jnp.where((a >= 0) & (away == hop), lax.rem(a, 2), chosen)
            rows.append(chosen)
        for i, row in enumerate(rows):
            s.meta[core, b, i : i + 1, :] = jnp.full((1, W), row, jnp.int32)
        s.meta[core, b, 6:7, :] = seg[b : b + 1, :]
        s.meta[core, b, 7:8, :] = resp[b : b + 1, :]

    pl.semaphore_wait(barrier, ring - 1 + groups - 1)

    for h in range(2):
        for kv, src in ((K_, k), (V_, v)):
            send(src.at[:, kcols(other, h)], s.kvp.at[kv, h, 4 + core], s.mate_kv, mate)
    for i in range(1, groups):
        pltpu.make_async_remote_copy(
            src_ref=s.lens.at[z],
            dst_ref=s.lens.at[z],
            send_sem=s.lens_send,
            recv_sem=s.lens_recv,
            device_id={"dp": lax.rem(z + i, groups)},
            device_id_type=MESH,
        ).start()
    send(s.meta.at[core], s.meta.at[core], s.meta_recv, mate)

    def send_chain(h, kv, hop):
        for lane in range(2):
            send(
                (k, v)[kv].at[:, kcols(lane, h)],
                s.kvp.at[kv, h, 2 * (2 - hop) + core],
                s.kv_recv.at[kv, h],
                2 * lax.rem(chip + hop, chips) + lane,
            )

    def send_qu(h):
        send(q.at[:, qcols(other, h)], s.qb.at[core, h], s.qu_recv.at[h, 0], mate)
        send(u.at[:, qcols(other, h)], s.ub.at[core, h], s.qu_recv.at[h, 1], mate)

    for copy in own_kv:
        copy.wait()
    await_bytes(s.kvp.at[0, 0, pl.ds(0, 4)], s.mate_kv)
    def to_chips(start):
        def step(i, carry):
            start(lax.rem(chip + i, chips))
            return carry

        lax.fori_loop(1, chips, step, 0)

    def loop_send(src, dst, send_sem, recv_sem, to):
        pltpu.make_async_remote_copy(
            src_ref=src,
            dst_ref=dst,
            send_sem=send_sem,
            recv_sem=recv_sem,
            device_id={"ctx": to},
            device_id_type=MESH,
        ).start()

    for h in range(2):
        for kv in range(2):
            x = lax.select(root_core == 0, s.kvp[kv, h, 4], s.kvp[kv, h, 5])
            s.cand[h, :, kv] = x.reshape(16, 16, W)
        scat[h][chip] = s.cand[h, chip]
        to_chips(
            lambda c, h=h: loop_send(
                s.cand.at[h, c],
                scat[h].at[chip],
                s.pr_send.at[0, h],
                s.pr_recv.at[0, h],
                2 * c + core,
            )
        )
    send_chain(0, K_, 1)
    send_qu(0)

    await_bytes(s.meta.at[0], s.meta_recv)
    await_bytes(s.lens.at[pl.ds(0, groups - 1)], s.lens_recv)
    everything = s.lens[0, 0:1, :]
    for i in range(1, groups):
        everything = everything + s.lens[i, 0:1, :]
    scale = float(groups * 16 * W) / everything.astype(F32)
    scored = [rew[i].astype(F32) for i in range(16)]
    centre = functools.reduce(lambda a, b: a + b, scored) * (1.0 / 16)
    apart = [x - centre for x in scored]
    variance = functools.reduce(lambda a, b: a + b, [x * x for x in apart]) * (1.0 / 16)
    spread = jnp.sqrt(jnp.full((1, W), variance, F32))
    divisor = jnp.maximum(spread, 0.5)
    key_row = lax.broadcasted_iota(jnp.int32, (W, W), 0)
    query_col = lax.broadcasted_iota(jnp.int32, (W, W), 1)
    for o in range(2):
        for b in range(2):
            answer = s.meta[o, b, 7:8, :]
            row = jnp.zeros((1, W), F32)
            for i in range(16):
                row = row + jnp.where(answer == i, apart[i], 0.0)
            row = row / divisor * scale
            s.wt[o, b] = jnp.transpose(jnp.broadcast_to(row, (W, W)))
            of_query = jnp.broadcast_to(s.meta[o, b, 6:7, :].astype(F32), (W, W))
            of_key = jnp.transpose(of_query)
            seen = (key_row <= query_col) & (of_query >= 0.0)
            seen = seen & ((of_key == of_query) | (of_key == 0.0))
            seen = seen | (key_row == query_col)
            s.mb[o, b] = jnp.where(seen, 0.0, -jnp.inf)

    for h in range(2):
        await_bytes(scat[h].at[pl.ds(0, chips - 1)], s.pr_recv.at[0, h])
        prompt_slice = scat[h][root_chip]
        s.sel[h] = prompt_slice
        s.gath[h, chip] = prompt_slice
        to_chips(
            lambda c, h=h: loop_send(
                s.sel.at[h],
                s.gath.at[h, chip],
                s.pr_send.at[1, h],
                s.pr_recv.at[1, h],
                2 * c + core,
            )
        )
        if h == 0:
            send_chain(0, K_, 2)
            send_chain(0, V_, 1)
            send_chain(0, V_, 2)
    for kv in range(2):
        send_chain(1, kv, 1)
        send_chain(1, kv, 2)
    send_qu(1)

    def where_is(t, h):
        return lax.rem(core + t // 2 + h, 2), lax.rem(t, 2)

    def gather_block(t, h, kv, to):
        o, b = where_is(t, h)
        to[t, 0 : 2 * W] = s.gath[h, :, kv].reshape(T, W)
        for i in range(HOPS):
            chosen = s.meta[o, b, 5 - i : 6 - i, :]
            both = s.kvp[kv, h, o + i].astype(F32)
            picked = jnp.where(jnp.broadcast_to(chosen, (W, W)) == 1, both[W:], both[:W])
            to[t, (2 + i) * W : (3 + i) * W] = picked.astype(BF16)
        to[t, 6 * W :] = s.kvp[kv, h, o + 4, pl.ds(pl.multiple_of(b * W, W), W), :]

    def spread_blocks(h):
        def step(t, carry):
            o, b = where_is(t, h)
            s.pacc[...] += s.acc[t, 0 : 2 * W]
            for i in range(HOPS):
                chosen = jnp.broadcast_to(s.meta[o, b, 5 - i : 6 - i, :], (W, W)) == 1
                x = s.acc[t, (2 + i) * W : (3 + i) * W]
                s.gacc[o + i, 0:W] += jnp.where(chosen, 0.0, x)
                s.gacc[o + i, W:] += jnp.where(chosen, x, 0.0)
            s.gacc[o + 4, pl.ds(pl.multiple_of(b * W, W), W), :] += s.acc[t, 6 * W :]
            return carry

        lax.fori_loop(0, 4, step, 0)

    def chunk(j, h):
        t = j // 4
        o, b = where_is(t, h)
        return t, o, b, lax.rem(j, 4)

    def pair(ref, o, h, b, g):
        rows = pl.ds(pl.multiple_of(b * W, W), W)
        return [
            ref.at[o, h, rows, pl.ds(pl.multiple_of((2 * g + i) * W, W), W)] for i in range(2)
        ]

    def joined(ref, o, h, b, g):
        return jnp.concatenate([x[...] for x in pair(ref, o, h, b, g)], axis=0)

    def twice(row):
        return jnp.concatenate([row, row], axis=1)

    META_ROWS = (0, 1, 5, 4, 3, 2)

    def biases(o, b):
        rows = []
        for i in range(6):
            row = s.meta[o, b, META_ROWS[i] : META_ROWS[i] + 1, :]
            unseen = row <= 0 if i < 2 else row < 0
            rows.append(twice(jnp.where(unseen, -jnp.inf, 0.0)))
        return rows

    def score(j, h, ps, pk):
        t, o, b, g = chunk(j, h)
        scores = nt(s.ku[t], joined(s.qb, o, h, b, g))
        seen = scores[6 * W :] + twice(s.mb[o, b])
        peak = jnp.max(seen, axis=0, keepdims=True)
        for i, bias in enumerate(biases(o, b)):
            top = jnp.max(scores[i * W : (i + 1) * W], axis=0, keepdims=True)
            peak = jnp.maximum(peak, top + bias)
        ps[0 : 6 * W] = scores[0 : 6 * W]
        ps[6 * W :] = seen
        pk[0:1] = peak * exp_scale

    def soften(j, h, ps, pk, low, do):
        t, o, b, g = chunk(j, h)
        shift = pk[0:1]
        bias = biases(o, b)
        denominator = jnp.zeros((1, 2 * W), F32)
        for i in range(7):
            here = shift if i == 6 else shift - bias[i]
            e = jnp.exp2(ps[i * W : (i + 1) * W] * exp_scale - here)
            ps[i * W : (i + 1) * W] = e
            denominator = denominator + jnp.sum(e, axis=0, keepdims=True)
        inverse = 1.0 / denominator
        for i in range(7):
            probs = ps[i * W : (i + 1) * W] * inverse
            s.pf[j, i * W : (i + 1) * W] = probs
            low[i * W : (i + 1) * W] = probs.astype(BF16)
        weight = s.wt[o, b]
        up = [x[...].astype(F32) * weight for x in pair(s.ub, o, h, b, g)]
        grad_out = jnp.concatenate(up, axis=0).astype(BF16)
        do[...] = grad_out
        s.do[j] = grad_out

    def attend(j, h, low, do):
        t, o, b, g = chunk(j, h)
        attended = jnp.transpose(nn(s.vt[t], low[...])).astype(BF16)
        s.acc[t] += nn(low[...], do[...])
        for i, x in enumerate(pair(s.ob, o, h, b, g)):
            x[...] = attended[i * W : (i + 1) * W]
        product = do[...].astype(F32) * attended.astype(F32)
        s.dl[j, 0:1] = jnp.sum(jnp.transpose(product), axis=0, keepdims=True)

    def forward(h):
        def prepare(t, carry):
            gather_block(t, h, K_, s.ku)
            gather_block(t, h, V_, s.vu)
            s.kt[t] = jnp.transpose(s.ku[t])
            s.vt[t] = jnp.transpose(s.vu[t])
            return carry

        lax.fori_loop(0, 4, prepare, 0)
        s.acc[...] = jnp.zeros_like(s.acc)
        even, odd = (s.ps0, s.pk0), (s.ps1, s.pk1)
        low_even, low_odd = (s.low0, s.do0), (s.low1, s.do1)
        score(0, h, *even)
        score(1, h, *odd)
        soften(0, h, *even, *low_even)

        def step(i, carry):
            j = 2 * i
            attend(j - 2, h, *low_even)
            score(j, h, *even)
            soften(j - 1, h, *odd, *low_odd)
            attend(j - 1, h, *low_odd)
            score(j + 1, h, *odd)
            soften(j, h, *even, *low_even)
            return carry

        lax.fori_loop(1, 8, step, 0)
        attend(14, h, *low_even)
        soften(15, h, *odd, *low_odd)
        attend(15, h, *low_odd)
        spread_blocks(h)

    def score_grad(j, h, low):
        t, o, b, g = chunk(j, h)
        dprobs = nt(s.vu[t], s.do[j])
        low[...] = (s.pf[j] * (dprobs - s.dl[j, 0:1]) * inv_root).astype(BF16)

    def input_grads(j, h, low):
        t, o, b, g = chunk(j, h)
        grad = jnp.transpose(nn(s.kt[t], low[...])).astype(BF16)
        s.acc[t] += nn(low[...], joined(s.qb, o, h, b, g))
        for i, x in enumerate(pair(s.gb, o, h, b, g)):
            x[...] = grad[i * W : (i + 1) * W]

    def backward(h):
        s.acc[...] = jnp.zeros_like(s.acc)
        score_grad(0, h, s.low0)

        def step(i, carry):
            j = 2 * i
            score_grad(j + 1, h, s.low1)
            input_grads(j, h, s.low0)
            score_grad(j + 2, h, s.low0)
            input_grads(j + 1, h, s.low1)
            return carry

        lax.fori_loop(0, 7, step, 0)
        score_grad(15, h, s.low1)
        input_grads(14, h, s.low0)
        input_grads(15, h, s.low1)
        spread_blocks(h)

    def clear():
        s.gacc[...] = jnp.zeros_like(s.gacc)
        s.pacc[...] = jnp.zeros_like(s.pacc)

    def send_grads(kv, h):
        s.psend[kv, h] = s.pacc[...].reshape(16, 16, W).astype(BF16)
        to_chips(
            lambda c: loop_send(
                s.psend.at[kv, h, c],
                s.prec.at[kv, h, chip],
                s.ps_send.at[kv, h],
                s.ps_recv.at[kv, h],
                2 * c + core,
            )
        )
        s.prec[kv, h, chip] = s.psend[kv, h, chip]
        for i in range(4):
            s.gsend[kv, h, i] = s.gacc[i].astype(BF16)
            hop = 2 if i < 2 else 1
            send(
                s.gsend.at[kv, h, i],
                s.grecv.at[kv, h, hop - 1, core],
                s.g_recv.at[kv, h],
                2 * lax.rem(chip - hop + chips, chips) + i % 2,
            )
        s.msend[kv, h] = s.gacc[4 + other]
        send(s.msend.at[kv, h], s.mrecv.at[kv, h], s.m_recv.at[kv, h], mate)
        s.own[kv, h] = s.gacc[4 + core]

    own_out = []

    def send_rows(staged, out, h, recv_sem):
        send(staged.at[other, h], out.at[:, qcols(core, h)], recv_sem, mate)
        own_out.append(fetch(staged.at[core, h], out.at[:, qcols(core, h)]))

    def sum_prompt(kv, h):
        await_bytes(s.prec.at[kv, h, pl.ds(0, chips - 1)], s.ps_recv.at[kv, h])
        summed = jnp.sum(s.prec[kv, h].astype(F32), axis=0).astype(BF16)
        s.agsend[kv, h] = summed
        s.ag[kv, h, 16 * core + chip] = summed

        def step(i, carry):
            loop_send(
                s.agsend.at[kv, h],
                s.ag.at[kv, h, 16 * core + chip],
                s.ag_send.at[kv, h],
                s.ag_recv.at[kv, h],
                lax.rem(me + i, ring),
            )
            return carry

        lax.fori_loop(1, ring, step, 0)

    def finish(kv, h):
        out = (gk, gv)[kv]
        await_bytes(s.grecv.at[kv, h], s.g_recv.at[kv, h])
        await_bytes(s.mrecv.at[kv, h], s.m_recv.at[kv, h])
        await_bytes(s.ag.at[kv, h, pl.ds(0, ring - 1)], s.ag_recv.at[kv, h])
        for lane, mine in ((core, s.own), (other, s.mrecv)):
            x = mine[kv, h] + s.grecv[kv, h, 0, lane].astype(F32)
            x = x + s.grecv[kv, h, 1, lane].astype(F32)
            prompt = s.ag[kv, h, pl.ds(16 * lane, 16)].astype(F32).reshape(T, W)
            here = jnp.full((T, W), root, jnp.int32) == me
            out[:, kcols(lane, h)] = x + jnp.where(here, prompt, 0.0)

    for h in range(2):
        await_bytes(s.gath.at[h, pl.ds(0, chips - 1)], s.pr_recv.at[1, h])
        for kv in range(2):
            await_bytes(s.kvp.at[kv, h, pl.ds(0, 4)], s.kv_recv.at[kv, h])
            await_bytes((s.qb, s.ub)[kv].at[other, h], s.qu_recv.at[h, kv])
            own_qu[h][kv].wait()
        clear()
        forward(h)
        send_grads(V_, h)
        send_rows(s.ob, attn, h, s.out_recv.at[0, h])
        if h == 1:
            sum_prompt(K_, 0)
        clear()
        backward(h)
        send_grads(K_, h)
        sum_prompt(V_, h)
        send_rows(s.gb, gq, h, s.out_recv.at[1, h])
    finish(V_, 0)
    finish(K_, 0)
    finish(V_, 1)
    sum_prompt(K_, 1)
    finish(K_, 1)

    for copy in own_out:
        copy.wait()
    for h in range(2):
        for i in range(2):
            await_bytes(s.ob.at[other, h], s.out_recv.at[i, h])
    for copy in sends:
        copy.wait_send()
    await_bytes(s.lens.at[pl.ds(0, groups - 1)], s.lens_send)
    for i in range(2):
        for h in range(2):
            await_bytes(s.gath.at[h, pl.ds(0, chips - 1)], s.pr_send.at[i, h])
            await_bytes(s.ag.at[i, h, pl.ds(0, ring - 1)], s.ag_send.at[i, h])
            await_bytes(s.prec.at[i, h, pl.ds(0, chips - 1)], s.ps_send.at[i, h])


def write_out(*refs):
    sems = refs[8]
    copies = [pltpu.make_async_copy(refs[i], refs[4 + i], sems.at[i]) for i in range(4)]
    for copy in copies:
        copy.start()
    for copy in copies:
        copy.wait()


def body(queries, keys, values, upstream, ancestors, segments, responses, rewards, lengths):
    any_spec = pl.BlockSpec(memory_space=pltpu.HBM)
    smem = pl.BlockSpec(memory_space=pltpu.SMEM)
    vmem = pl.BlockSpec(memory_space=pltpu.VMEM)
    results = pl.pallas_call(
        functools.partial(kernel, lax.axis_size("dp"), lax.axis_size("ctx")),
        out_shape=[
            pltpu.VMEM(queries.shape, BF16),
            pltpu.VMEM(queries.shape, BF16),
            pltpu.VMEM(keys.shape, F32),
            pltpu.VMEM(keys.shape, F32),
        ],
        in_specs=[any_spec] * 4 + [smem, vmem, vmem, smem, smem],
        out_specs=[vmem] * 4,
        scratch_shapes=list(SCRATCH.values()),
        compiler_params=pltpu.CompilerParams(
            collective_id=0, has_side_effects=True, vmem_limit_bytes=56 * 1024 * 1024
        ),
    )(
        queries,
        keys,
        values,
        upstream,
        ancestors,
        segments.reshape(2, W),
        responses.reshape(2, W),
        rewards,
        lengths,
    )
    return pl.pallas_call(
        write_out,
        out_shape=[jax.ShapeDtypeStruct(x.shape, x.dtype) for x in results],
        in_specs=[vmem] * 4,
        out_specs=[any_spec] * 4,
        scratch_shapes=[pltpu.SemaphoreType.DMA((4,))],
        compiler_params=pltpu.CompilerParams(vmem_limit_bytes=1024 * 1024),
    )(*[pltpu.with_memory_space_constraint(x, pltpu.VMEM) for x in results])


def solution(mesh):
    rows, flat = P(("dp", "ctx"), None), P(("dp", "ctx"))
    return jax.shard_map(
        body,
        mesh=mesh,
        in_specs=(rows, rows, rows, rows, rows, flat, flat, P("dp"), P("dp")),
        out_specs=(rows, rows, rows, rows),
        check_vma=False,
    )
```

```python
import functools
import math

import jax
import jax.numpy as jnp
from jax import lax
from jax.experimental import pallas as pl
from jax.experimental.pallas import tpu as pltpu
from jax.sharding import PartitionSpec as P

MESH = pl.DeviceIdType.MESH
F32, BF16 = jnp.float32, jnp.bfloat16
W = 128
T = 2 * W
R = 8
C = R * W
N = 7 * W
HOPS = 4
K_, V_ = 0, 1
CUTS = ((0, 4), (4, 7))


def nn(a, b):
    return lax.dot_general(a, b, (((1,), (0,)), ((), ())), preferred_element_type=F32)


def nt(a, b):
    return lax.dot_general(a, b, (((1,), (1,)), ((), ())), preferred_element_type=F32)


def tn(a, b):
    return lax.dot_general(a, b, (((0,), (0,)), ((), ())), preferred_element_type=F32)


SCRATCH = dict(
    kvp=pltpu.VMEM((2, 2, 6, T, W), BF16),
    qb=pltpu.VMEM((2, 2, T, C), BF16),
    ub=pltpu.VMEM((2, 2, T, C), BF16),
    ob=pltpu.VMEM((2, 2, T, C), BF16),
    gb=pltpu.VMEM((2, 2, T, C), BF16),
    cand=pltpu.VMEM((2, 16, 2, 16, W), BF16),
    scat0=pltpu.VMEM((16, 2, 16, W), BF16),
    scat1=pltpu.VMEM((16, 2, 16, W), BF16),
    sel=pltpu.VMEM((2, 2, 16, W), BF16),
    gath=pltpu.VMEM((2, 16, 2, 16, W), BF16),
    meta=pltpu.VMEM((2, 2, 8, W), jnp.int32),
    lens=pltpu.VMEM((4, 8, W), jnp.int32),
    wt=pltpu.VMEM((2, 2, W, W), F32),
    mb=pltpu.VMEM((2, 2, W, W), F32),
    ku=pltpu.VMEM((4, N, W), BF16),
    vu=pltpu.VMEM((4, N, W), BF16),
    kt=pltpu.VMEM((4, W, N), BF16),
    vt=pltpu.VMEM((4, W, N), BF16),
    pf=pltpu.VMEM((16, N, 2 * W), F32),
    dl=pltpu.VMEM((16, 8, 2 * W), F32),
    do=pltpu.VMEM((16, 2 * W, W), BF16),
    ps0=pltpu.VMEM((N, 2 * W), F32),
    ps1=pltpu.VMEM((N, 2 * W), F32),
    pk0=pltpu.VMEM((8, 2 * W), F32),
    pk1=pltpu.VMEM((8, 2 * W), F32),
    low0=pltpu.VMEM((N, 2 * W), BF16),
    low1=pltpu.VMEM((N, 2 * W), BF16),
    do0=pltpu.VMEM((2 * W, W), BF16),
    do1=pltpu.VMEM((2 * W, W), BF16),
    acc=pltpu.VMEM((4, N, W), F32),
    gacc=pltpu.VMEM((6, T, W), F32),
    pacc=pltpu.VMEM((T, W), F32),
    own=pltpu.VMEM((2, 2, T, W), F32),
    msend=pltpu.VMEM((2, 2, T, W), F32),
    mrecv=pltpu.VMEM((2, 2, T, W), F32),
    gsend=pltpu.VMEM((2, 2, 4, T, W), BF16),
    grecv=pltpu.VMEM((2, 2, 2, 2, T, W), BF16),
    psend=pltpu.VMEM((2, 2, 16, 16, W), BF16),
    prec=pltpu.VMEM((2, 2, 16, 16, W), BF16),
    agsend=pltpu.VMEM((2, 2, 16, W), BF16),
    ag=pltpu.VMEM((2, 2, 32, 16, W), BF16),
    one_send=pltpu.SemaphoreType.DMA((64,)),
    local=pltpu.SemaphoreType.DMA((12,)),
    kv_recv=pltpu.SemaphoreType.DMA((2, 2)),
    kv_relay=pltpu.SemaphoreType.DMA((2, 2)),
    mate_kv=pltpu.SemaphoreType.DMA,
    meta_recv=pltpu.SemaphoreType.DMA,
    lens_send=pltpu.SemaphoreType.DMA,
    lens_recv=pltpu.SemaphoreType.DMA,
    qu_recv=pltpu.SemaphoreType.DMA((2, 2)),
    out_recv=pltpu.SemaphoreType.DMA((2, 2)),
    pr_send=pltpu.SemaphoreType.DMA((2, 2)),
    pr_recv=pltpu.SemaphoreType.DMA((2, 2)),
    g_recv=pltpu.SemaphoreType.DMA((2, 2)),
    m_recv=pltpu.SemaphoreType.DMA((2, 2)),
    ps_send=pltpu.SemaphoreType.DMA((2, 2)),
    ps_recv=pltpu.SemaphoreType.DMA((2, 2)),
    ag_send=pltpu.SemaphoreType.DMA((2, 2)),
    ag_recv=pltpu.SemaphoreType.DMA((2, 2)),
)


class Names:
    def __init__(self, names, refs):
        for name, ref in zip(names, refs):
            setattr(self, name, ref)


def kernel(groups, ring, q, k, v, u, anc, seg, resp, rew, leng, attn, gq, gk, gv, *refs):
    s = Names(list(SCRATCH), refs)
    me, z = lax.axis_index("ctx"), lax.axis_index("dp")
    chips = ring // 2
    chip, core = me // 2, lax.rem(me, 2)
    other = 1 - core
    mate = 2 * chip + other
    inv_root = 1.0 / math.sqrt(W)
    exp_scale = math.log2(math.e) * inv_root

    first = anc[0, 0]
    root = jnp.where(first < 0, me, lax.div(first, 2))
    root_chip, root_core = lax.div(root, 2), lax.rem(root, 2)

    sends = []
    scat = (s.scat0, s.scat1)

    def send(src, dst, recv_sem, to):
        copy = pltpu.make_async_remote_copy(
            src_ref=src,
            dst_ref=dst,
            send_sem=s.one_send.at[len(sends)],
            recv_sem=recv_sem,
            device_id={"ctx": to},
            device_id_type=MESH,
        )
        copy.start()
        sends.append(copy)

    def await_bytes(ref, sem):
        pltpu.make_async_copy(ref, ref, sem).wait()

    barrier = pltpu.get_barrier_semaphore()

    def greet(i, carry):
        pl.semaphore_signal(
            barrier, inc=1, device_id={"ctx": lax.rem(me + i, ring)}, device_id_type=MESH
        )
        return carry

    lax.fori_loop(1, ring, greet, 0)
    for i in range(1, groups):
        pl.semaphore_signal(
            barrier, inc=1, device_id={"dp": lax.rem(z + i, groups)}, device_id_type=MESH
        )

    def kcols(lane, h):
        return pl.ds(pl.multiple_of((2 * lane + h) * W, W), W)

    def qcols(lane, h):
        return pl.ds(pl.multiple_of((2 * lane + h) * C, C), C)

    local = []

    def fetch(src, dst):
        copy = pltpu.make_async_copy(src, dst, s.local.at[len(local)])
        copy.start()
        local.append(copy)
        return copy

    own_kv = [
        fetch(src.at[:, kcols(core, h)], s.kvp.at[kv, h, 4 + core])
        for h in range(2)
        for kv, src in ((K_, k), (V_, v))
    ]
    own_qu = [
        (
            fetch(q.at[:, qcols(core, h)], s.qb.at[core, h]),
            fetch(u.at[:, qcols(core, h)], s.ub.at[core, h]),
        )
        for h in range(2)
    ]

    total = leng[0]
    for i in range(1, 16):
        total = total + leng[i]
    s.lens[z] = jnp.full((8, W), total, jnp.int32)
    for b in range(2):
        rows = [jnp.where(anc[b, 0] >= 0, 1, 0), jnp.where(anc[b, 1] >= 0, 1, 0)]
        for hop in range(1, HOPS + 1):
            chosen = jnp.int32(-1)
            for slot in range(2, 6):
                a = anc[b, slot]
                away = lax.rem(me - lax.div(jnp.maximum(a, 0), 2) + ring, ring)
                chosen = jnp.where((a >= 0) & (away == hop), lax.rem(a, 2), chosen)
            rows.append(chosen)
        for i, row in enumerate(rows):
            s.meta[core, b, i : i + 1, :] = jnp.full((1, W), row, jnp.int32)
        s.meta[core, b, 6:7, :] = seg[b : b + 1, :]
        s.meta[core, b, 7:8, :] = resp[b : b + 1, :]

    pl.semaphore_wait(barrier, ring - 1 + groups - 1)

    for h in range(2):
        for kv, src in ((K_, k), (V_, v)):
            send(src.at[:, kcols(other, h)], s.kvp.at[kv, h, 4 + core], s.mate_kv, mate)
    for i in range(1, groups):
        pltpu.make_async_remote_copy(
            src_ref=s.lens.at[z],
            dst_ref=s.lens.at[z],
            send_sem=s.lens_send,
            recv_sem=s.lens_recv,
            device_id={"dp": lax.rem(z + i, groups)},
            device_id_type=MESH,
        ).start()
    send(s.meta.at[core], s.meta.at[core], s.meta_recv, mate)

    def send_chain(h, kv):
        for lane in range(2):
            send(
                (k, v)[kv].at[:, kcols(lane, h)],
                s.kvp.at[kv, h, 2 + core],
                s.kv_recv.at[kv, h],
                2 * lax.rem(chip + 1, chips) + lane,
            )

    def relay_chain(h, kv):
        await_bytes(s.kvp.at[kv, h, pl.ds(2, 2)], s.kv_recv.at[kv, h])
        send(
            s.kvp.at[kv, h, pl.ds(2, 2)],
            s.kvp.at[kv, h, pl.ds(0, 2)],
            s.kv_relay.at[kv, h],
            2 * lax.rem(chip + 1, chips) + core,
        )

    def send_qu(h):
        send(q.at[:, qcols(other, h)], s.qb.at[core, h], s.qu_recv.at[h, 0], mate)
        send(u.at[:, qcols(other, h)], s.ub.at[core, h], s.qu_recv.at[h, 1], mate)

    send_chain(0, K_)

    for copy in own_kv:
        copy.wait()
    await_bytes(s.kvp.at[0, 0, pl.ds(0, 4)], s.mate_kv)
    def to_chips(start):
        def step(i, carry):
            start(lax.rem(chip + i, chips))
            return carry

        lax.fori_loop(1, chips, step, 0)

    def loop_send(src, dst, send_sem, recv_sem, to):
        pltpu.make_async_remote_copy(
            src_ref=src,
            dst_ref=dst,
            send_sem=send_sem,
            recv_sem=recv_sem,
            device_id={"ctx": to},
            device_id_type=MESH,
        ).start()

    for h in range(2):
        for kv in range(2):
            x = lax.select(root_core == 0, s.kvp[kv, h, 4], s.kvp[kv, h, 5])
            s.cand[h, :, kv] = x.reshape(16, 16, W)
        scat[h][chip] = s.cand[h, chip]
        to_chips(
            lambda c, h=h: loop_send(
                s.cand.at[h, c],
                scat[h].at[chip],
                s.pr_send.at[0, h],
                s.pr_recv.at[0, h],
                2 * c + core,
            )
        )
        if h == 0:
            send_chain(0, V_)
    send_qu(0)

    await_bytes(s.meta.at[0], s.meta_recv)
    await_bytes(s.lens.at[pl.ds(0, groups - 1)], s.lens_recv)
    everything = s.lens[0, 0:1, :]
    for i in range(1, groups):
        everything = everything + s.lens[i, 0:1, :]
    scale = float(groups * 16 * W) / everything.astype(F32)
    scored = [rew[i].astype(F32) for i in range(16)]
    centre = functools.reduce(lambda a, b: a + b, scored) * (1.0 / 16)
    apart = [x - centre for x in scored]
    variance = functools.reduce(lambda a, b: a + b, [x * x for x in apart]) * (1.0 / 16)
    spread = jnp.sqrt(jnp.full((1, W), variance, F32))
    divisor = jnp.maximum(spread, 0.5)
    key_row = lax.broadcasted_iota(jnp.int32, (W, W), 0)
    query_col = lax.broadcasted_iota(jnp.int32, (W, W), 1)
    for o in range(2):
        for b in range(2):
            answer = s.meta[o, b, 7:8, :]
            row = jnp.zeros((1, W), F32)
            for i in range(16):
                row = row + jnp.where(answer == i, apart[i], 0.0)
            row = row / divisor * scale
            s.wt[o, b] = jnp.transpose(jnp.broadcast_to(row, (W, W)))
            of_query = jnp.broadcast_to(s.meta[o, b, 6:7, :].astype(F32), (W, W))
            of_key = jnp.transpose(of_query)
            seen = (key_row <= query_col) & (of_query >= 0.0)
            seen = seen & ((of_key == of_query) | (of_key == 0.0))
            seen = seen | (key_row == query_col)
            s.mb[o, b] = jnp.where(seen, 0.0, -jnp.inf)

    for h in range(2):
        await_bytes(scat[h].at[pl.ds(0, chips - 1)], s.pr_recv.at[0, h])
        prompt_slice = scat[h][root_chip]
        s.sel[h] = prompt_slice
        s.gath[h, chip] = prompt_slice
        to_chips(
            lambda c, h=h: loop_send(
                s.sel.at[h],
                s.gath.at[h, chip],
                s.pr_send.at[1, h],
                s.pr_recv.at[1, h],
                2 * c + core,
            )
        )
        if h == 0:
            relay_chain(0, K_)
            relay_chain(0, V_)
    for kv in range(2):
        send_chain(1, kv)
    send_qu(1)

    def where_is(t, h):
        return lax.rem(core + t // 2 + h, 2), lax.rem(t, 2)

    def gather_block(t, h, kv, to):
        o, b = where_is(t, h)
        to[t, 0 : 2 * W] = s.gath[h, :, kv].reshape(T, W)
        for i in range(HOPS):
            chosen = s.meta[o, b, 5 - i : 6 - i, :]
            both = s.kvp[kv, h, o + i].astype(F32)
            picked = jnp.where(jnp.broadcast_to(chosen, (W, W)) == 1, both[W:], both[:W])
            to[t, (2 + i) * W : (3 + i) * W] = picked.astype(BF16)
        to[t, 6 * W :] = s.kvp[kv, h, o + 4, pl.ds(pl.multiple_of(b * W, W), W), :]

    def spread_blocks(h):
        def step(t, carry):
            o, b = where_is(t, h)
            s.pacc[...] += s.acc[t, 0 : 2 * W]
            for i in range(HOPS):
                chosen = jnp.broadcast_to(s.meta[o, b, 5 - i : 6 - i, :], (W, W)) == 1
                x = s.acc[t, (2 + i) * W : (3 + i) * W]
                s.gacc[o + i, 0:W] += jnp.where(chosen, 0.0, x)
                s.gacc[o + i, W:] += jnp.where(chosen, x, 0.0)
            s.gacc[o + 4, pl.ds(pl.multiple_of(b * W, W), W), :] += s.acc[t, 6 * W :]
            return carry

        lax.fori_loop(0, 4, step, 0)

    def chunk(j, h):
        t = j // 4
        o, b = where_is(t, h)
        return t, o, b, lax.rem(j, 4)

    def pair(ref, o, h, b, g):
        rows = pl.ds(pl.multiple_of(b * W, W), W)
        return [
            ref.at[o, h, rows, pl.ds(pl.multiple_of((2 * g + i) * W, W), W)] for i in range(2)
        ]

    def joined(ref, o, h, b, g):
        return jnp.concatenate([x[...] for x in pair(ref, o, h, b, g)], axis=0)

    def twice(row):
        return jnp.concatenate([row, row], axis=1)

    META_ROWS = (0, 1, 5, 4, 3, 2)

    def biases(o, b):
        rows = []
        for i in range(6):
            row = s.meta[o, b, META_ROWS[i] : META_ROWS[i] + 1, :]
            unseen = row <= 0 if i < 2 else row < 0
            rows.append(twice(jnp.where(unseen, -jnp.inf, 0.0)))
        return rows

    def score(j, h, ps, pk):
        t, o, b, g = chunk(j, h)
        queries = joined(s.qb, o, h, b, g)
        bias = biases(o, b)
        peak = None
        for lo, hi in CUTS:
            scores = nt(s.ku[t, lo * W : hi * W], queries)
            for i in range(lo, hi):
                part = scores[(i - lo) * W : (i + 1 - lo) * W]
                if i == 6:
                    part = part + twice(s.mb[o, b])
                ps[i * W : (i + 1) * W] = part
                top = jnp.max(part, axis=0, keepdims=True)
                if i < 6:
                    top = top + bias[i]
                peak = top if peak is None else jnp.maximum(peak, top)
        pk[0:1] = peak * exp_scale

    def soften(j, h, ps, pk, low, do):
        t, o, b, g = chunk(j, h)
        shift = pk[0:1]
        bias = biases(o, b)
        denominator = jnp.zeros((1, 2 * W), F32)
        for i in range(7):
            here = shift if i == 6 else shift - bias[i]
            e = jnp.exp2(ps[i * W : (i + 1) * W] * exp_scale - here)
            ps[i * W : (i + 1) * W] = e
            denominator = denominator + jnp.sum(e, axis=0, keepdims=True)
        inverse = 1.0 / denominator
        for i in range(7):
            probs = ps[i * W : (i + 1) * W] * inverse
            s.pf[j, i * W : (i + 1) * W] = probs
            low[i * W : (i + 1) * W] = probs.astype(BF16)
        weight = s.wt[o, b]
        up = [x[...].astype(F32) * weight for x in pair(s.ub, o, h, b, g)]
        grad_out = jnp.concatenate(up, axis=0).astype(BF16)
        do[...] = grad_out
        s.do[j] = grad_out

    def attend(j, h, low, do):
        t, o, b, g = chunk(j, h)
        attended = [nn(s.vt[t, :, lo * W : hi * W], low[lo * W : hi * W]) for lo, hi in CUTS]
        attended = jnp.transpose(attended[0] + attended[1]).astype(BF16)
        for lo, hi in CUTS:
            s.acc[t, lo * W : hi * W] += nn(low[lo * W : hi * W], do[...])
        for i, x in enumerate(pair(s.ob, o, h, b, g)):
            x[...] = attended[i * W : (i + 1) * W]
        product = do[...].astype(F32) * attended.astype(F32)
        s.dl[j, 0:1] = jnp.sum(jnp.transpose(product), axis=0, keepdims=True)

    def forward(h):
        def prepare(kv, whole, turned):
            await_bytes(s.kvp.at[kv, h, pl.ds(0, 2)], s.kv_relay.at[kv, h])

            def step(t, carry):
                gather_block(t, h, kv, whole)
                turned[t] = jnp.transpose(whole[t])
                return carry

            lax.fori_loop(0, 4, step, 0)

        even, odd = (s.ps0, s.pk0), (s.ps1, s.pk1)
        low_even, low_odd = (s.low0, s.do0), (s.low1, s.do1)
        prepare(K_, s.ku, s.kt)
        score(0, h, *even)
        score(1, h, *odd)
        soften(0, h, *even, *low_even)
        s.acc[...] = jnp.zeros_like(s.acc)
        prepare(V_, s.vu, s.vt)

        def step(i, carry):
            j = 2 * i
            attend(j - 2, h, *low_even)
            score(j, h, *even)
            soften(j - 1, h, *odd, *low_odd)
            attend(j - 1, h, *low_odd)
            score(j + 1, h, *odd)
            soften(j, h, *even, *low_even)
            return carry

        lax.fori_loop(1, 8, step, 0)
        attend(14, h, *low_even)
        soften(15, h, *odd, *low_odd)
        attend(15, h, *low_odd)
        spread_blocks(h)

    def score_grad(j, h, low):
        t, o, b, g = chunk(j, h)
        delta = s.dl[j, 0:1]
        for lo, hi in CUTS:
            rows = pl.ds(lo * W, (hi - lo) * W)
            dprobs = nt(s.vu[t, rows], s.do[j])
            low[rows] = (s.pf[j, rows] * (dprobs - delta) * inv_root).astype(BF16)

    def input_grads(j, h, low):
        t, o, b, g = chunk(j, h)
        grad = [nn(s.kt[t, :, lo * W : hi * W], low[lo * W : hi * W]) for lo, hi in CUTS]
        grad = jnp.transpose(grad[0] + grad[1]).astype(BF16)
        queries = joined(s.qb, o, h, b, g)
        for lo, hi in CUTS:
            s.acc[t, lo * W : hi * W] += nn(low[lo * W : hi * W], queries)
        for i, x in enumerate(pair(s.gb, o, h, b, g)):
            x[...] = grad[i * W : (i + 1) * W]

    def backward(h):
        s.acc[...] = jnp.zeros_like(s.acc)
        score_grad(0, h, s.low0)

        def step(i, carry):
            j = 2 * i
            score_grad(j + 1, h, s.low1)
            input_grads(j, h, s.low0)
            score_grad(j + 2, h, s.low0)
            input_grads(j + 1, h, s.low1)
            return carry

        lax.fori_loop(0, 7, step, 0)
        score_grad(15, h, s.low1)
        input_grads(14, h, s.low0)
        input_grads(15, h, s.low1)
        spread_blocks(h)

    def clear():
        s.gacc[...] = jnp.zeros_like(s.gacc)
        s.pacc[...] = jnp.zeros_like(s.pacc)

    def send_grads(kv, h):
        s.psend[kv, h] = s.pacc[...].reshape(16, 16, W).astype(BF16)
        to_chips(
            lambda c: loop_send(
                s.psend.at[kv, h, c],
                s.prec.at[kv, h, chip],
                s.ps_send.at[kv, h],
                s.ps_recv.at[kv, h],
                2 * c + core,
            )
        )
        s.prec[kv, h, chip] = s.psend[kv, h, chip]
        for i in range(4):
            s.gsend[kv, h, i] = s.gacc[i].astype(BF16)
            hop = 2 if i < 2 else 1
            send(
                s.gsend.at[kv, h, i],
                s.grecv.at[kv, h, hop - 1, core],
                s.g_recv.at[kv, h],
                2 * lax.rem(chip - hop + chips, chips) + i % 2,
            )
        s.msend[kv, h] = s.gacc[4 + other]
        send(s.msend.at[kv, h], s.mrecv.at[kv, h], s.m_recv.at[kv, h], mate)
        s.own[kv, h] = s.gacc[4 + core]

    own_out = []

    def send_rows(staged, out, h, recv_sem):
        send(staged.at[other, h], out.at[:, qcols(core, h)], recv_sem, mate)
        own_out.append(fetch(staged.at[core, h], out.at[:, qcols(core, h)]))

    def sum_prompt(kv, h):
        await_bytes(s.prec.at[kv, h, pl.ds(0, chips - 1)], s.ps_recv.at[kv, h])
        summed = jnp.sum(s.prec[kv, h].astype(F32), axis=0).astype(BF16)
        s.agsend[kv, h] = summed
        s.ag[kv, h, 16 * core + chip] = summed

        def step(i, carry):
            loop_send(
                s.agsend.at[kv, h],
                s.ag.at[kv, h, 16 * core + chip],
                s.ag_send.at[kv, h],
                s.ag_recv.at[kv, h],
                lax.rem(me + i, ring),
            )
            return carry

        lax.fori_loop(1, ring, step, 0)

    def finish(kv, h):
        out = (gk, gv)[kv]
        await_bytes(s.grecv.at[kv, h], s.g_recv.at[kv, h])
        await_bytes(s.mrecv.at[kv, h], s.m_recv.at[kv, h])
        await_bytes(s.ag.at[kv, h, pl.ds(0, ring - 1)], s.ag_recv.at[kv, h])
        for lane, mine in ((core, s.own), (other, s.mrecv)):
            x = mine[kv, h] + s.grecv[kv, h, 0, lane].astype(F32)
            x = x + s.grecv[kv, h, 1, lane].astype(F32)
            prompt = s.ag[kv, h, pl.ds(16 * lane, 16)].astype(F32).reshape(T, W)
            here = jnp.full((T, W), root, jnp.int32) == me
            out[:, kcols(lane, h)] = x + jnp.where(here, prompt, 0.0)

    for h in range(2):
        await_bytes(s.gath.at[h, pl.ds(0, chips - 1)], s.pr_recv.at[1, h])
        for i in range(2):
            await_bytes((s.qb, s.ub)[i].at[other, h], s.qu_recv.at[h, i])
            own_qu[h][i].wait()
        clear()
        forward(h)
        send_grads(V_, h)
        send_rows(s.ob, attn, h, s.out_recv.at[0, h])
        if h == 0:
            relay_chain(1, K_)
            relay_chain(1, V_)
        if h == 1:
            sum_prompt(K_, 0)
        clear()
        backward(h)
        send_grads(K_, h)
        sum_prompt(V_, h)
        send_rows(s.gb, gq, h, s.out_recv.at[1, h])
    finish(V_, 0)
    finish(K_, 0)
    finish(V_, 1)
    sum_prompt(K_, 1)
    finish(K_, 1)

    for copy in own_out:
        copy.wait()
    for h in range(2):
        for i in range(2):
            await_bytes(s.ob.at[other, h], s.out_recv.at[i, h])
    for copy in sends:
        copy.wait_send()
    await_bytes(s.lens.at[pl.ds(0, groups - 1)], s.lens_send)
    for i in range(2):
        for h in range(2):
            await_bytes(s.gath.at[h, pl.ds(0, chips - 1)], s.pr_send.at[i, h])
            await_bytes(s.ag.at[i, h, pl.ds(0, ring - 1)], s.ag_send.at[i, h])
            await_bytes(s.prec.at[i, h, pl.ds(0, chips - 1)], s.ps_send.at[i, h])


def write_out(*refs):
    sems = refs[8]
    copies = [pltpu.make_async_copy(refs[i], refs[4 + i], sems.at[i]) for i in range(4)]
    for copy in copies:
        copy.start()
    for copy in copies:
        copy.wait()


def body(queries, keys, values, upstream, ancestors, segments, responses, rewards, lengths):
    any_spec = pl.BlockSpec(memory_space=pltpu.HBM)
    smem = pl.BlockSpec(memory_space=pltpu.SMEM)
    vmem = pl.BlockSpec(memory_space=pltpu.VMEM)
    results = pl.pallas_call(
        functools.partial(kernel, lax.axis_size("dp"), lax.axis_size("ctx")),
        out_shape=[
            pltpu.VMEM(queries.shape, BF16),
            pltpu.VMEM(queries.shape, BF16),
            pltpu.VMEM(keys.shape, F32),
            pltpu.VMEM(keys.shape, F32),
        ],
        in_specs=[any_spec] * 4 + [smem, vmem, vmem, smem, smem],
        out_specs=[vmem] * 4,
        scratch_shapes=list(SCRATCH.values()),
        compiler_params=pltpu.CompilerParams(
            collective_id=0, has_side_effects=True, vmem_limit_bytes=56 * 1024 * 1024
        ),
    )(
        queries,
        keys,
        values,
        upstream,
        ancestors,
        segments.reshape(2, W),
        responses.reshape(2, W),
        rewards,
        lengths,
    )
    return pl.pallas_call(
        write_out,
        out_shape=[jax.ShapeDtypeStruct(x.shape, x.dtype) for x in results],
        in_specs=[vmem] * 4,
        out_specs=[any_spec] * 4,
        scratch_shapes=[pltpu.SemaphoreType.DMA((4,))],
        compiler_params=pltpu.CompilerParams(vmem_limit_bytes=1024 * 1024),
    )(*[pltpu.with_memory_space_constraint(x, pltpu.VMEM) for x in results])


def solution(mesh):
    rows, flat = P(("dp", "ctx"), None), P(("dp", "ctx"))
    return jax.shard_map(
        body,
        mesh=mesh,
        in_specs=(rows, rows, rows, rows, rows, flat, flat, P("dp"), P("dp")),
        out_specs=(rows, rows, rows, rows),
        check_vma=False,
    )
```

```python
import functools
import math

import jax
import jax.numpy as jnp
from jax import lax
from jax.experimental import pallas as pl
from jax.experimental.pallas import tpu as pltpu
from jax.sharding import PartitionSpec as P

MESH = pl.DeviceIdType.MESH
F32, BF16 = jnp.float32, jnp.bfloat16
W = 128
T = 2 * W
R = 8
C = R * W
N = 7 * W
H = 4
M = H * W
HOPS = 4
K_, V_ = 0, 1
CUTS = ((0, 4), (4, 7))


def nn(a, b):
    return lax.dot_general(a, b, (((1,), (0,)), ((), ())), preferred_element_type=F32)


def nt(a, b):
    return lax.dot_general(a, b, (((1,), (1,)), ((), ())), preferred_element_type=F32)


SCRATCH = dict(
    kvp=pltpu.VMEM((2, 2, 6, T, W), BF16),
    qb=pltpu.VMEM((2, 2, T, C), BF16),
    ub=pltpu.VMEM((2, 2, T, C), BF16),
    ob=pltpu.VMEM((2, 2, T, C), BF16),
    gb=pltpu.VMEM((2, 2, T, C), BF16),
    cand=pltpu.VMEM((2, 16, 2, 16, W), BF16),
    scat0=pltpu.VMEM((16, 2, 16, W), BF16),
    scat1=pltpu.VMEM((16, 2, 16, W), BF16),
    sel=pltpu.VMEM((2, 2, 16, W), BF16),
    gath=pltpu.VMEM((2, 16, 2, 16, W), BF16),
    meta=pltpu.VMEM((2, 2, 8, W), jnp.int32),
    lens=pltpu.VMEM((4, 8, W), jnp.int32),
    wt=pltpu.VMEM((2, 2, W, W), F32),
    mb=pltpu.VMEM((2, 2, W, W), F32),
    ku=pltpu.VMEM((4, N, W), BF16),
    vu=pltpu.VMEM((4, N, W), BF16),
    kt=pltpu.VMEM((4, W, N), BF16),
    vt=pltpu.VMEM((4, W, N), BF16),
    qt=pltpu.VMEM((8, W, M), BF16),
    dt=pltpu.VMEM((8, W, M), BF16),
    pf=pltpu.VMEM((8, N, M), F32),
    dl=pltpu.VMEM((8, 8, M), F32),
    ps0=pltpu.VMEM((N, M), F32),
    ps1=pltpu.VMEM((N, M), F32),
    pk0=pltpu.VMEM((8, M), F32),
    pk1=pltpu.VMEM((8, M), F32),
    low0=pltpu.VMEM((N, M), BF16),
    low1=pltpu.VMEM((N, M), BF16),
    do0=pltpu.VMEM((W, M), BF16),
    do1=pltpu.VMEM((W, M), BF16),
    acc=pltpu.VMEM((4, W, N), F32),
    gacc=pltpu.VMEM((6, T, W), F32),
    pacc=pltpu.VMEM((T, W), F32),
    own=pltpu.VMEM((2, 2, T, W), F32),
    msend=pltpu.VMEM((2, 2, T, W), F32),
    mrecv=pltpu.VMEM((2, 2, T, W), F32),
    gsend=pltpu.VMEM((2, 2, 4, T, W), BF16),
    grecv=pltpu.VMEM((2, 2, 2, 2, T, W), BF16),
    psend=pltpu.VMEM((2, 2, 16, 16, W), BF16),
    prec=pltpu.VMEM((2, 2, 16, 16, W), BF16),
    agsend=pltpu.VMEM((2, 2, 16, W), BF16),
    ag=pltpu.VMEM((2, 2, 32, 16, W), BF16),
    one_send=pltpu.SemaphoreType.DMA((64,)),
    local=pltpu.SemaphoreType.DMA((12,)),
    kv_recv=pltpu.SemaphoreType.DMA((2, 2)),
    kv_relay=pltpu.SemaphoreType.DMA((2, 2)),
    mate_kv=pltpu.SemaphoreType.DMA,
    meta_recv=pltpu.SemaphoreType.DMA,
    lens_send=pltpu.SemaphoreType.DMA,
    lens_recv=pltpu.SemaphoreType.DMA,
    qu_recv=pltpu.SemaphoreType.DMA((2, 2)),
    out_recv=pltpu.SemaphoreType.DMA((2, 2)),
    pr_send=pltpu.SemaphoreType.DMA((2, 2)),
    pr_recv=pltpu.SemaphoreType.DMA((2, 2)),
    g_recv=pltpu.SemaphoreType.DMA((2, 2)),
    m_recv=pltpu.SemaphoreType.DMA((2, 2)),
    ps_send=pltpu.SemaphoreType.DMA((2, 2)),
    ps_recv=pltpu.SemaphoreType.DMA((2, 2)),
    ag_send=pltpu.SemaphoreType.DMA((2, 2)),
    ag_recv=pltpu.SemaphoreType.DMA((2, 2)),
)


class Names:
    def __init__(self, names, refs):
        for name, ref in zip(names, refs):
            setattr(self, name, ref)


def kernel(groups, ring, q, k, v, u, anc, seg, resp, rew, leng, attn, gq, gk, gv, *refs):
    s = Names(list(SCRATCH), refs)
    me, z = lax.axis_index("ctx"), lax.axis_index("dp")
    chips = ring // 2
    chip, core = me // 2, lax.rem(me, 2)
    other = 1 - core
    mate = 2 * chip + other
    inv_root = 1.0 / math.sqrt(W)
    exp_scale = math.log2(math.e) * inv_root

    first = anc[0, 0]
    root = jnp.where(first < 0, me, lax.div(first, 2))
    root_chip, root_core = lax.div(root, 2), lax.rem(root, 2)

    sends = []
    scat = (s.scat0, s.scat1)

    def send(src, dst, recv_sem, to):
        copy = pltpu.make_async_remote_copy(
            src_ref=src,
            dst_ref=dst,
            send_sem=s.one_send.at[len(sends)],
            recv_sem=recv_sem,
            device_id={"ctx": to},
            device_id_type=MESH,
        )
        copy.start()
        sends.append(copy)

    def await_bytes(ref, sem):
        pltpu.make_async_copy(ref, ref, sem).wait()

    barrier = pltpu.get_barrier_semaphore()

    def greet(i, carry):
        pl.semaphore_signal(
            barrier, inc=1, device_id={"ctx": lax.rem(me + i, ring)}, device_id_type=MESH
        )
        return carry

    lax.fori_loop(1, ring, greet, 0)
    for i in range(1, groups):
        pl.semaphore_signal(
            barrier, inc=1, device_id={"dp": lax.rem(z + i, groups)}, device_id_type=MESH
        )

    def kcols(lane, h):
        return pl.ds(pl.multiple_of((2 * lane + h) * W, W), W)

    def qcols(lane, h):
        return pl.ds(pl.multiple_of((2 * lane + h) * C, C), C)

    local = []

    def fetch(src, dst):
        copy = pltpu.make_async_copy(src, dst, s.local.at[len(local)])
        copy.start()
        local.append(copy)
        return copy

    own_kv = [
        fetch(src.at[:, kcols(core, h)], s.kvp.at[kv, h, 4 + core])
        for h in range(2)
        for kv, src in ((K_, k), (V_, v))
    ]
    own_qu = [
        (
            fetch(q.at[:, qcols(core, h)], s.qb.at[core, h]),
            fetch(u.at[:, qcols(core, h)], s.ub.at[core, h]),
        )
        for h in range(2)
    ]

    total = leng[0]
    for i in range(1, 16):
        total = total + leng[i]
    s.lens[z] = jnp.full((8, W), total, jnp.int32)
    for b in range(2):
        rows = [jnp.where(anc[b, 0] >= 0, 1, 0), jnp.where(anc[b, 1] >= 0, 1, 0)]
        for hop in range(1, HOPS + 1):
            chosen = jnp.int32(-1)
            for slot in range(2, 6):
                a = anc[b, slot]
                away = lax.rem(me - lax.div(jnp.maximum(a, 0), 2) + ring, ring)
                chosen = jnp.where((a >= 0) & (away == hop), lax.rem(a, 2), chosen)
            rows.append(chosen)
        for i, row in enumerate(rows):
            s.meta[core, b, i : i + 1, :] = jnp.full((1, W), row, jnp.int32)
        s.meta[core, b, 6:7, :] = seg[b : b + 1, :]
        s.meta[core, b, 7:8, :] = resp[b : b + 1, :]

    pl.semaphore_wait(barrier, ring - 1 + groups - 1)

    for h in range(2):
        for kv, src in ((K_, k), (V_, v)):
            send(src.at[:, kcols(other, h)], s.kvp.at[kv, h, 4 + core], s.mate_kv, mate)
    for i in range(1, groups):
        pltpu.make_async_remote_copy(
            src_ref=s.lens.at[z],
            dst_ref=s.lens.at[z],
            send_sem=s.lens_send,
            recv_sem=s.lens_recv,
            device_id={"dp": lax.rem(z + i, groups)},
            device_id_type=MESH,
        ).start()
    send(s.meta.at[core], s.meta.at[core], s.meta_recv, mate)

    def send_chain(h, kv):
        for lane in range(2):
            send(
                (k, v)[kv].at[:, kcols(lane, h)],
                s.kvp.at[kv, h, 2 + core],
                s.kv_recv.at[kv, h],
                2 * lax.rem(chip + 1, chips) + lane,
            )

    def relay_chain(h, kv):
        await_bytes(s.kvp.at[kv, h, pl.ds(2, 2)], s.kv_recv.at[kv, h])
        send(
            s.kvp.at[kv, h, pl.ds(2, 2)],
            s.kvp.at[kv, h, pl.ds(0, 2)],
            s.kv_relay.at[kv, h],
            2 * lax.rem(chip + 1, chips) + core,
        )

    def send_qu(h):
        send(q.at[:, qcols(other, h)], s.qb.at[core, h], s.qu_recv.at[h, 0], mate)
        send(u.at[:, qcols(other, h)], s.ub.at[core, h], s.qu_recv.at[h, 1], mate)

    send_chain(0, K_)

    for copy in own_kv:
        copy.wait()
    await_bytes(s.kvp.at[0, 0, pl.ds(0, 4)], s.mate_kv)
    def to_chips(start):
        def step(i, carry):
            start(lax.rem(chip + i, chips))
            return carry

        lax.fori_loop(1, chips, step, 0)

    def loop_send(src, dst, send_sem, recv_sem, to):
        pltpu.make_async_remote_copy(
            src_ref=src,
            dst_ref=dst,
            send_sem=send_sem,
            recv_sem=recv_sem,
            device_id={"ctx": to},
            device_id_type=MESH,
        ).start()

    for h in range(2):
        for kv in range(2):
            x = lax.select(root_core == 0, s.kvp[kv, h, 4], s.kvp[kv, h, 5])
            s.cand[h, :, kv] = x.reshape(16, 16, W)
        scat[h][chip] = s.cand[h, chip]
        to_chips(
            lambda c, h=h: loop_send(
                s.cand.at[h, c],
                scat[h].at[chip],
                s.pr_send.at[0, h],
                s.pr_recv.at[0, h],
                2 * c + core,
            )
        )
        if h == 0:
            send_chain(0, V_)
    send_qu(0)

    await_bytes(s.meta.at[0], s.meta_recv)
    await_bytes(s.lens.at[pl.ds(0, groups - 1)], s.lens_recv)
    everything = s.lens[0, 0:1, :]
    for i in range(1, groups):
        everything = everything + s.lens[i, 0:1, :]
    scale = float(groups * 16 * W) / everything.astype(F32)
    scored = [rew[i].astype(F32) for i in range(16)]
    centre = functools.reduce(lambda a, b: a + b, scored) * (1.0 / 16)
    apart = [x - centre for x in scored]
    variance = functools.reduce(lambda a, b: a + b, [x * x for x in apart]) * (1.0 / 16)
    spread = jnp.sqrt(jnp.full((1, W), variance, F32))
    divisor = jnp.maximum(spread, 0.5)
    key_row = lax.broadcasted_iota(jnp.int32, (W, W), 0)
    query_col = lax.broadcasted_iota(jnp.int32, (W, W), 1)
    for o in range(2):
        for b in range(2):
            answer = s.meta[o, b, 7:8, :]
            row = jnp.zeros((1, W), F32)
            for i in range(16):
                row = row + jnp.where(answer == i, apart[i], 0.0)
            row = row / divisor * scale
            s.wt[o, b] = jnp.transpose(jnp.broadcast_to(row, (W, W)))
            of_query = jnp.broadcast_to(s.meta[o, b, 6:7, :].astype(F32), (W, W))
            of_key = jnp.transpose(of_query)
            seen = (key_row <= query_col) & (of_query >= 0.0)
            seen = seen & ((of_key == of_query) | (of_key == 0.0))
            seen = seen | (key_row == query_col)
            s.mb[o, b] = jnp.where(seen, 0.0, -jnp.inf)

    for h in range(2):
        await_bytes(scat[h].at[pl.ds(0, chips - 1)], s.pr_recv.at[0, h])
        prompt_slice = scat[h][root_chip]
        s.sel[h] = prompt_slice
        s.gath[h, chip] = prompt_slice
        to_chips(
            lambda c, h=h: loop_send(
                s.sel.at[h],
                s.gath.at[h, chip],
                s.pr_send.at[1, h],
                s.pr_recv.at[1, h],
                2 * c + core,
            )
        )
        if h == 0:
            relay_chain(0, K_)
            relay_chain(0, V_)
    for kv in range(2):
        send_chain(1, kv)
    send_qu(1)

    def where_is(t, h):
        return lax.rem(core + t // 2 + h, 2), lax.rem(t, 2)

    def gather_block(t, h, kv, to):
        o, b = where_is(t, h)
        to[t, 0 : 2 * W] = s.gath[h, :, kv].reshape(T, W)
        for i in range(HOPS):
            chosen = s.meta[o, b, 5 - i : 6 - i, :]
            both = s.kvp[kv, h, o + i].astype(F32)
            picked = jnp.where(jnp.broadcast_to(chosen, (W, W)) == 1, both[W:], both[:W])
            to[t, (2 + i) * W : (3 + i) * W] = picked.astype(BF16)
        to[t, 6 * W :] = s.kvp[kv, h, o + 4, pl.ds(pl.multiple_of(b * W, W), W), :]

    def spread_blocks(h):
        def step(t, carry):
            o, b = where_is(t, h)
            x = jnp.transpose(s.acc[t])
            s.pacc[...] += x[0 : 2 * W]
            for i in range(HOPS):
                chosen = jnp.broadcast_to(s.meta[o, b, 5 - i : 6 - i, :], (W, W)) == 1
                y = x[(2 + i) * W : (3 + i) * W]
                s.gacc[o + i, 0:W] += jnp.where(chosen, 0.0, y)
                s.gacc[o + i, W:] += jnp.where(chosen, y, 0.0)
            s.gacc[o + 4, pl.ds(pl.multiple_of(b * W, W), W), :] += x[6 * W :]
            return carry

        lax.fori_loop(0, 4, step, 0)

    def chunk(j, h):
        t = j // 2
        o, b = where_is(t, h)
        return t, o, b, lax.rem(j, 2)

    def heads(ref, o, h, b, g):
        rows = pl.ds(pl.multiple_of(b * W, W), W)
        return [
            ref.at[o, h, rows, pl.ds(pl.multiple_of((H * g + i) * W, W), W)] for i in range(H)
        ]

    def across(row):
        return jnp.concatenate([row] * H, axis=1)

    META_ROWS = (0, 1, 5, 4, 3, 2)

    def biases(o, b):
        rows = []
        for i in range(6):
            row = s.meta[o, b, META_ROWS[i] : META_ROWS[i] + 1, :]
            unseen = row <= 0 if i < 2 else row < 0
            rows.append(across(jnp.where(unseen, -jnp.inf, 0.0)))
        return rows

    def score(j, h, ps, pk):
        t, o, b, g = chunk(j, h)
        queries = jnp.concatenate([jnp.transpose(x[...]) for x in heads(s.qb, o, h, b, g)], axis=1)
        s.qt[j] = queries
        bias = biases(o, b)
        peak = None
        for lo, hi in CUTS:
            scores = nn(s.ku[t, lo * W : hi * W], queries)
            for i in range(lo, hi):
                part = scores[(i - lo) * W : (i + 1 - lo) * W]
                if i == 6:
                    part = part + across(s.mb[o, b])
                ps[i * W : (i + 1) * W] = part
                top = jnp.max(part, axis=0, keepdims=True)
                if i < 6:
                    top = top + bias[i]
                peak = top if peak is None else jnp.maximum(peak, top)
        pk[0:1] = peak * exp_scale

    def soften(j, h, ps, pk, low, do):
        t, o, b, g = chunk(j, h)
        shift = pk[0:1]
        bias = biases(o, b)
        denominator = jnp.zeros((1, M), F32)
        for i in range(7):
            here = shift if i == 6 else shift - bias[i]
            e = jnp.exp2(ps[i * W : (i + 1) * W] * exp_scale - here)
            ps[i * W : (i + 1) * W] = e
            denominator = denominator + jnp.sum(e, axis=0, keepdims=True)
        inverse = 1.0 / denominator
        for i in range(7):
            probs = ps[i * W : (i + 1) * W] * inverse
            s.pf[j, i * W : (i + 1) * W] = probs
            low[i * W : (i + 1) * W] = probs.astype(BF16)
        weight = s.wt[o, b]
        up = [
            jnp.transpose((x[...].astype(F32) * weight).astype(BF16))
            for x in heads(s.ub, o, h, b, g)
        ]
        grad_out = jnp.concatenate(up, axis=1)
        do[...] = grad_out
        s.dt[j] = grad_out

    def attend(j, h, low, do):
        t, o, b, g = chunk(j, h)
        attended = nn(s.vt[t], low[...]).astype(BF16)
        s.acc[t] += nt(do[...], low[...])
        for i, x in enumerate(heads(s.ob, o, h, b, g)):
            x[...] = jnp.transpose(attended[:, i * W : (i + 1) * W])
        product = do[...].astype(F32) * attended.astype(F32)
        s.dl[j, 0:1] = jnp.sum(product, axis=0, keepdims=True)

    def forward(h):
        def prepare(kv, whole, turned):
            await_bytes(s.kvp.at[kv, h, pl.ds(0, 2)], s.kv_relay.at[kv, h])

            def step(t, carry):
                gather_block(t, h, kv, whole)
                turned[t] = jnp.transpose(whole[t])
                return carry

            lax.fori_loop(0, 4, step, 0)

        even, odd = (s.ps0, s.pk0), (s.ps1, s.pk1)
        low_even, low_odd = (s.low0, s.do0), (s.low1, s.do1)
        prepare(K_, s.ku, s.kt)
        score(0, h, *even)
        score(1, h, *odd)
        soften(0, h, *even, *low_even)
        s.acc[...] = jnp.zeros_like(s.acc)
        prepare(V_, s.vu, s.vt)

        def step(i, carry):
            j = 2 * i
            if h == 0:

                @pl.when(i == 2)
                def _():
                    await_mate(h)

            attend(j - 2, h, *low_even)
            score(j, h, *even)
            soften(j - 1, h, *odd, *low_odd)
            attend(j - 1, h, *low_odd)
            score(j + 1, h, *odd)
            soften(j, h, *even, *low_even)
            return carry

        lax.fori_loop(1, 4, step, 0)
        attend(6, h, *low_even)
        soften(7, h, *odd, *low_odd)
        attend(7, h, *low_odd)
        spread_blocks(h)

    def await_mate(h):
        for i in range(2):
            await_bytes((s.qb, s.ub)[i].at[other, h], s.qu_recv.at[h, i])

    def score_grad(j, h, low):
        t = j // 2
        delta = s.dl[j, 0:1]
        for lo, hi in CUTS:
            rows = pl.ds(lo * W, (hi - lo) * W)
            dprobs = nn(s.vu[t, rows], s.dt[j])
            low[rows] = (s.pf[j, rows] * (dprobs - delta) * inv_root).astype(BF16)

    def input_grads(j, h, low):
        t, o, b, g = chunk(j, h)
        grad = nn(s.kt[t], low[...]).astype(BF16)
        s.acc[t] += nt(s.qt[j], low[...])
        for i, x in enumerate(heads(s.gb, o, h, b, g)):
            x[...] = jnp.transpose(grad[:, i * W : (i + 1) * W])

    def backward(h):
        s.acc[...] = jnp.zeros_like(s.acc)
        score_grad(0, h, s.low0)

        def step(i, carry):
            j = 2 * i
            score_grad(j + 1, h, s.low1)
            input_grads(j, h, s.low0)
            score_grad(j + 2, h, s.low0)
            input_grads(j + 1, h, s.low1)
            return carry

        lax.fori_loop(0, 3, step, 0)
        score_grad(7, h, s.low1)
        input_grads(6, h, s.low0)
        input_grads(7, h, s.low1)
        spread_blocks(h)

    def clear():
        s.gacc[...] = jnp.zeros_like(s.gacc)
        s.pacc[...] = jnp.zeros_like(s.pacc)

    def send_grads(kv, h):
        s.psend[kv, h] = s.pacc[...].reshape(16, 16, W).astype(BF16)
        to_chips(
            lambda c: loop_send(
                s.psend.at[kv, h, c],
                s.prec.at[kv, h, chip],
                s.ps_send.at[kv, h],
                s.ps_recv.at[kv, h],
                2 * c + core,
            )
        )
        s.prec[kv, h, chip] = s.psend[kv, h, chip]
        for i in range(4):
            s.gsend[kv, h, i] = s.gacc[i].astype(BF16)
            hop = 2 if i < 2 else 1
            send(
                s.gsend.at[kv, h, i],
                s.grecv.at[kv, h, hop - 1, core],
                s.g_recv.at[kv, h],
                2 * lax.rem(chip - hop + chips, chips) + i % 2,
            )
        s.msend[kv, h] = s.gacc[4 + other]
        send(s.msend.at[kv, h], s.mrecv.at[kv, h], s.m_recv.at[kv, h], mate)
        s.own[kv, h] = s.gacc[4 + core]

    own_out = []

    def send_rows(staged, out, h, recv_sem):
        send(staged.at[other, h], out.at[:, qcols(core, h)], recv_sem, mate)
        own_out.append(fetch(staged.at[core, h], out.at[:, qcols(core, h)]))

    def sum_prompt(kv, h):
        await_bytes(s.prec.at[kv, h, pl.ds(0, chips - 1)], s.ps_recv.at[kv, h])
        summed = jnp.sum(s.prec[kv, h].astype(F32), axis=0).astype(BF16)
        s.agsend[kv, h] = summed
        s.ag[kv, h, 16 * core + chip] = summed

        def step(i, carry):
            loop_send(
                s.agsend.at[kv, h],
                s.ag.at[kv, h, 16 * core + chip],
                s.ag_send.at[kv, h],
                s.ag_recv.at[kv, h],
                lax.rem(me + i, ring),
            )
            return carry

        lax.fori_loop(1, ring, step, 0)

    def finish(kv, h):
        out = (gk, gv)[kv]
        await_bytes(s.grecv.at[kv, h], s.g_recv.at[kv, h])
        await_bytes(s.mrecv.at[kv, h], s.m_recv.at[kv, h])
        await_bytes(s.ag.at[kv, h, pl.ds(0, ring - 1)], s.ag_recv.at[kv, h])
        for lane, mine in ((core, s.own), (other, s.mrecv)):
            x = mine[kv, h] + s.grecv[kv, h, 0, lane].astype(F32)
            x = x + s.grecv[kv, h, 1, lane].astype(F32)
            prompt = s.ag[kv, h, pl.ds(16 * lane, 16)].astype(F32).reshape(T, W)
            here = jnp.full((T, W), root, jnp.int32) == me
            out[:, kcols(lane, h)] = x + jnp.where(here, prompt, 0.0)

    for h in range(2):
        await_bytes(s.gath.at[h, pl.ds(0, chips - 1)], s.pr_recv.at[1, h])
        for copy in own_qu[h]:
            copy.wait()
        if h == 1:
            await_mate(h)
        clear()
        forward(h)
        send_grads(V_, h)
        send_rows(s.ob, attn, h, s.out_recv.at[0, h])
        if h == 0:
            relay_chain(1, K_)
            relay_chain(1, V_)
        if h == 1:
            sum_prompt(K_, 0)
        clear()
        backward(h)
        send_grads(K_, h)
        sum_prompt(V_, h)
        send_rows(s.gb, gq, h, s.out_recv.at[1, h])
    finish(V_, 0)
    finish(K_, 0)
    finish(V_, 1)
    sum_prompt(K_, 1)
    finish(K_, 1)

    for copy in own_out:
        copy.wait()
    for h in range(2):
        for i in range(2):
            await_bytes(s.ob.at[other, h], s.out_recv.at[i, h])
    for copy in sends:
        copy.wait_send()
    await_bytes(s.lens.at[pl.ds(0, groups - 1)], s.lens_send)
    for i in range(2):
        for h in range(2):
            await_bytes(s.gath.at[h, pl.ds(0, chips - 1)], s.pr_send.at[i, h])
            await_bytes(s.ag.at[i, h, pl.ds(0, ring - 1)], s.ag_send.at[i, h])
            await_bytes(s.prec.at[i, h, pl.ds(0, chips - 1)], s.ps_send.at[i, h])


def write_out(*refs):
    sems = refs[8]
    copies = [pltpu.make_async_copy(refs[i], refs[4 + i], sems.at[i]) for i in range(4)]
    for copy in copies:
        copy.start()
    for copy in copies:
        copy.wait()


def body(queries, keys, values, upstream, ancestors, segments, responses, rewards, lengths):
    any_spec = pl.BlockSpec(memory_space=pltpu.HBM)
    smem = pl.BlockSpec(memory_space=pltpu.SMEM)
    vmem = pl.BlockSpec(memory_space=pltpu.VMEM)
    results = pl.pallas_call(
        functools.partial(kernel, lax.axis_size("dp"), lax.axis_size("ctx")),
        out_shape=[
            pltpu.VMEM(queries.shape, BF16),
            pltpu.VMEM(queries.shape, BF16),
            pltpu.VMEM(keys.shape, F32),
            pltpu.VMEM(keys.shape, F32),
        ],
        in_specs=[any_spec] * 4 + [smem, vmem, vmem, smem, smem],
        out_specs=[vmem] * 4,
        scratch_shapes=list(SCRATCH.values()),
        compiler_params=pltpu.CompilerParams(
            collective_id=0, has_side_effects=True, vmem_limit_bytes=56 * 1024 * 1024
        ),
    )(
        queries,
        keys,
        values,
        upstream,
        ancestors,
        segments.reshape(2, W),
        responses.reshape(2, W),
        rewards,
        lengths,
    )
    return pl.pallas_call(
        write_out,
        out_shape=[jax.ShapeDtypeStruct(x.shape, x.dtype) for x in results],
        in_specs=[vmem] * 4,
        out_specs=[any_spec] * 4,
        scratch_shapes=[pltpu.SemaphoreType.DMA((4,))],
        compiler_params=pltpu.CompilerParams(vmem_limit_bytes=1024 * 1024),
    )(*[pltpu.with_memory_space_constraint(x, pltpu.VMEM) for x in results])


def solution(mesh):
    rows, flat = P(("dp", "ctx"), None), P(("dp", "ctx"))
    return jax.shard_map(
        body,
        mesh=mesh,
        in_specs=(rows, rows, rows, rows, rows, flat, flat, P("dp"), P("dp")),
        out_specs=(rows, rows, rows, rows),
        check_vma=False,
    )
```

```python
import functools
import math

import jax
import jax.numpy as jnp
from jax import lax
from jax.experimental import pallas as pl
from jax.experimental.pallas import tpu as pltpu
from jax.sharding import PartitionSpec as P

MESH = pl.DeviceIdType.MESH
F32, BF16 = jnp.float32, jnp.bfloat16
W = 128
T = 2 * W
R = 8
C = R * W
N = 7 * W
HOPS = 4
K_, V_ = 0, 1
CUTS = ((0, 4), (4, 7))


def nn(a, b):
    return lax.dot_general(a, b, (((1,), (0,)), ((), ())), preferred_element_type=F32)


def nt(a, b):
    return lax.dot_general(a, b, (((1,), (1,)), ((), ())), preferred_element_type=F32)


SCRATCH = dict(
    kvp=pltpu.VMEM((2, 2, 6, T, W), BF16),
    qb=pltpu.VMEM((2, 2, T, C), BF16),
    ub=pltpu.VMEM((2, 2, T, C), BF16),
    ob=pltpu.VMEM((2, 2, T, C), BF16),
    gb=pltpu.VMEM((2, 2, T, C), BF16),
    cand=pltpu.VMEM((16, 2, 2, 16, W), BF16),
    scat=pltpu.VMEM((16, 2, 2, 16, W), BF16),
    sel=pltpu.VMEM((2, 2, 16, W), BF16),
    gath=pltpu.VMEM((16, 2, 2, 16, W), BF16),
    meta=pltpu.VMEM((2, 2, 8, W), jnp.int32),
    lens=pltpu.VMEM((4, 8, W), jnp.int32),
    wt=pltpu.VMEM((2, 2, W, W), F32),
    mb=pltpu.VMEM((2, 2, W, W), F32),
    ku=pltpu.VMEM((4, N, W), BF16),
    vu=pltpu.VMEM((4, N, W), BF16),
    kt=pltpu.VMEM((4, W, N), BF16),
    vt=pltpu.VMEM((4, W, N), BF16),
    pf=pltpu.VMEM((16, N, 2 * W), F32),
    dl=pltpu.VMEM((16, 8, 2 * W), F32),
    do=pltpu.VMEM((16, 2 * W, W), BF16),
    ps0=pltpu.VMEM((N, 2 * W), F32),
    ps1=pltpu.VMEM((N, 2 * W), F32),
    pk0=pltpu.VMEM((8, 2 * W), F32),
    pk1=pltpu.VMEM((8, 2 * W), F32),
    low0=pltpu.VMEM((N, 2 * W), BF16),
    low1=pltpu.VMEM((N, 2 * W), BF16),
    do0=pltpu.VMEM((2 * W, W), BF16),
    do1=pltpu.VMEM((2 * W, W), BF16),
    acc=pltpu.VMEM((4, N, W), F32),
    gacc=pltpu.VMEM((6, T, W), F32),
    pacc=pltpu.VMEM((T, W), F32),
    own=pltpu.VMEM((2, 2, T, W), F32),
    msend=pltpu.VMEM((2, 2, T, W), F32),
    mrecv=pltpu.VMEM((2, 2, T, W), F32),
    gsend=pltpu.VMEM((2, 2, 4, T, W), BF16),
    grecv=pltpu.VMEM((2, 2, 2, 2, T, W), BF16),
    psend=pltpu.VMEM((2, 16, 2, 16, W), BF16),
    prec=pltpu.VMEM((2, 16, 2, 16, W), BF16),
    agsend=pltpu.VMEM((2, 2, 16, W), BF16),
    ag=pltpu.VMEM((2, 32, 2, 16, W), BF16),
    one_send=pltpu.SemaphoreType.DMA((64,)),
    local=pltpu.SemaphoreType.DMA((12,)),
    kv_recv=pltpu.SemaphoreType.DMA((2, 2)),
    kv_relay=pltpu.SemaphoreType.DMA((2, 2)),
    mate_kv=pltpu.SemaphoreType.DMA,
    meta_recv=pltpu.SemaphoreType.DMA,
    lens_send=pltpu.SemaphoreType.DMA,
    lens_recv=pltpu.SemaphoreType.DMA,
    qu_recv=pltpu.SemaphoreType.DMA((2, 2)),
    out_recv=pltpu.SemaphoreType.DMA((2, 2)),
    pr_send=pltpu.SemaphoreType.DMA((2,)),
    pr_recv=pltpu.SemaphoreType.DMA((2,)),
    g_recv=pltpu.SemaphoreType.DMA((2, 2)),
    m_recv=pltpu.SemaphoreType.DMA((2, 2)),
    ps_send=pltpu.SemaphoreType.DMA((2,)),
    ps_recv=pltpu.SemaphoreType.DMA((2,)),
    ag_send=pltpu.SemaphoreType.DMA((2,)),
    ag_recv=pltpu.SemaphoreType.DMA((2,)),
    ag_mate=pltpu.SemaphoreType.DMA((2,)),
)


class Names:
    def __init__(self, names, refs):
        for name, ref in zip(names, refs):
            setattr(self, name, ref)


def kernel(groups, ring, q, k, v, u, anc, seg, resp, rew, leng, attn, gq, gk, gv, *refs):
    s = Names(list(SCRATCH), refs)
    me, z = lax.axis_index("ctx"), lax.axis_index("dp")
    chips = ring // 2
    chip, core = me // 2, lax.rem(me, 2)
    other = 1 - core
    mate = 2 * chip + other
    inv_root = 1.0 / math.sqrt(W)
    exp_scale = math.log2(math.e) * inv_root

    first = anc[0, 0]
    root = jnp.where(first < 0, me, lax.div(first, 2))
    root_chip, root_core = lax.div(root, 2), lax.rem(root, 2)

    sends = []

    def send(src, dst, recv_sem, to):
        copy = pltpu.make_async_remote_copy(
            src_ref=src,
            dst_ref=dst,
            send_sem=s.one_send.at[len(sends)],
            recv_sem=recv_sem,
            device_id={"ctx": to},
            device_id_type=MESH,
        )
        copy.start()
        sends.append(copy)

    def await_bytes(ref, sem):
        pltpu.make_async_copy(ref, ref, sem).wait()

    barrier = pltpu.get_barrier_semaphore()

    def greet(to):
        pl.semaphore_signal(barrier, inc=1, device_id={"ctx": to}, device_id_type=MESH)

    def greet_chip(i, carry):
        greet(2 * lax.rem(chip + i, chips) + core)
        return carry

    lax.fori_loop(1, chips, greet_chip, 0)
    greet(mate)
    for i in (1, 2, chips - 2, chips - 1):
        greet(2 * lax.rem(chip + i, chips) + other)
    for i in range(1, groups):
        pl.semaphore_signal(
            barrier, inc=1, device_id={"dp": lax.rem(z + i, groups)}, device_id_type=MESH
        )

    def kcols(lane, h):
        return pl.ds(pl.multiple_of((2 * lane + h) * W, W), W)

    def qcols(lane, h):
        return pl.ds(pl.multiple_of((2 * lane + h) * C, C), C)

    local = []

    def fetch(src, dst):
        copy = pltpu.make_async_copy(src, dst, s.local.at[len(local)])
        copy.start()
        local.append(copy)
        return copy

    own_kv = [
        fetch(src.at[:, kcols(core, h)], s.kvp.at[kv, h, 4 + core])
        for h in range(2)
        for kv, src in ((K_, k), (V_, v))
    ]
    own_qu = [
        (
            fetch(q.at[:, qcols(core, h)], s.qb.at[core, h]),
            fetch(u.at[:, qcols(core, h)], s.ub.at[core, h]),
        )
        for h in range(2)
    ]

    total = leng[0]
    for i in range(1, 16):
        total = total + leng[i]
    s.lens[z] = jnp.full((8, W), total, jnp.int32)
    for b in range(2):
        rows = [jnp.where(anc[b, 0] >= 0, 1, 0), jnp.where(anc[b, 1] >= 0, 1, 0)]
        for hop in range(1, HOPS + 1):
            chosen = jnp.int32(-1)
            for slot in range(2, 6):
                a = anc[b, slot]
                away = lax.rem(me - lax.div(jnp.maximum(a, 0), 2) + ring, ring)
                chosen = jnp.where((a >= 0) & (away == hop), lax.rem(a, 2), chosen)
            rows.append(chosen)
        for i, row in enumerate(rows):
            s.meta[core, b, i : i + 1, :] = jnp.full((1, W), row, jnp.int32)
        s.meta[core, b, 6:7, :] = seg[b : b + 1, :]
        s.meta[core, b, 7:8, :] = resp[b : b + 1, :]

    pl.semaphore_wait(barrier, chips - 1 + 1 + 4 + groups - 1)

    for h in range(2):
        for kv, src in ((K_, k), (V_, v)):
            send(src.at[:, kcols(other, h)], s.kvp.at[kv, h, 4 + core], s.mate_kv, mate)
    for i in range(1, groups):
        pltpu.make_async_remote_copy(
            src_ref=s.lens.at[z],
            dst_ref=s.lens.at[z],
            send_sem=s.lens_send,
            recv_sem=s.lens_recv,
            device_id={"dp": lax.rem(z + i, groups)},
            device_id_type=MESH,
        ).start()
    send(s.meta.at[core], s.meta.at[core], s.meta_recv, mate)

    def send_chain(h, kv):
        for lane in range(2):
            send(
                (k, v)[kv].at[:, kcols(lane, h)],
                s.kvp.at[kv, h, 2 + core],
                s.kv_recv.at[kv, h],
                2 * lax.rem(chip + 1, chips) + lane,
            )

    def relay_chain(h, kv):
        await_bytes(s.kvp.at[kv, h, pl.ds(2, 2)], s.kv_recv.at[kv, h])
        send(
            s.kvp.at[kv, h, pl.ds(2, 2)],
            s.kvp.at[kv, h, pl.ds(0, 2)],
            s.kv_relay.at[kv, h],
            2 * lax.rem(chip + 1, chips) + core,
        )

    def send_qu(h):
        send(q.at[:, qcols(other, h)], s.qb.at[core, h], s.qu_recv.at[h, 0], mate)
        send(u.at[:, qcols(other, h)], s.ub.at[core, h], s.qu_recv.at[h, 1], mate)

    send_chain(0, K_)

    for copy in own_kv:
        copy.wait()
    await_bytes(s.kvp.at[0, 0, pl.ds(0, 4)], s.mate_kv)
    def to_chips(start):
        def step(i, carry):
            start(lax.rem(chip + i, chips))
            return carry

        lax.fori_loop(1, chips, step, 0)

    def loop_send(src, dst, send_sem, recv_sem, to):
        pltpu.make_async_remote_copy(
            src_ref=src,
            dst_ref=dst,
            send_sem=send_sem,
            recv_sem=recv_sem,
            device_id={"ctx": to},
            device_id_type=MESH,
        ).start()

    for h in range(2):
        for kv in range(2):
            x = lax.select(root_core == 0, s.kvp[kv, h, 4], s.kvp[kv, h, 5])
            s.cand[:, h, kv] = x.reshape(16, 16, W)
    s.scat[chip] = s.cand[chip]
    to_chips(
        lambda c: loop_send(
            s.cand.at[c], s.scat.at[chip], s.pr_send.at[0], s.pr_recv.at[0], 2 * c + core
        )
    )
    send_chain(0, V_)

    await_bytes(s.meta.at[0], s.meta_recv)
    await_bytes(s.lens.at[pl.ds(0, groups - 1)], s.lens_recv)
    everything = s.lens[0, 0:1, :]
    for i in range(1, groups):
        everything = everything + s.lens[i, 0:1, :]
    scale = float(groups * 16 * W) / everything.astype(F32)
    scored = [rew[i].astype(F32) for i in range(16)]
    centre = functools.reduce(lambda a, b: a + b, scored) * (1.0 / 16)
    apart = [x - centre for x in scored]
    variance = functools.reduce(lambda a, b: a + b, [x * x for x in apart]) * (1.0 / 16)
    spread = jnp.sqrt(jnp.full((1, W), variance, F32))
    divisor = jnp.maximum(spread, 0.5)
    key_row = lax.broadcasted_iota(jnp.int32, (W, W), 0)
    query_col = lax.broadcasted_iota(jnp.int32, (W, W), 1)
    for o in range(2):
        for b in range(2):
            answer = s.meta[o, b, 7:8, :]
            row = jnp.zeros((1, W), F32)
            for i in range(16):
                row = row + jnp.where(answer == i, apart[i], 0.0)
            row = row / divisor * scale
            s.wt[o, b] = jnp.transpose(jnp.broadcast_to(row, (W, W)))
            of_query = jnp.broadcast_to(s.meta[o, b, 6:7, :].astype(F32), (W, W))
            of_key = jnp.transpose(of_query)
            seen = (key_row <= query_col) & (of_query >= 0.0)
            seen = seen & ((of_key == of_query) | (of_key == 0.0))
            seen = seen | (key_row == query_col)
            s.mb[o, b] = jnp.where(seen, 0.0, -jnp.inf)

    await_bytes(s.scat.at[pl.ds(0, chips - 1)], s.pr_recv.at[0])
    prompt_slice = s.scat[root_chip]
    s.sel[...] = prompt_slice
    s.gath[chip] = prompt_slice
    to_chips(
        lambda c: loop_send(s.sel, s.gath.at[chip], s.pr_send.at[1], s.pr_recv.at[1], 2 * c + core)
    )
    relay_chain(0, K_)
    relay_chain(0, V_)
    send_qu(0)
    for kv in range(2):
        send_chain(1, kv)
    send_qu(1)

    def where_is(t, h):
        return lax.rem(core + t // 2 + h, 2), lax.rem(t, 2)

    def gather_block(t, h, kv, to):
        o, b = where_is(t, h)
        to[t, 0 : 2 * W] = s.gath[:, h, kv].reshape(T, W)
        for i in range(HOPS):
            chosen = s.meta[o, b, 5 - i : 6 - i, :]
            both = s.kvp[kv, h, o + i].astype(F32)
            picked = jnp.where(jnp.broadcast_to(chosen, (W, W)) == 1, both[W:], both[:W])
            to[t, (2 + i) * W : (3 + i) * W] = picked.astype(BF16)
        to[t, 6 * W :] = s.kvp[kv, h, o + 4, pl.ds(pl.multiple_of(b * W, W), W), :]

    def spread_blocks(h):
        def step(t, carry):
            o, b = where_is(t, h)
            s.pacc[...] += s.acc[t, 0 : 2 * W]
            for i in range(HOPS):
                chosen = jnp.broadcast_to(s.meta[o, b, 5 - i : 6 - i, :], (W, W)) == 1
                x = s.acc[t, (2 + i) * W : (3 + i) * W]
                s.gacc[o + i, 0:W] += jnp.where(chosen, 0.0, x)
                s.gacc[o + i, W:] += jnp.where(chosen, x, 0.0)
            s.gacc[o + 4, pl.ds(pl.multiple_of(b * W, W), W), :] += s.acc[t, 6 * W :]
            return carry

        lax.fori_loop(0, 4, step, 0)

    def chunk(j, h):
        t = j // 4
        o, b = where_is(t, h)
        return t, o, b, lax.rem(j, 4)

    def pair(ref, o, h, b, g):
        rows = pl.ds(pl.multiple_of(b * W, W), W)
        return [
            ref.at[o, h, rows, pl.ds(pl.multiple_of((2 * g + i) * W, W), W)] for i in range(2)
        ]

    def joined(ref, o, h, b, g):
        return jnp.concatenate([x[...] for x in pair(ref, o, h, b, g)], axis=0)

    def twice(row):
        return jnp.concatenate([row, row], axis=1)

    META_ROWS = (0, 1, 5, 4, 3, 2)

    def biases(o, b):
        rows = []
        for i in range(6):
            row = s.meta[o, b, META_ROWS[i] : META_ROWS[i] + 1, :]
            unseen = row <= 0 if i < 2 else row < 0
            rows.append(twice(jnp.where(unseen, -jnp.inf, 0.0)))
        return rows

    def score(j, h, ps, pk):
        t, o, b, g = chunk(j, h)
        queries = joined(s.qb, o, h, b, g)
        bias = biases(o, b)
        peak = None
        for lo, hi in CUTS:
            scores = nt(s.ku[t, lo * W : hi * W], queries)
            for i in range(lo, hi):
                part = scores[(i - lo) * W : (i + 1 - lo) * W]
                if i == 6:
                    part = part + twice(s.mb[o, b])
                ps[i * W : (i + 1) * W] = part
                top = jnp.max(part, axis=0, keepdims=True)
                if i < 6:
                    top = top + bias[i]
                peak = top if peak is None else jnp.maximum(peak, top)
        pk[0:1] = peak * exp_scale

    def soften(j, h, ps, pk, low, do):
        t, o, b, g = chunk(j, h)
        shift = pk[0:1]
        bias = biases(o, b)
        denominator = jnp.zeros((1, 2 * W), F32)
        for i in range(7):
            here = shift if i == 6 else shift - bias[i]
            e = jnp.exp2(ps[i * W : (i + 1) * W] * exp_scale - here)
            ps[i * W : (i + 1) * W] = e
            denominator = denominator + jnp.sum(e, axis=0, keepdims=True)
        inverse = 1.0 / denominator
        for i in range(7):
            probs = ps[i * W : (i + 1) * W] * inverse
            s.pf[j, i * W : (i + 1) * W] = probs
            low[i * W : (i + 1) * W] = probs.astype(BF16)
        weight = s.wt[o, b]
        up = [x[...].astype(F32) * weight for x in pair(s.ub, o, h, b, g)]
        grad_out = jnp.concatenate(up, axis=0).astype(BF16)
        do[...] = grad_out
        s.do[j] = grad_out

    def attend(j, h, low, do):
        t, o, b, g = chunk(j, h)
        attended = [nn(s.vt[t, :, lo * W : hi * W], low[lo * W : hi * W]) for lo, hi in CUTS]
        attended = jnp.transpose(attended[0] + attended[1]).astype(BF16)
        for lo, hi in CUTS:
            s.acc[t, lo * W : hi * W] += nn(low[lo * W : hi * W], do[...])
        for i, x in enumerate(pair(s.ob, o, h, b, g)):
            x[...] = attended[i * W : (i + 1) * W]
        product = do[...].astype(F32) * attended.astype(F32)
        s.dl[j, 0:1] = jnp.sum(jnp.transpose(product), axis=0, keepdims=True)

    def forward(h):
        def prepare(kv, whole, turned):
            await_bytes(s.kvp.at[kv, h, pl.ds(0, 2)], s.kv_relay.at[kv, h])

            def step(t, carry):
                gather_block(t, h, kv, whole)
                turned[t] = jnp.transpose(whole[t])
                return carry

            lax.fori_loop(0, 4, step, 0)

        even, odd = (s.ps0, s.pk0), (s.ps1, s.pk1)
        low_even, low_odd = (s.low0, s.do0), (s.low1, s.do1)
        prepare(K_, s.ku, s.kt)
        score(0, h, *even)
        score(1, h, *odd)
        soften(0, h, *even, *low_even)
        s.acc[...] = jnp.zeros_like(s.acc)
        prepare(V_, s.vu, s.vt)

        def step(i, carry):
            j = 2 * i
            if h == 0:

                @pl.when(i == 4)
                def _():
                    await_mate(h)

            attend(j - 2, h, *low_even)
            score(j, h, *even)
            soften(j - 1, h, *odd, *low_odd)
            attend(j - 1, h, *low_odd)
            score(j + 1, h, *odd)
            soften(j, h, *even, *low_even)
            return carry

        lax.fori_loop(1, 8, step, 0)
        attend(14, h, *low_even)
        soften(15, h, *odd, *low_odd)
        attend(15, h, *low_odd)
        spread_blocks(h)

    def await_mate(h):
        for i in range(2):
            await_bytes((s.qb, s.ub)[i].at[other, h], s.qu_recv.at[h, i])

    def score_grad(j, h, low):
        t, o, b, g = chunk(j, h)
        delta = s.dl[j, 0:1]
        for lo, hi in CUTS:
            rows = pl.ds(lo * W, (hi - lo) * W)
            dprobs = nt(s.vu[t, rows], s.do[j])
            low[rows] = (s.pf[j, rows] * (dprobs - delta) * inv_root).astype(BF16)

    def input_grads(j, h, low):
        t, o, b, g = chunk(j, h)
        grad = [nn(s.kt[t, :, lo * W : hi * W], low[lo * W : hi * W]) for lo, hi in CUTS]
        grad = jnp.transpose(grad[0] + grad[1]).astype(BF16)
        queries = joined(s.qb, o, h, b, g)
        for lo, hi in CUTS:
            s.acc[t, lo * W : hi * W] += nn(low[lo * W : hi * W], queries)
        for i, x in enumerate(pair(s.gb, o, h, b, g)):
            x[...] = grad[i * W : (i + 1) * W]

    def backward(h):
        s.acc[...] = jnp.zeros_like(s.acc)
        score_grad(0, h, s.low0)

        def step(i, carry):
            j = 2 * i
            score_grad(j + 1, h, s.low1)
            input_grads(j, h, s.low0)
            score_grad(j + 2, h, s.low0)
            input_grads(j + 1, h, s.low1)
            return carry

        lax.fori_loop(0, 7, step, 0)
        score_grad(15, h, s.low1)
        input_grads(14, h, s.low0)
        input_grads(15, h, s.low1)
        spread_blocks(h)

    def clear():
        s.gacc[...] = jnp.zeros_like(s.gacc)
        s.pacc[...] = jnp.zeros_like(s.pacc)

    def send_grads(kv, h):
        s.psend[h, :, kv] = s.pacc[...].reshape(16, 16, W).astype(BF16)
        if kv == K_:
            s.prec[h, chip] = s.psend[h, chip]
            to_chips(
                lambda c: loop_send(
                    s.psend.at[h, c],
                    s.prec.at[h, chip],
                    s.ps_send.at[h],
                    s.ps_recv.at[h],
                    2 * c + core,
                )
            )
        for i in range(4):
            s.gsend[kv, h, i] = s.gacc[i].astype(BF16)
            hop = 2 if i < 2 else 1
            send(
                s.gsend.at[kv, h, i],
                s.grecv.at[kv, h, hop - 1, core],
                s.g_recv.at[kv, h],
                2 * lax.rem(chip - hop + chips, chips) + i % 2,
            )
        s.msend[kv, h] = s.gacc[4 + other]
        send(s.msend.at[kv, h], s.mrecv.at[kv, h], s.m_recv.at[kv, h], mate)
        s.own[kv, h] = s.gacc[4 + core]

    own_out = []

    def send_rows(staged, out, h, recv_sem):
        send(staged.at[other, h], out.at[:, qcols(core, h)], recv_sem, mate)
        own_out.append(fetch(staged.at[core, h], out.at[:, qcols(core, h)]))

    def sum_prompt(h):
        await_bytes(s.prec.at[h, pl.ds(0, chips - 1)], s.ps_recv.at[h])
        summed = jnp.sum(s.prec[h].astype(F32), axis=0).astype(BF16)
        s.agsend[h] = summed
        s.ag[h, 16 * core + chip] = summed
        to_chips(
            lambda c: loop_send(
                s.agsend.at[h],
                s.ag.at[h, 16 * core + chip],
                s.ag_send.at[h],
                s.ag_recv.at[h],
                2 * c + core,
            )
        )

    def share_prompt(h):
        await_bytes(s.ag.at[h, pl.ds(0, chips - 1)], s.ag_recv.at[h])
        lane = pl.ds(16 * core, 16)
        send(s.ag.at[h, lane], s.ag.at[h, lane], s.ag_mate.at[h], mate)

    def finish(kv, h):
        out = (gk, gv)[kv]
        await_bytes(s.grecv.at[kv, h], s.g_recv.at[kv, h])
        await_bytes(s.mrecv.at[kv, h], s.m_recv.at[kv, h])
        for lane, mine in ((core, s.own), (other, s.mrecv)):
            x = mine[kv, h] + s.grecv[kv, h, 0, lane].astype(F32)
            x = x + s.grecv[kv, h, 1, lane].astype(F32)
            prompt = s.ag[h, pl.ds(16 * lane, 16), kv].astype(F32).reshape(T, W)
            here = jnp.full((T, W), root, jnp.int32) == me
            out[:, kcols(lane, h)] = x + jnp.where(here, prompt, 0.0)

    def await_shared(h):
        await_bytes(s.ag.at[h, pl.ds(0, chips)], s.ag_mate.at[h])

    await_bytes(s.gath.at[pl.ds(0, chips - 1)], s.pr_recv.at[1])
    for h in range(2):
        for copy in own_qu[h]:
            copy.wait()
        if h == 1:
            await_mate(h)
        clear()
        forward(h)
        send_grads(V_, h)
        send_rows(s.ob, attn, h, s.out_recv.at[0, h])
        if h == 0:
            relay_chain(1, K_)
            relay_chain(1, V_)
        else:
            sum_prompt(0)
        clear()
        backward(h)
        send_grads(K_, h)
        send_rows(s.gb, gq, h, s.out_recv.at[1, h])
    share_prompt(0)
    sum_prompt(1)
    await_shared(0)
    finish(V_, 0)
    finish(K_, 0)
    share_prompt(1)
    await_shared(1)
    finish(V_, 1)
    finish(K_, 1)

    for copy in own_out:
        copy.wait()
    for h in range(2):
        for i in range(2):
            await_bytes(s.ob.at[other, h], s.out_recv.at[i, h])
    for copy in sends:
        copy.wait_send()
    await_bytes(s.lens.at[pl.ds(0, groups - 1)], s.lens_send)
    for i in range(2):
        await_bytes(s.scat.at[pl.ds(0, chips - 1)], s.pr_send.at[i])
        await_bytes(s.ag.at[i, pl.ds(0, chips - 1)], s.ag_send.at[i])
        await_bytes(s.prec.at[i, pl.ds(0, chips - 1)], s.ps_send.at[i])


def write_out(*refs):
    sems = refs[8]
    copies = [pltpu.make_async_copy(refs[i], refs[4 + i], sems.at[i]) for i in range(4)]
    for copy in copies:
        copy.start()
    for copy in copies:
        copy.wait()


def body(queries, keys, values, upstream, ancestors, segments, responses, rewards, lengths):
    any_spec = pl.BlockSpec(memory_space=pltpu.HBM)
    smem = pl.BlockSpec(memory_space=pltpu.SMEM)
    vmem = pl.BlockSpec(memory_space=pltpu.VMEM)
    results = pl.pallas_call(
        functools.partial(kernel, lax.axis_size("dp"), lax.axis_size("ctx")),
        out_shape=[
            pltpu.VMEM(queries.shape, BF16),
            pltpu.VMEM(queries.shape, BF16),
            pltpu.VMEM(keys.shape, F32),
            pltpu.VMEM(keys.shape, F32),
        ],
        in_specs=[any_spec] * 4 + [smem, vmem, vmem, smem, smem],
        out_specs=[vmem] * 4,
        scratch_shapes=list(SCRATCH.values()),
        compiler_params=pltpu.CompilerParams(
            collective_id=0, has_side_effects=True, vmem_limit_bytes=56 * 1024 * 1024
        ),
    )(
        queries,
        keys,
        values,
        upstream,
        ancestors,
        segments.reshape(2, W),
        responses.reshape(2, W),
        rewards,
        lengths,
    )
    return pl.pallas_call(
        write_out,
        out_shape=[jax.ShapeDtypeStruct(x.shape, x.dtype) for x in results],
        in_specs=[vmem] * 4,
        out_specs=[any_spec] * 4,
        scratch_shapes=[pltpu.SemaphoreType.DMA((4,))],
        compiler_params=pltpu.CompilerParams(vmem_limit_bytes=1024 * 1024),
    )(*[pltpu.with_memory_space_constraint(x, pltpu.VMEM) for x in results])


def solution(mesh):
    rows, flat = P(("dp", "ctx"), None), P(("dp", "ctx"))
    return jax.shard_map(
        body,
        mesh=mesh,
        in_specs=(rows, rows, rows, rows, rows, flat, flat, P("dp"), P("dp")),
        out_specs=(rows, rows, rows, rows),
        check_vma=False,
    )
```

```python
import functools
import math

import jax
import jax.numpy as jnp
from jax import lax
from jax.experimental import pallas as pl
from jax.experimental.pallas import tpu as pltpu
from jax.sharding import PartitionSpec as P

MESH = pl.DeviceIdType.MESH
F32, BF16 = jnp.float32, jnp.bfloat16
W = 128
T = 2 * W
R = 8
C = R * W
N = 7 * W
HOPS = 4
K_, V_ = 0, 1
CUTS = ((0, 4), (4, 7))


def nn(a, b):
    return lax.dot_general(a, b, (((1,), (0,)), ((), ())), preferred_element_type=F32)


def nt(a, b):
    return lax.dot_general(a, b, (((1,), (1,)), ((), ())), preferred_element_type=F32)


SCRATCH = dict(
    kvp=pltpu.VMEM((2, 2, 6, T, W), BF16),
    qb=pltpu.VMEM((2, 2, T, C), BF16),
    ub=pltpu.VMEM((2, 2, T, C), BF16),
    ob=pltpu.VMEM((2, 2, T, C), BF16),
    gb=pltpu.VMEM((2, 2, T, C), BF16),
    cand=pltpu.VMEM((16, 2, 2, 16, W), BF16),
    scat=pltpu.VMEM((16, 2, 2, 16, W), BF16),
    sel=pltpu.VMEM((2, 2, 16, W), BF16),
    gath=pltpu.VMEM((16, 2, 2, 16, W), BF16),
    meta=pltpu.VMEM((2, 2, 8, W), jnp.int32),
    lens=pltpu.VMEM((4, 8, W), jnp.int32),
    wt=pltpu.VMEM((2, 2, W, W), F32),
    mb=pltpu.VMEM((2, 2, W, W), F32),
    ku=pltpu.VMEM((4, N, W), BF16),
    vu=pltpu.VMEM((4, N, W), BF16),
    kt=pltpu.VMEM((4, W, N), BF16),
    vt=pltpu.VMEM((4, W, N), BF16),
    pf=pltpu.VMEM((16, N, 2 * W), F32),
    dl=pltpu.VMEM((16, 8, 2 * W), F32),
    do=pltpu.VMEM((16, 2 * W, W), BF16),
    ps0=pltpu.VMEM((N, 2 * W), F32),
    ps1=pltpu.VMEM((N, 2 * W), F32),
    pk0=pltpu.VMEM((8, 2 * W), F32),
    pk1=pltpu.VMEM((8, 2 * W), F32),
    low0=pltpu.VMEM((N, 2 * W), BF16),
    low1=pltpu.VMEM((N, 2 * W), BF16),
    do0=pltpu.VMEM((2 * W, W), BF16),
    do1=pltpu.VMEM((2 * W, W), BF16),
    ds0=pltpu.VMEM((N, 2 * W), BF16),
    ds1=pltpu.VMEM((N, 2 * W), BF16),
    acc=pltpu.VMEM((4, N, W), F32),
    kacc=pltpu.VMEM((4, N, W), F32),
    gacc=pltpu.VMEM((6, T, W), F32),
    pacc=pltpu.VMEM((T, W), F32),
    own=pltpu.VMEM((2, 2, T, W), F32),
    msend=pltpu.VMEM((2, 2, T, W), F32),
    mrecv=pltpu.VMEM((2, 2, T, W), F32),
    gsend=pltpu.VMEM((2, 2, 4, T, W), BF16),
    grecv=pltpu.VMEM((2, 2, 2, 2, T, W), BF16),
    psend=pltpu.VMEM((2, 16, 2, 16, W), BF16),
    prec=pltpu.VMEM((2, 16, 2, 16, W), BF16),
    agsend=pltpu.VMEM((2, 2, 16, W), BF16),
    ag=pltpu.VMEM((2, 32, 2, 16, W), BF16),
    one_send=pltpu.SemaphoreType.DMA((64,)),
    local=pltpu.SemaphoreType.DMA((12,)),
    kv_recv=pltpu.SemaphoreType.DMA((2, 2)),
    kv_relay=pltpu.SemaphoreType.DMA((2, 2)),
    mate_kv=pltpu.SemaphoreType.DMA,
    meta_recv=pltpu.SemaphoreType.DMA,
    lens_send=pltpu.SemaphoreType.DMA,
    lens_recv=pltpu.SemaphoreType.DMA,
    qu_recv=pltpu.SemaphoreType.DMA((2, 2)),
    out_recv=pltpu.SemaphoreType.DMA((2, 2)),
    pr_send=pltpu.SemaphoreType.DMA((2,)),
    pr_recv=pltpu.SemaphoreType.DMA((2,)),
    g_recv=pltpu.SemaphoreType.DMA((2, 2)),
    m_recv=pltpu.SemaphoreType.DMA((2, 2)),
    ps_send=pltpu.SemaphoreType.DMA((2,)),
    ps_recv=pltpu.SemaphoreType.DMA((2,)),
    ag_send=pltpu.SemaphoreType.DMA((2,)),
    ag_recv=pltpu.SemaphoreType.DMA((2,)),
    ag_mate=pltpu.SemaphoreType.DMA((2,)),
)


class Names:
    def __init__(self, names, refs):
        for name, ref in zip(names, refs):
            setattr(self, name, ref)


def kernel(groups, ring, q, k, v, u, anc, seg, resp, rew, leng, attn, gq, gk, gv, *refs):
    s = Names(list(SCRATCH), refs)
    me, z = lax.axis_index("ctx"), lax.axis_index("dp")
    chips = ring // 2
    chip, core = me // 2, lax.rem(me, 2)
    other = 1 - core
    mate = 2 * chip + other
    inv_root = 1.0 / math.sqrt(W)
    exp_scale = math.log2(math.e) * inv_root

    first = anc[0, 0]
    root = jnp.where(first < 0, me, lax.div(first, 2))
    root_chip, root_core = lax.div(root, 2), lax.rem(root, 2)

    sends = []

    def send(src, dst, recv_sem, to):
        copy = pltpu.make_async_remote_copy(
            src_ref=src,
            dst_ref=dst,
            send_sem=s.one_send.at[len(sends)],
            recv_sem=recv_sem,
            device_id={"ctx": to},
            device_id_type=MESH,
        )
        copy.start()
        sends.append(copy)

    def await_bytes(ref, sem):
        pltpu.make_async_copy(ref, ref, sem).wait()

    barrier = pltpu.get_barrier_semaphore()

    def greet(to):
        pl.semaphore_signal(barrier, inc=1, device_id={"ctx": to}, device_id_type=MESH)

    def greet_chip(i, carry):
        greet(2 * lax.rem(chip + i, chips) + core)
        return carry

    lax.fori_loop(1, chips, greet_chip, 0)
    greet(mate)
    for i in (1, 2, chips - 2, chips - 1):
        greet(2 * lax.rem(chip + i, chips) + other)
    for i in range(1, groups):
        pl.semaphore_signal(
            barrier, inc=1, device_id={"dp": lax.rem(z + i, groups)}, device_id_type=MESH
        )

    def kcols(lane, h):
        return pl.ds(pl.multiple_of((2 * lane + h) * W, W), W)

    def qcols(lane, h):
        return pl.ds(pl.multiple_of((2 * lane + h) * C, C), C)

    local = []

    def fetch(src, dst):
        copy = pltpu.make_async_copy(src, dst, s.local.at[len(local)])
        copy.start()
        local.append(copy)
        return copy

    own_kv = [
        fetch(src.at[:, kcols(core, h)], s.kvp.at[kv, h, 4 + core])
        for h in range(2)
        for kv, src in ((K_, k), (V_, v))
    ]
    own_qu = [
        (
            fetch(q.at[:, qcols(core, h)], s.qb.at[core, h]),
            fetch(u.at[:, qcols(core, h)], s.ub.at[core, h]),
        )
        for h in range(2)
    ]

    total = leng[0]
    for i in range(1, 16):
        total = total + leng[i]
    s.lens[z] = jnp.full((8, W), total, jnp.int32)
    for b in range(2):
        rows = [jnp.where(anc[b, 0] >= 0, 1, 0), jnp.where(anc[b, 1] >= 0, 1, 0)]
        for hop in range(1, HOPS + 1):
            chosen = jnp.int32(-1)
            for slot in range(2, 6):
                a = anc[b, slot]
                away = lax.rem(me - lax.div(jnp.maximum(a, 0), 2) + ring, ring)
                chosen = jnp.where((a >= 0) & (away == hop), lax.rem(a, 2), chosen)
            rows.append(chosen)
        for i, row in enumerate(rows):
            s.meta[core, b, i : i + 1, :] = jnp.full((1, W), row, jnp.int32)
        s.meta[core, b, 6:7, :] = seg[b : b + 1, :]
        s.meta[core, b, 7:8, :] = resp[b : b + 1, :]

    pl.semaphore_wait(barrier, chips - 1 + 1 + 4 + groups - 1)

    for h in range(2):
        for kv, src in ((K_, k), (V_, v)):
            send(src.at[:, kcols(other, h)], s.kvp.at[kv, h, 4 + core], s.mate_kv, mate)
    for i in range(1, groups):
        pltpu.make_async_remote_copy(
            src_ref=s.lens.at[z],
            dst_ref=s.lens.at[z],
            send_sem=s.lens_send,
            recv_sem=s.lens_recv,
            device_id={"dp": lax.rem(z + i, groups)},
            device_id_type=MESH,
        ).start()
    send(s.meta.at[core], s.meta.at[core], s.meta_recv, mate)

    def send_chain(h, kv):
        for lane in range(2):
            send(
                (k, v)[kv].at[:, kcols(lane, h)],
                s.kvp.at[kv, h, 2 + core],
                s.kv_recv.at[kv, h],
                2 * lax.rem(chip + 1, chips) + lane,
            )

    def relay_chain(h, kv):
        await_bytes(s.kvp.at[kv, h, pl.ds(2, 2)], s.kv_recv.at[kv, h])
        send(
            s.kvp.at[kv, h, pl.ds(2, 2)],
            s.kvp.at[kv, h, pl.ds(0, 2)],
            s.kv_relay.at[kv, h],
            2 * lax.rem(chip + 1, chips) + core,
        )

    def send_qu(h):
        send(q.at[:, qcols(other, h)], s.qb.at[core, h], s.qu_recv.at[h, 0], mate)
        send(u.at[:, qcols(other, h)], s.ub.at[core, h], s.qu_recv.at[h, 1], mate)

    send_chain(0, K_)

    for copy in own_kv:
        copy.wait()
    await_bytes(s.kvp.at[0, 0, pl.ds(0, 4)], s.mate_kv)
    def to_chips(start):
        def step(i, carry):
            start(lax.rem(chip + i, chips))
            return carry

        lax.fori_loop(1, chips, step, 0)

    def loop_send(src, dst, send_sem, recv_sem, to):
        pltpu.make_async_remote_copy(
            src_ref=src,
            dst_ref=dst,
            send_sem=send_sem,
            recv_sem=recv_sem,
            device_id={"ctx": to},
            device_id_type=MESH,
        ).start()

    for h in range(2):
        for kv in range(2):
            x = lax.select(root_core == 0, s.kvp[kv, h, 4], s.kvp[kv, h, 5])
            s.cand[:, h, kv] = x.reshape(16, 16, W)
    s.scat[chip] = s.cand[chip]
    to_chips(
        lambda c: loop_send(
            s.cand.at[c], s.scat.at[chip], s.pr_send.at[0], s.pr_recv.at[0], 2 * c + core
        )
    )
    send_chain(0, V_)

    await_bytes(s.meta.at[0], s.meta_recv)
    await_bytes(s.lens.at[pl.ds(0, groups - 1)], s.lens_recv)
    everything = s.lens[0, 0:1, :]
    for i in range(1, groups):
        everything = everything + s.lens[i, 0:1, :]
    scale = float(groups * 16 * W) / everything.astype(F32)
    scored = [rew[i].astype(F32) for i in range(16)]
    centre = functools.reduce(lambda a, b: a + b, scored) * (1.0 / 16)
    apart = [x - centre for x in scored]
    variance = functools.reduce(lambda a, b: a + b, [x * x for x in apart]) * (1.0 / 16)
    spread = jnp.sqrt(jnp.full((1, W), variance, F32))
    divisor = jnp.maximum(spread, 0.5)
    key_row = lax.broadcasted_iota(jnp.int32, (W, W), 0)
    query_col = lax.broadcasted_iota(jnp.int32, (W, W), 1)
    for o in range(2):
        for b in range(2):
            answer = s.meta[o, b, 7:8, :]
            row = jnp.zeros((1, W), F32)
            for i in range(16):
                row = row + jnp.where(answer == i, apart[i], 0.0)
            row = row / divisor * scale
            s.wt[o, b] = jnp.transpose(jnp.broadcast_to(row, (W, W)))
            of_query = jnp.broadcast_to(s.meta[o, b, 6:7, :].astype(F32), (W, W))
            of_key = jnp.transpose(of_query)
            seen = (key_row <= query_col) & (of_query >= 0.0)
            seen = seen & ((of_key == of_query) | (of_key == 0.0))
            seen = seen | (key_row == query_col)
            s.mb[o, b] = jnp.where(seen, 0.0, -jnp.inf)

    await_bytes(s.scat.at[pl.ds(0, chips - 1)], s.pr_recv.at[0])
    prompt_slice = s.scat[root_chip]
    s.sel[...] = prompt_slice
    s.gath[chip] = prompt_slice
    to_chips(
        lambda c: loop_send(s.sel, s.gath.at[chip], s.pr_send.at[1], s.pr_recv.at[1], 2 * c + core)
    )
    relay_chain(0, K_)
    relay_chain(0, V_)
    send_qu(0)
    for kv in range(2):
        send_chain(1, kv)
    send_qu(1)

    def where_is(t, h):
        return lax.rem(core + t // 2 + h, 2), lax.rem(t, 2)

    def gather_block(t, h, kv, to):
        o, b = where_is(t, h)
        to[t, 0 : 2 * W] = s.gath[:, h, kv].reshape(T, W)
        for i in range(HOPS):
            chosen = s.meta[o, b, 5 - i : 6 - i, :]
            both = s.kvp[kv, h, o + i].astype(F32)
            picked = jnp.where(jnp.broadcast_to(chosen, (W, W)) == 1, both[W:], both[:W])
            to[t, (2 + i) * W : (3 + i) * W] = picked.astype(BF16)
        to[t, 6 * W :] = s.kvp[kv, h, o + 4, pl.ds(pl.multiple_of(b * W, W), W), :]

    def spread_blocks(h, acc):
        def step(t, carry):
            o, b = where_is(t, h)
            s.pacc[...] += acc[t, 0 : 2 * W]
            for i in range(HOPS):
                chosen = jnp.broadcast_to(s.meta[o, b, 5 - i : 6 - i, :], (W, W)) == 1
                x = acc[t, (2 + i) * W : (3 + i) * W]
                s.gacc[o + i, 0:W] += jnp.where(chosen, 0.0, x)
                s.gacc[o + i, W:] += jnp.where(chosen, x, 0.0)
            s.gacc[o + 4, pl.ds(pl.multiple_of(b * W, W), W), :] += acc[t, 6 * W :]
            return carry

        lax.fori_loop(0, 4, step, 0)

    def chunk(j, h):
        t = j // 4
        o, b = where_is(t, h)
        return t, o, b, lax.rem(j, 4)

    def pair(ref, o, h, b, g):
        rows = pl.ds(pl.multiple_of(b * W, W), W)
        return [
            ref.at[o, h, rows, pl.ds(pl.multiple_of((2 * g + i) * W, W), W)] for i in range(2)
        ]

    def joined(ref, o, h, b, g):
        return jnp.concatenate([x[...] for x in pair(ref, o, h, b, g)], axis=0)

    def twice(row):
        return jnp.concatenate([row, row], axis=1)

    META_ROWS = (0, 1, 5, 4, 3, 2)

    def biases(o, b):
        rows = []
        for i in range(6):
            row = s.meta[o, b, META_ROWS[i] : META_ROWS[i] + 1, :]
            unseen = row <= 0 if i < 2 else row < 0
            rows.append(twice(jnp.where(unseen, -jnp.inf, 0.0)))
        return rows

    def score(j, h, ps, pk):
        t, o, b, g = chunk(j, h)
        queries = joined(s.qb, o, h, b, g)
        bias = biases(o, b)
        peak = None
        for lo, hi in CUTS:
            scores = nt(s.ku[t, lo * W : hi * W], queries)
            for i in range(lo, hi):
                part = scores[(i - lo) * W : (i + 1 - lo) * W]
                if i == 6:
                    part = part + twice(s.mb[o, b])
                ps[i * W : (i + 1) * W] = part
                top = jnp.max(part, axis=0, keepdims=True)
                if i < 6:
                    top = top + bias[i]
                peak = top if peak is None else jnp.maximum(peak, top)
        pk[0:1] = peak * exp_scale

    def soften(j, h, ps, pk, low, do):
        t, o, b, g = chunk(j, h)
        shift = pk[0:1]
        bias = biases(o, b)
        denominator = jnp.zeros((1, 2 * W), F32)
        for i in range(7):
            here = shift if i == 6 else shift - bias[i]
            e = jnp.exp2(ps[i * W : (i + 1) * W] * exp_scale - here)
            ps[i * W : (i + 1) * W] = e
            denominator = denominator + jnp.sum(e, axis=0, keepdims=True)
        inverse = 1.0 / denominator
        for i in range(7):
            probs = ps[i * W : (i + 1) * W] * inverse
            s.pf[j, i * W : (i + 1) * W] = probs
            low[i * W : (i + 1) * W] = probs.astype(BF16)
        weight = s.wt[o, b]
        up = [x[...].astype(F32) * weight for x in pair(s.ub, o, h, b, g)]
        grad_out = jnp.concatenate(up, axis=0).astype(BF16)
        do[...] = grad_out
        s.do[j] = grad_out

    def attend(j, h, low, do):
        t, o, b, g = chunk(j, h)
        attended = [nn(s.vt[t, :, lo * W : hi * W], low[lo * W : hi * W]) for lo, hi in CUTS]
        turned = (attended[0] + attended[1]).astype(BF16)
        attended = jnp.transpose(turned)
        for lo, hi in CUTS:
            s.acc[t, lo * W : hi * W] += nn(low[lo * W : hi * W], do[...])
        for i, x in enumerate(pair(s.ob, o, h, b, g)):
            x[...] = attended[i * W : (i + 1) * W]
        product = jnp.transpose(do[...]).astype(F32) * turned.astype(F32)
        s.dl[j, 0:1] = jnp.sum(product, axis=0, keepdims=True)

    def forward(h):
        def prepare(kv, whole, turned):
            await_bytes(s.kvp.at[kv, h, pl.ds(0, 2)], s.kv_relay.at[kv, h])

            def step(t, carry):
                gather_block(t, h, kv, whole)
                turned[t] = jnp.transpose(whole[t])
                return carry

            lax.fori_loop(0, 4, step, 0)

        even, odd = (s.ps0, s.pk0), (s.ps1, s.pk1)
        low_even, low_odd = (s.low0, s.do0), (s.low1, s.do1)
        prepare(K_, s.ku, s.kt)
        score(0, h, *even)
        score(1, h, *odd)
        soften(0, h, *even, *low_even)
        s.acc[...] = jnp.zeros_like(s.acc)
        prepare(V_, s.vu, s.vt)

        def step(i, carry):
            j = 2 * i
            if h == 0:

                @pl.when(i == 4)
                def _():
                    await_mate(h)

            attend(j - 2, h, *low_even)
            score(j, h, *even)
            soften(j - 1, h, *odd, *low_odd)
            attend(j - 1, h, *low_odd)
            score(j + 1, h, *odd)
            soften(j, h, *even, *low_even)
            return carry

        lax.fori_loop(1, 8, step, 0)
        attend(14, h, *low_even)
        soften(15, h, *odd, *low_odd)
        s.kacc[...] = jnp.zeros_like(s.kacc)
        score_grad(0, h, s.ds0)
        attend(15, h, *low_odd)
        score_grad(1, h, s.ds1)
        input_grads(0, h, s.ds0)
        spread_blocks(h, s.acc)

    def await_mate(h):
        for i in range(2):
            await_bytes((s.qb, s.ub)[i].at[other, h], s.qu_recv.at[h, i])

    def score_grad(j, h, low):
        t, o, b, g = chunk(j, h)
        delta = s.dl[j, 0:1]
        for lo, hi in CUTS:
            rows = pl.ds(lo * W, (hi - lo) * W)
            dprobs = nt(s.vu[t, rows], s.do[j])
            low[rows] = (s.pf[j, rows] * (dprobs - delta) * inv_root).astype(BF16)

    def input_grads(j, h, low):
        t, o, b, g = chunk(j, h)
        grad = [nn(s.kt[t, :, lo * W : hi * W], low[lo * W : hi * W]) for lo, hi in CUTS]
        grad = jnp.transpose((grad[0] + grad[1]).astype(BF16))
        queries = joined(s.qb, o, h, b, g)
        for lo, hi in CUTS:
            s.kacc[t, lo * W : hi * W] += nn(low[lo * W : hi * W], queries)
        for i, x in enumerate(pair(s.gb, o, h, b, g)):
            x[...] = grad[i * W : (i + 1) * W]

    def backward(h):
        def step(i, carry):
            j = 2 * i
            score_grad(j, h, s.ds0)
            input_grads(j - 1, h, s.ds1)
            score_grad(j + 1, h, s.ds1)
            input_grads(j, h, s.ds0)
            return carry

        lax.fori_loop(1, 8, step, 0)
        input_grads(15, h, s.ds1)
        spread_blocks(h, s.kacc)

    def clear():
        s.gacc[...] = jnp.zeros_like(s.gacc)
        s.pacc[...] = jnp.zeros_like(s.pacc)

    def send_grads(kv, h):
        s.psend[h, :, kv] = s.pacc[...].reshape(16, 16, W).astype(BF16)
        if kv == K_:
            s.prec[h, chip] = s.psend[h, chip]
            to_chips(
                lambda c: loop_send(
                    s.psend.at[h, c],
                    s.prec.at[h, chip],
                    s.ps_send.at[h],
                    s.ps_recv.at[h],
                    2 * c + core,
                )
            )
        for i in range(4):
            s.gsend[kv, h, i] = s.gacc[i].astype(BF16)
            hop = 2 if i < 2 else 1
            send(
                s.gsend.at[kv, h, i],
                s.grecv.at[kv, h, hop - 1, core],
                s.g_recv.at[kv, h],
                2 * lax.rem(chip - hop + chips, chips) + i % 2,
            )
        s.msend[kv, h] = s.gacc[4 + other]
        send(s.msend.at[kv, h], s.mrecv.at[kv, h], s.m_recv.at[kv, h], mate)
        s.own[kv, h] = s.gacc[4 + core]

    own_out = []

    def send_rows(staged, out, h, recv_sem):
        send(staged.at[other, h], out.at[:, qcols(core, h)], recv_sem, mate)
        own_out.append(fetch(staged.at[core, h], out.at[:, qcols(core, h)]))

    def sum_prompt(h):
        await_bytes(s.prec.at[h, pl.ds(0, chips - 1)], s.ps_recv.at[h])
        summed = jnp.sum(s.prec[h].astype(F32), axis=0).astype(BF16)
        s.agsend[h] = summed
        s.ag[h, 16 * core + chip] = summed
        to_chips(
            lambda c: loop_send(
                s.agsend.at[h],
                s.ag.at[h, 16 * core + chip],
                s.ag_send.at[h],
                s.ag_recv.at[h],
                2 * c + core,
            )
        )

    def share_prompt(h):
        await_bytes(s.ag.at[h, pl.ds(0, chips - 1)], s.ag_recv.at[h])
        lane = pl.ds(16 * core, 16)
        send(s.ag.at[h, lane], s.ag.at[h, lane], s.ag_mate.at[h], mate)

    def finish(kv, h):
        out = (gk, gv)[kv]
        await_bytes(s.grecv.at[kv, h], s.g_recv.at[kv, h])
        await_bytes(s.mrecv.at[kv, h], s.m_recv.at[kv, h])
        for lane, mine in ((core, s.own), (other, s.mrecv)):
            x = mine[kv, h] + s.grecv[kv, h, 0, lane].astype(F32)
            x = x + s.grecv[kv, h, 1, lane].astype(F32)
            prompt = s.ag[h, pl.ds(16 * lane, 16), kv].astype(F32).reshape(T, W)
            here = jnp.full((T, W), root, jnp.int32) == me
            out[:, kcols(lane, h)] = x + jnp.where(here, prompt, 0.0)

    def await_shared(h):
        await_bytes(s.ag.at[h, pl.ds(0, chips)], s.ag_mate.at[h])

    await_bytes(s.gath.at[pl.ds(0, chips - 1)], s.pr_recv.at[1])
    for h in range(2):
        for copy in own_qu[h]:
            copy.wait()
        if h == 1:
            await_mate(h)
        clear()
        forward(h)
        send_grads(V_, h)
        send_rows(s.ob, attn, h, s.out_recv.at[0, h])
        if h == 0:
            relay_chain(1, K_)
            relay_chain(1, V_)
        else:
            sum_prompt(0)
        clear()
        backward(h)
        send_grads(K_, h)
        send_rows(s.gb, gq, h, s.out_recv.at[1, h])
    share_prompt(0)
    sum_prompt(1)
    await_shared(0)
    finish(V_, 0)
    finish(K_, 0)
    share_prompt(1)
    await_shared(1)
    finish(V_, 1)
    finish(K_, 1)

    for copy in own_out:
        copy.wait()
    for h in range(2):
        for i in range(2):
            await_bytes(s.ob.at[other, h], s.out_recv.at[i, h])
    for copy in sends:
        copy.wait_send()
    await_bytes(s.lens.at[pl.ds(0, groups - 1)], s.lens_send)
    for i in range(2):
        await_bytes(s.scat.at[pl.ds(0, chips - 1)], s.pr_send.at[i])
        await_bytes(s.ag.at[i, pl.ds(0, chips - 1)], s.ag_send.at[i])
        await_bytes(s.prec.at[i, pl.ds(0, chips - 1)], s.ps_send.at[i])


def write_out(*refs):
    sems = refs[8]
    copies = [pltpu.make_async_copy(refs[i], refs[4 + i], sems.at[i]) for i in range(4)]
    for copy in copies:
        copy.start()
    for copy in copies:
        copy.wait()


def body(queries, keys, values, upstream, ancestors, segments, responses, rewards, lengths):
    any_spec = pl.BlockSpec(memory_space=pltpu.HBM)
    smem = pl.BlockSpec(memory_space=pltpu.SMEM)
    vmem = pl.BlockSpec(memory_space=pltpu.VMEM)
    results = pl.pallas_call(
        functools.partial(kernel, lax.axis_size("dp"), lax.axis_size("ctx")),
        out_shape=[
            pltpu.VMEM(queries.shape, BF16),
            pltpu.VMEM(queries.shape, BF16),
            pltpu.VMEM(keys.shape, F32),
            pltpu.VMEM(keys.shape, F32),
        ],
        in_specs=[any_spec] * 4 + [smem, vmem, vmem, smem, smem],
        out_specs=[vmem] * 4,
        scratch_shapes=list(SCRATCH.values()),
        compiler_params=pltpu.CompilerParams(
            collective_id=0, has_side_effects=True, vmem_limit_bytes=56 * 1024 * 1024
        ),
    )(
        queries,
        keys,
        values,
        upstream,
        ancestors,
        segments.reshape(2, W),
        responses.reshape(2, W),
        rewards,
        lengths,
    )
    return pl.pallas_call(
        write_out,
        out_shape=[jax.ShapeDtypeStruct(x.shape, x.dtype) for x in results],
        in_specs=[vmem] * 4,
        out_specs=[any_spec] * 4,
        scratch_shapes=[pltpu.SemaphoreType.DMA((4,))],
        compiler_params=pltpu.CompilerParams(vmem_limit_bytes=1024 * 1024),
    )(*[pltpu.with_memory_space_constraint(x, pltpu.VMEM) for x in results])


def solution(mesh):
    rows, flat = P(("dp", "ctx"), None), P(("dp", "ctx"))
    return jax.shard_map(
        body,
        mesh=mesh,
        in_specs=(rows, rows, rows, rows, rows, flat, flat, P("dp"), P("dp")),
        out_specs=(rows, rows, rows, rows),
        check_vma=False,
    )
```

```python
import functools
import math

import jax
import jax.numpy as jnp
from jax import lax
from jax.experimental import pallas as pl
from jax.experimental.pallas import tpu as pltpu
from jax.sharding import PartitionSpec as P

MESH = pl.DeviceIdType.MESH
F32, BF16 = jnp.float32, jnp.bfloat16
W = 128
T = 2 * W
R = 8
C = R * W
N = 7 * W
HOPS = 4
K_, V_ = 0, 1
CUTS = ((0, 7),)


def nn(a, b):
    return lax.dot_general(a, b, (((1,), (0,)), ((), ())), preferred_element_type=F32)


def nt(a, b):
    return lax.dot_general(a, b, (((1,), (1,)), ((), ())), preferred_element_type=F32)


SCRATCH = dict(
    kvp=pltpu.VMEM((2, 2, 6, T, W), BF16),
    qb=pltpu.VMEM((2, 2, T, C), BF16),
    ub=pltpu.VMEM((2, 2, T, C), BF16),
    ob=pltpu.VMEM((2, 2, T, C), BF16),
    gb=pltpu.VMEM((2, 2, T, C), BF16),
    cand=pltpu.VMEM((16, 2, 2, 16, W), BF16),
    scat=pltpu.VMEM((16, 2, 2, 16, W), BF16),
    sel=pltpu.VMEM((2, 2, 16, W), BF16),
    gath=pltpu.VMEM((16, 2, 2, 16, W), BF16),
    meta=pltpu.VMEM((2, 2, 8, W), jnp.int32),
    lens=pltpu.VMEM((4, 8, W), jnp.int32),
    wt=pltpu.VMEM((2, 2, W, W), F32),
    mb=pltpu.VMEM((2, 2, W, W), F32),
    ku=pltpu.VMEM((4, N, W), BF16),
    vu=pltpu.VMEM((4, N, W), BF16),
    kt=pltpu.VMEM((4, W, N), BF16),
    vt=pltpu.VMEM((4, W, N), BF16),
    pf=pltpu.VMEM((16, N, 2 * W), F32),
    dl=pltpu.VMEM((16, 8, 2 * W), F32),
    do=pltpu.VMEM((16, 2 * W, W), BF16),
    ps0=pltpu.VMEM((N, 2 * W), F32),
    ps1=pltpu.VMEM((N, 2 * W), F32),
    pk0=pltpu.VMEM((8, 2 * W), F32),
    pk1=pltpu.VMEM((8, 2 * W), F32),
    low0=pltpu.VMEM((N, 2 * W), BF16),
    low1=pltpu.VMEM((N, 2 * W), BF16),
    do0=pltpu.VMEM((2 * W, W), BF16),
    do1=pltpu.VMEM((2 * W, W), BF16),
    ds0=pltpu.VMEM((N, 2 * W), BF16),
    ds1=pltpu.VMEM((N, 2 * W), BF16),
    acc=pltpu.VMEM((4, N, W), F32),
    kacc=pltpu.VMEM((4, N, W), F32),
    gacc=pltpu.VMEM((6, T, W), F32),
    pacc=pltpu.VMEM((T, W), F32),
    own=pltpu.VMEM((2, 2, T, W), F32),
    msend=pltpu.VMEM((2, 2, T, W), F32),
    mrecv=pltpu.VMEM((2, 2, T, W), F32),
    gsend=pltpu.VMEM((2, 2, 4, T, W), BF16),
    grecv=pltpu.VMEM((2, 2, 2, 2, T, W), BF16),
    psend=pltpu.VMEM((2, 16, 2, 16, W), BF16),
    prec=pltpu.VMEM((2, 16, 2, 16, W), BF16),
    agsend=pltpu.VMEM((2, 2, 16, W), BF16),
    ag=pltpu.VMEM((2, 32, 2, 16, W), BF16),
    one_send=pltpu.SemaphoreType.DMA((64,)),
    local=pltpu.SemaphoreType.DMA((12,)),
    kv_recv=pltpu.SemaphoreType.DMA((2, 2)),
    kv_relay=pltpu.SemaphoreType.DMA((2, 2)),
    mate_kv=pltpu.SemaphoreType.DMA,
    meta_recv=pltpu.SemaphoreType.DMA,
    lens_send=pltpu.SemaphoreType.DMA,
    lens_recv=pltpu.SemaphoreType.DMA,
    qu_recv=pltpu.SemaphoreType.DMA((2, 2)),
    out_recv=pltpu.SemaphoreType.DMA((2, 2)),
    pr_send=pltpu.SemaphoreType.DMA((2,)),
    pr_recv=pltpu.SemaphoreType.DMA((2,)),
    g_recv=pltpu.SemaphoreType.DMA((2, 2)),
    m_recv=pltpu.SemaphoreType.DMA((2, 2)),
    ps_send=pltpu.SemaphoreType.DMA((2,)),
    ps_recv=pltpu.SemaphoreType.DMA((2,)),
    ag_send=pltpu.SemaphoreType.DMA((2,)),
    ag_recv=pltpu.SemaphoreType.DMA((2,)),
    ag_mate=pltpu.SemaphoreType.DMA((2,)),
)


class Names:
    def __init__(self, names, refs):
        for name, ref in zip(names, refs):
            setattr(self, name, ref)


def kernel(groups, ring, q, k, v, u, anc, seg, resp, rew, leng, attn, gq, gk, gv, *refs):
    s = Names(list(SCRATCH), refs)
    me, z = lax.axis_index("ctx"), lax.axis_index("dp")
    chips = ring // 2
    chip, core = me // 2, lax.rem(me, 2)
    other = 1 - core
    mate = 2 * chip + other
    inv_root = 1.0 / math.sqrt(W)
    exp_scale = math.log2(math.e) * inv_root

    first = anc[0, 0]
    root = jnp.where(first < 0, me, lax.div(first, 2))
    root_chip, root_core = lax.div(root, 2), lax.rem(root, 2)

    sends = []

    def send(src, dst, recv_sem, to):
        copy = pltpu.make_async_remote_copy(
            src_ref=src,
            dst_ref=dst,
            send_sem=s.one_send.at[len(sends)],
            recv_sem=recv_sem,
            device_id={"ctx": to},
            device_id_type=MESH,
        )
        copy.start()
        sends.append(copy)

    def await_bytes(ref, sem):
        pltpu.make_async_copy(ref, ref, sem).wait()

    barrier = pltpu.get_barrier_semaphore()

    def greet(to):
        pl.semaphore_signal(barrier, inc=1, device_id={"ctx": to}, device_id_type=MESH)

    def greet_chip(i, carry):
        greet(2 * lax.rem(chip + i, chips) + core)
        return carry

    lax.fori_loop(1, chips, greet_chip, 0)
    greet(mate)
    for i in (1, 2, chips - 2, chips - 1):
        greet(2 * lax.rem(chip + i, chips) + other)
    for i in range(1, groups):
        pl.semaphore_signal(
            barrier, inc=1, device_id={"dp": lax.rem(z + i, groups)}, device_id_type=MESH
        )

    def kcols(lane, h):
        return pl.ds(pl.multiple_of((2 * lane + h) * W, W), W)

    def qcols(lane, h):
        return pl.ds(pl.multiple_of((2 * lane + h) * C, C), C)

    local = []

    def fetch(src, dst):
        copy = pltpu.make_async_copy(src, dst, s.local.at[len(local)])
        copy.start()
        local.append(copy)
        return copy

    own_kv = [
        fetch(src.at[:, kcols(core, h)], s.kvp.at[kv, h, 4 + core])
        for h in range(2)
        for kv, src in ((K_, k), (V_, v))
    ]
    own_qu = [
        (
            fetch(q.at[:, qcols(core, h)], s.qb.at[core, h]),
            fetch(u.at[:, qcols(core, h)], s.ub.at[core, h]),
        )
        for h in range(2)
    ]

    total = leng[0]
    for i in range(1, 16):
        total = total + leng[i]
    s.lens[z] = jnp.full((8, W), total, jnp.int32)
    for b in range(2):
        rows = [jnp.where(anc[b, 0] >= 0, 1, 0), jnp.where(anc[b, 1] >= 0, 1, 0)]
        for hop in range(1, HOPS + 1):
            chosen = jnp.int32(-1)
            for slot in range(2, 6):
                a = anc[b, slot]
                away = lax.rem(me - lax.div(jnp.maximum(a, 0), 2) + ring, ring)
                chosen = jnp.where((a >= 0) & (away == hop), lax.rem(a, 2), chosen)
            rows.append(chosen)
        for i, row in enumerate(rows):
            s.meta[core, b, i : i + 1, :] = jnp.full((1, W), row, jnp.int32)
        s.meta[core, b, 6:7, :] = seg[b : b + 1, :]
        s.meta[core, b, 7:8, :] = resp[b : b + 1, :]

    pl.semaphore_wait(barrier, chips - 1 + 1 + 4 + groups - 1)

    for h in range(2):
        for kv, src in ((K_, k), (V_, v)):
            send(src.at[:, kcols(other, h)], s.kvp.at[kv, h, 4 + core], s.mate_kv, mate)
    for i in range(1, groups):
        pltpu.make_async_remote_copy(
            src_ref=s.lens.at[z],
            dst_ref=s.lens.at[z],
            send_sem=s.lens_send,
            recv_sem=s.lens_recv,
            device_id={"dp": lax.rem(z + i, groups)},
            device_id_type=MESH,
        ).start()
    send(s.meta.at[core], s.meta.at[core], s.meta_recv, mate)

    def send_chain(h, kv):
        for lane in range(2):
            send(
                (k, v)[kv].at[:, kcols(lane, h)],
                s.kvp.at[kv, h, 2 + core],
                s.kv_recv.at[kv, h],
                2 * lax.rem(chip + 1, chips) + lane,
            )

    def relay_chain(h, kv):
        await_bytes(s.kvp.at[kv, h, pl.ds(2, 2)], s.kv_recv.at[kv, h])
        send(
            s.kvp.at[kv, h, pl.ds(2, 2)],
            s.kvp.at[kv, h, pl.ds(0, 2)],
            s.kv_relay.at[kv, h],
            2 * lax.rem(chip + 1, chips) + core,
        )

    def send_qu(h):
        send(q.at[:, qcols(other, h)], s.qb.at[core, h], s.qu_recv.at[h, 0], mate)
        send(u.at[:, qcols(other, h)], s.ub.at[core, h], s.qu_recv.at[h, 1], mate)

    send_chain(0, K_)

    for copy in own_kv:
        copy.wait()
    await_bytes(s.kvp.at[0, 0, pl.ds(0, 4)], s.mate_kv)
    def to_chips(start):
        def step(i, carry):
            start(lax.rem(chip + i, chips))
            return carry

        lax.fori_loop(1, chips, step, 0)

    def loop_send(src, dst, send_sem, recv_sem, to):
        pltpu.make_async_remote_copy(
            src_ref=src,
            dst_ref=dst,
            send_sem=send_sem,
            recv_sem=recv_sem,
            device_id={"ctx": to},
            device_id_type=MESH,
        ).start()

    for h in range(2):
        for kv in range(2):
            x = lax.select(root_core == 0, s.kvp[kv, h, 4], s.kvp[kv, h, 5])
            s.cand[:, h, kv] = x.reshape(16, 16, W)
    s.scat[chip] = s.cand[chip]
    to_chips(
        lambda c: loop_send(
            s.cand.at[c], s.scat.at[chip], s.pr_send.at[0], s.pr_recv.at[0], 2 * c + core
        )
    )
    send_chain(0, V_)

    await_bytes(s.meta.at[0], s.meta_recv)
    await_bytes(s.lens.at[pl.ds(0, groups - 1)], s.lens_recv)
    everything = s.lens[0, 0:1, :]
    for i in range(1, groups):
        everything = everything + s.lens[i, 0:1, :]
    scale = float(groups * 16 * W) / everything.astype(F32)
    scored = [rew[i].astype(F32) for i in range(16)]
    centre = functools.reduce(lambda a, b: a + b, scored) * (1.0 / 16)
    apart = [x - centre for x in scored]
    variance = functools.reduce(lambda a, b: a + b, [x * x for x in apart]) * (1.0 / 16)
    spread = jnp.sqrt(jnp.full((1, W), variance, F32))
    divisor = jnp.maximum(spread, 0.5)
    key_row = lax.broadcasted_iota(jnp.int32, (W, W), 0)
    query_col = lax.broadcasted_iota(jnp.int32, (W, W), 1)
    for o in range(2):
        for b in range(2):
            answer = s.meta[o, b, 7:8, :]
            row = jnp.zeros((1, W), F32)
            for i in range(16):
                row = row + jnp.where(answer == i, apart[i], 0.0)
            row = row / divisor * scale
            s.wt[o, b] = jnp.transpose(jnp.broadcast_to(row, (W, W)))
            of_query = jnp.broadcast_to(s.meta[o, b, 6:7, :].astype(F32), (W, W))
            of_key = jnp.transpose(of_query)
            seen = (key_row <= query_col) & (of_query >= 0.0)
            seen = seen & ((of_key == of_query) | (of_key == 0.0))
            seen = seen | (key_row == query_col)
            s.mb[o, b] = jnp.where(seen, 0.0, -jnp.inf)

    await_bytes(s.scat.at[pl.ds(0, chips - 1)], s.pr_recv.at[0])
    prompt_slice = s.scat[root_chip]
    s.sel[...] = prompt_slice
    s.gath[chip] = prompt_slice
    to_chips(
        lambda c: loop_send(s.sel, s.gath.at[chip], s.pr_send.at[1], s.pr_recv.at[1], 2 * c + core)
    )
    relay_chain(0, K_)
    relay_chain(0, V_)
    send_qu(0)
    for kv in range(2):
        send_chain(1, kv)
    send_qu(1)

    def where_is(t, h):
        return lax.rem(core + t // 2 + h, 2), lax.rem(t, 2)

    def gather_block(t, h, kv, to):
        o, b = where_is(t, h)
        to[t, 0 : 2 * W] = s.gath[:, h, kv].reshape(T, W)
        for i in range(HOPS):
            chosen = s.meta[o, b, 5 - i : 6 - i, :]
            both = s.kvp[kv, h, o + i].astype(F32)
            picked = jnp.where(jnp.broadcast_to(chosen, (W, W)) == 1, both[W:], both[:W])
            to[t, (2 + i) * W : (3 + i) * W] = picked.astype(BF16)
        to[t, 6 * W :] = s.kvp[kv, h, o + 4, pl.ds(pl.multiple_of(b * W, W), W), :]

    def spread_blocks(h, acc):
        def step(t, carry):
            o, b = where_is(t, h)
            s.pacc[...] += acc[t, 0 : 2 * W]
            for i in range(HOPS):
                chosen = jnp.broadcast_to(s.meta[o, b, 5 - i : 6 - i, :], (W, W)) == 1
                x = acc[t, (2 + i) * W : (3 + i) * W]
                s.gacc[o + i, 0:W] += jnp.where(chosen, 0.0, x)
                s.gacc[o + i, W:] += jnp.where(chosen, x, 0.0)
            s.gacc[o + 4, pl.ds(pl.multiple_of(b * W, W), W), :] += acc[t, 6 * W :]
            return carry

        lax.fori_loop(0, 4, step, 0)

    def chunk(j, h):
        t = j // 4
        o, b = where_is(t, h)
        return t, o, b, lax.rem(j, 4)

    def pair(ref, o, h, b, g):
        rows = pl.ds(pl.multiple_of(b * W, W), W)
        return [
            ref.at[o, h, rows, pl.ds(pl.multiple_of((2 * g + i) * W, W), W)] for i in range(2)
        ]

    def joined(ref, o, h, b, g):
        return jnp.concatenate([x[...] for x in pair(ref, o, h, b, g)], axis=0)

    def twice(row):
        return jnp.concatenate([row, row], axis=1)

    META_ROWS = (0, 1, 5, 4, 3, 2)

    def biases(o, b):
        rows = []
        for i in range(6):
            row = s.meta[o, b, META_ROWS[i] : META_ROWS[i] + 1, :]
            unseen = row <= 0 if i < 2 else row < 0
            rows.append(twice(jnp.where(unseen, -jnp.inf, 0.0)))
        return rows

    def score(j, h, ps, pk):
        t, o, b, g = chunk(j, h)
        queries = joined(s.qb, o, h, b, g)
        bias = biases(o, b)
        peak = None
        for lo, hi in CUTS:
            scores = nt(s.ku[t, lo * W : hi * W], queries)
            for i in range(lo, hi):
                part = scores[(i - lo) * W : (i + 1 - lo) * W]
                if i == 6:
                    part = part + twice(s.mb[o, b])
                ps[i * W : (i + 1) * W] = part
                top = jnp.max(part, axis=0, keepdims=True)
                if i < 6:
                    top = top + bias[i]
                peak = top if peak is None else jnp.maximum(peak, top)
        pk[0:1] = peak * exp_scale

    def soften(j, h, ps, pk, low, do):
        t, o, b, g = chunk(j, h)
        shift = pk[0:1]
        bias = biases(o, b)
        denominator = jnp.zeros((1, 2 * W), F32)
        for i in range(7):
            here = shift if i == 6 else shift - bias[i]
            e = jnp.exp2(ps[i * W : (i + 1) * W] * exp_scale - here)
            ps[i * W : (i + 1) * W] = e
            denominator = denominator + jnp.sum(e, axis=0, keepdims=True)
        inverse = 1.0 / denominator
        for i in range(7):
            probs = ps[i * W : (i + 1) * W] * inverse
            s.pf[j, i * W : (i + 1) * W] = probs
            low[i * W : (i + 1) * W] = probs.astype(BF16)
        weight = s.wt[o, b]
        up = [x[...].astype(F32) * weight for x in pair(s.ub, o, h, b, g)]
        grad_out = jnp.concatenate(up, axis=0).astype(BF16)
        do[...] = grad_out
        s.do[j] = grad_out

    def attend(j, h, low, do):
        t, o, b, g = chunk(j, h)
        attended = [nn(s.vt[t, :, lo * W : hi * W], low[lo * W : hi * W]) for lo, hi in CUTS]
        turned = sum(attended[1:], attended[0]).astype(BF16)
        attended = jnp.transpose(turned)
        for lo, hi in CUTS:
            s.acc[t, lo * W : hi * W] += nn(low[lo * W : hi * W], do[...])
        for i, x in enumerate(pair(s.ob, o, h, b, g)):
            x[...] = attended[i * W : (i + 1) * W]
        product = jnp.transpose(do[...]).astype(F32) * turned.astype(F32)
        s.dl[j, 0:1] = jnp.sum(product, axis=0, keepdims=True)

    def forward(h):
        def prepare(kv, whole, turned):
            await_bytes(s.kvp.at[kv, h, pl.ds(0, 2)], s.kv_relay.at[kv, h])

            def step(t, carry):
                gather_block(t, h, kv, whole)
                turned[t] = jnp.transpose(whole[t])
                return carry

            lax.fori_loop(0, 4, step, 0)

        even, odd = (s.ps0, s.pk0), (s.ps1, s.pk1)
        low_even, low_odd = (s.low0, s.do0), (s.low1, s.do1)
        prepare(K_, s.ku, s.kt)
        score(0, h, *even)
        score(1, h, *odd)
        soften(0, h, *even, *low_even)
        s.acc[...] = jnp.zeros_like(s.acc)
        prepare(V_, s.vu, s.vt)

        def step(i, carry):
            j = 2 * i
            if h == 0:

                @pl.when(i == 4)
                def _():
                    await_mate(h)

            attend(j - 2, h, *low_even)
            score(j, h, *even)
            soften(j - 1, h, *odd, *low_odd)
            attend(j - 1, h, *low_odd)
            score(j + 1, h, *odd)
            soften(j, h, *even, *low_even)
            return carry

        lax.fori_loop(1, 8, step, 0)
        attend(14, h, *low_even)
        soften(15, h, *odd, *low_odd)
        s.kacc[...] = jnp.zeros_like(s.kacc)
        score_grad(0, h, s.ds0)
        attend(15, h, *low_odd)
        score_grad(1, h, s.ds1)
        input_grads(0, h, s.ds0)
        spread_blocks(h, s.acc)

    def await_mate(h):
        for i in range(2):
            await_bytes((s.qb, s.ub)[i].at[other, h], s.qu_recv.at[h, i])

    def score_grad(j, h, low):
        t, o, b, g = chunk(j, h)
        delta = s.dl[j, 0:1]
        for lo, hi in CUTS:
            rows = pl.ds(lo * W, (hi - lo) * W)
            dprobs = nt(s.vu[t, rows], s.do[j])
            low[rows] = (s.pf[j, rows] * (dprobs - delta) * inv_root).astype(BF16)

    def input_grads(j, h, low):
        t, o, b, g = chunk(j, h)
        grad = [nn(s.kt[t, :, lo * W : hi * W], low[lo * W : hi * W]) for lo, hi in CUTS]
        grad = jnp.transpose(sum(grad[1:], grad[0]).astype(BF16))
        queries = joined(s.qb, o, h, b, g)
        for lo, hi in CUTS:
            s.kacc[t, lo * W : hi * W] += nn(low[lo * W : hi * W], queries)
        for i, x in enumerate(pair(s.gb, o, h, b, g)):
            x[...] = grad[i * W : (i + 1) * W]

    def backward(h):
        def step(i, carry):
            j = 2 * i
            score_grad(j, h, s.ds0)
            input_grads(j - 1, h, s.ds1)
            score_grad(j + 1, h, s.ds1)
            input_grads(j, h, s.ds0)
            return carry

        lax.fori_loop(1, 8, step, 0)
        input_grads(15, h, s.ds1)
        spread_blocks(h, s.kacc)

    def clear():
        s.gacc[...] = jnp.zeros_like(s.gacc)
        s.pacc[...] = jnp.zeros_like(s.pacc)

    def send_grads(kv, h):
        s.psend[h, :, kv] = s.pacc[...].reshape(16, 16, W).astype(BF16)
        if kv == K_:
            s.prec[h, chip] = s.psend[h, chip]
            to_chips(
                lambda c: loop_send(
                    s.psend.at[h, c],
                    s.prec.at[h, chip],
                    s.ps_send.at[h],
                    s.ps_recv.at[h],
                    2 * c + core,
                )
            )
        for i in range(4):
            s.gsend[kv, h, i] = s.gacc[i].astype(BF16)
            hop = 2 if i < 2 else 1
            send(
                s.gsend.at[kv, h, i],
                s.grecv.at[kv, h, hop - 1, core],
                s.g_recv.at[kv, h],
                2 * lax.rem(chip - hop + chips, chips) + i % 2,
            )
        s.msend[kv, h] = s.gacc[4 + other]
        send(s.msend.at[kv, h], s.mrecv.at[kv, h], s.m_recv.at[kv, h], mate)
        s.own[kv, h] = s.gacc[4 + core]

    own_out = []

    def send_rows(staged, out, h, recv_sem):
        send(staged.at[other, h], out.at[:, qcols(core, h)], recv_sem, mate)
        own_out.append(fetch(staged.at[core, h], out.at[:, qcols(core, h)]))

    def sum_prompt(h):
        await_bytes(s.prec.at[h, pl.ds(0, chips - 1)], s.ps_recv.at[h])
        summed = jnp.sum(s.prec[h].astype(F32), axis=0).astype(BF16)
        s.agsend[h] = summed
        s.ag[h, 16 * core + chip] = summed
        to_chips(
            lambda c: loop_send(
                s.agsend.at[h],
                s.ag.at[h, 16 * core + chip],
                s.ag_send.at[h],
                s.ag_recv.at[h],
                2 * c + core,
            )
        )

    def share_prompt(h):
        await_bytes(s.ag.at[h, pl.ds(0, chips - 1)], s.ag_recv.at[h])
        lane = pl.ds(16 * core, 16)
        send(s.ag.at[h, lane], s.ag.at[h, lane], s.ag_mate.at[h], mate)

    def finish(kv, h):
        out = (gk, gv)[kv]
        await_bytes(s.grecv.at[kv, h], s.g_recv.at[kv, h])
        await_bytes(s.mrecv.at[kv, h], s.m_recv.at[kv, h])
        for lane, mine in ((core, s.own), (other, s.mrecv)):
            x = mine[kv, h] + s.grecv[kv, h, 0, lane].astype(F32)
            x = x + s.grecv[kv, h, 1, lane].astype(F32)
            prompt = s.ag[h, pl.ds(16 * lane, 16), kv].astype(F32).reshape(T, W)
            here = jnp.full((T, W), root, jnp.int32) == me
            out[:, kcols(lane, h)] = x + jnp.where(here, prompt, 0.0)

    def await_shared(h):
        await_bytes(s.ag.at[h, pl.ds(0, chips)], s.ag_mate.at[h])

    await_bytes(s.gath.at[pl.ds(0, chips - 1)], s.pr_recv.at[1])
    for h in range(2):
        for copy in own_qu[h]:
            copy.wait()
        if h == 1:
            await_mate(h)
        clear()
        forward(h)
        send_grads(V_, h)
        send_rows(s.ob, attn, h, s.out_recv.at[0, h])
        if h == 0:
            relay_chain(1, K_)
            relay_chain(1, V_)
        else:
            sum_prompt(0)
        clear()
        backward(h)
        send_grads(K_, h)
        send_rows(s.gb, gq, h, s.out_recv.at[1, h])
    share_prompt(0)
    sum_prompt(1)
    await_shared(0)
    finish(V_, 0)
    finish(K_, 0)
    share_prompt(1)
    await_shared(1)
    finish(V_, 1)
    finish(K_, 1)

    for copy in own_out:
        copy.wait()
    for h in range(2):
        for i in range(2):
            await_bytes(s.ob.at[other, h], s.out_recv.at[i, h])
    for copy in sends:
        copy.wait_send()
    await_bytes(s.lens.at[pl.ds(0, groups - 1)], s.lens_send)
    for i in range(2):
        await_bytes(s.scat.at[pl.ds(0, chips - 1)], s.pr_send.at[i])
        await_bytes(s.ag.at[i, pl.ds(0, chips - 1)], s.ag_send.at[i])
        await_bytes(s.prec.at[i, pl.ds(0, chips - 1)], s.ps_send.at[i])


def write_out(*refs):
    sems = refs[8]
    copies = [pltpu.make_async_copy(refs[i], refs[4 + i], sems.at[i]) for i in range(4)]
    for copy in copies:
        copy.start()
    for copy in copies:
        copy.wait()


def body(queries, keys, values, upstream, ancestors, segments, responses, rewards, lengths):
    any_spec = pl.BlockSpec(memory_space=pltpu.HBM)
    smem = pl.BlockSpec(memory_space=pltpu.SMEM)
    vmem = pl.BlockSpec(memory_space=pltpu.VMEM)
    results = pl.pallas_call(
        functools.partial(kernel, lax.axis_size("dp"), lax.axis_size("ctx")),
        out_shape=[
            pltpu.VMEM(queries.shape, BF16),
            pltpu.VMEM(queries.shape, BF16),
            pltpu.VMEM(keys.shape, F32),
            pltpu.VMEM(keys.shape, F32),
        ],
        in_specs=[any_spec] * 4 + [smem, vmem, vmem, smem, smem],
        out_specs=[vmem] * 4,
        scratch_shapes=list(SCRATCH.values()),
        compiler_params=pltpu.CompilerParams(
            collective_id=0, has_side_effects=True, vmem_limit_bytes=56 * 1024 * 1024
        ),
    )(
        queries,
        keys,
        values,
        upstream,
        ancestors,
        segments.reshape(2, W),
        responses.reshape(2, W),
        rewards,
        lengths,
    )
    return pl.pallas_call(
        write_out,
        out_shape=[jax.ShapeDtypeStruct(x.shape, x.dtype) for x in results],
        in_specs=[vmem] * 4,
        out_specs=[any_spec] * 4,
        scratch_shapes=[pltpu.SemaphoreType.DMA((4,))],
        compiler_params=pltpu.CompilerParams(vmem_limit_bytes=1024 * 1024),
    )(*[pltpu.with_memory_space_constraint(x, pltpu.VMEM) for x in results])


def solution(mesh):
    rows, flat = P(("dp", "ctx"), None), P(("dp", "ctx"))
    return jax.shard_map(
        body,
        mesh=mesh,
        in_specs=(rows, rows, rows, rows, rows, flat, flat, P("dp"), P("dp")),
        out_specs=(rows, rows, rows, rows),
        check_vma=False,
    )
```
